32 devices in a mesh: parts: 2 (over y), expert: 8 (over z, x), group: 1, tensor: 2 (over core).
Axes of the slice: x: 2, y: 2, z: 4, core: 2. Of those that a mesh axis runs over, the one named last changes fastest.
Arguments:
- hidden_in: bfloat16 [3, 64, 4096], P(None, ('parts', 'expert', 'group')), parts along dimension 1, may hold values from -6 to 6
- queries: bfloat16 [3, 64, 32, 128], P(None, ('parts', 'expert', 'group'), 'tensor'), parts along dimension 1, may hold values from -32 to 32
- new_keys: bfloat16 [3, 64, 4, 128], P(None, ('parts', 'expert', 'group'), 'tensor'), parts along dimension 1, may hold values from -4 to 4
- new_values: bfloat16 [3, 64, 4, 128], P(None, ('parts', 'expert', 'group'), 'tensor'), parts along dimension 1, may hold values from -8 to 8
- cache_keys: bfloat16 [64, 4, 128, 128], P(('parts', 'expert', 'group'), 'tensor'), parts along dimension 0, may hold values from -4 to 4
- cache_values: bfloat16 [64, 4, 128, 128], P(('parts', 'expert', 'group'), 'tensor'), parts along dimension 0, may hold values from -8 to 8
- route_ids: int32 [3, 64, 8], P(None, ('parts', 'expert', 'group')), parts along dimension 1, may hold values from 0 to 15, all different within a row; in each aligned block of 4 rows (0 to 3, 4 to 7, ..., all dimensions but the last counted through in order) at most 4 rows name the same one
- route_weights: float32 [3, 64, 8], P(None, ('parts', 'expert', 'group')), parts along dimension 1, may hold values from 0.1 to 1
- norm_gain: float32 [4096], replicated, may hold values from 0.25 to 1.75
- gate_weight: bfloat16 [16, 4096, 768], P('expert', 'group', 'tensor'), may hold values from -0.09375 to 0.09375
- up_weight: bfloat16 [16, 4096, 768], P('expert', 'group', 'tensor'), may hold values from -0.09375 to 0.09375
- down_weight: bfloat16 [16, 768, 4096], P('expert', None, ('group', 'tensor')), may hold values from -0.21875 to 0.21875
- ancestor_counts: int32 [64], P(('parts', 'expert', 'group')), parts along dimension 0, may hold values from 0 to 5, as said below
Outputs:
- layer_out: bfloat16 [3, 64, 4096], P(None, ('parts', 'expert', 'group')), parts along dimension 1
- resampled_keys: bfloat16 [64, 4, 131, 128], P(('parts', 'expert', 'group'), 'tensor'), parts along dimension 0
- resampled_values: bfloat16 [64, 4, 131, 128], P(('parts', 'expert', 'group'), 'tensor'), parts along dimension 0
The draws below stay inside these ranges and needn't reach their ends.
There are 2 independent parts, one for each index of `parts`. The reference program is written for one: setup_inputs(seed, part) draws one part's arguments, and reference() takes and returns one part's arrays. A program takes and returns all parts, laid end to end along the dimension named above; an argument that names none is the same for every part. Nothing has to cross between parts.
Inputs may be any that keep to these rules, and one draw needn't show every extreme that they name: `route_ids`: each row names 8 different experts; in each aligned block of 4 rows (the rows of one device in one step) no expert is named by more than 4 rows. `ancestor_counts`: the counts sum to 32, and every particle i descends from a particle within 2 positions of i.
All inputs are finite; a program needn't handle non-finite values.
Results may differ from the reference program's by a relative error of at most 0.0075.
Values may be sent and summed in bfloat16 or wider, within the bound.
No kernel may reach another device: no remote copies, remote signals or barrier semaphores. Data moves between devices by JAX's collectives and lax.ppermute only.
A program may use at most 64 MiB of HBM per device.

```python
import math
import jax
import jax.numpy as jnp
import numpy as np
from jax import lax

D = 4096
FF = 768
QH = 32
KVH = 4
HD = 128
TOPK = 8
STEPS = 3
REACH = 2
TOK_DEV = 4
CACHE = 128
EXPERTS = 16
PARTICLES = 32
CAP = 4
N_GROUP = 1


def drawn_pair(key):
    cached = jnp.clip(jax.random.normal(jax.random.fold_in(key, 41), (PARTICLES, KVH, CACHE, HD), jnp.float32), -4.0, 4.0)
    queries_drawn = jnp.clip(jax.random.normal(jax.random.fold_in(key, 42), (STEPS, PARTICLES, QH, HD), jnp.float32), -4.0, 4.0)
    return (queries_drawn, cached)


def draw_queries(key, part):
    return drawn_pair(key)[0].astype(jnp.bfloat16)


def draw_cache_keys(key, part):
    return drawn_pair(key)[1].astype(jnp.bfloat16)


def draw_ancestor_counts(key, part):
    indices = jnp.arange(PARTICLES, dtype=jnp.int32)
    offsets = jax.random.randint(jax.random.fold_in(key, 51), (PARTICLES,), -REACH, REACH + 1, dtype=jnp.int32)
    marked = jax.random.randint(jax.random.fold_in(key, 52), (), 0, PARTICLES - REACH, dtype=jnp.int32)
    offsets = jnp.where(indices == marked, REACH, offsets)
    before_edge = (indices >= TOK_DEV - 2 * REACH) & (indices < TOK_DEV)
    offsets = jnp.where(before_edge, jnp.minimum(offsets, TOK_DEV - REACH - indices), offsets)
    offsets = jnp.where(indices == TOK_DEV, -REACH, offsets)
    ancestor = lax.cummax(jnp.clip(indices + offsets, 0, PARTICLES - 1), axis=0)
    return jnp.sum((ancestor[:, None] == indices[None, :]).astype(jnp.int32), axis=0)


def steps_of(rng, shape, split, smallest, top_value):
    def one(dim, parts):
        draws = jax.random.uniform(jax.random.fold_in(jax.random.fold_in(rng, 6), dim), (parts,), jnp.float32, smallest / len(split), top_value / len(split))
        return jnp.repeat(jnp.exp(draws), shape[dim] // parts).reshape((-1,) + (1,) * (len(shape) - dim - 1))

    factor_of = one(*split[0])
    for cut in split[1:]:
        factor_of = factor_of * one(*cut)
    return factor_of


def assign_block(stream_key, own, number, rows, count, top, most, skew):
    order = jax.random.permutation(stream_key, count)
    crowded, usual = portions_of(count, rows * top, most, skew, True), portions_of(count, rows * top, most, skew, False)
    places = jnp.arange(count)

    def named(lengths, rotation):
        used = int((lengths > 0).sum())
        fixed = max(1, used // 4)
        passed = fixed + (places - fixed + rotation * (used - fixed)) % max(1, count - fixed)
        return jnp.zeros((count,), jnp.int32).at[order[jnp.where(places < fixed, places, passed)]].set(jnp.asarray(lengths, jnp.int32))

    lengths = jnp.where(number % 4 == 0, named(crowded, number // 4), named(usual, number - number // 4 - 1))
    mixed = jax.random.permutation(jax.random.fold_in(own, 3), count)
    giver, receiver = mixed[0:count // 2 * 2:2], mixed[1:count // 2 * 2:2]
    slack = jnp.minimum(lengths[giver] - 1, most - lengths[receiver]) // 2
    slack = jnp.where((giver == order[0]) | (receiver == order[0]) | (lengths[receiver] == 0), 0, jnp.maximum(slack, 0))
    passed = jax.random.randint(jax.random.fold_in(own, 4), (count // 2,), 0, 1 << 20) % (slack + 1)
    lengths = lengths.at[giver].add(-passed).at[receiver].add(passed)
    labels = jnp.searchsorted(jnp.cumsum(lengths), jnp.arange(rows * top), side="right").astype(jnp.int32)
    listing = labels.reshape(top, rows).T
    listing = listing[jax.random.permutation(jax.random.fold_in(own, 1), rows)]
    rotation = jax.random.randint(jax.random.fold_in(own, 2), (rows, 1), 0, top)
    return jnp.take_along_axis(listing, (jnp.arange(top)[None, :] + rotation) % top, axis=1)


def portions_of(count, total, limit, slope, full):
    weights = [(1 << 20) // math.isqrt(rank ** slope) + 1 for rank in range(1, count + 1)]
    largest = limit if full else min(limit, max(-(-total // count), total * weights[0] // sum(weights)))
    least = 1 if total - largest >= count - 1 else 0
    holding, spare = [largest] + [least] * (count - 1), total - largest - least * (count - 1)
    while spare > 0:
        free = [i for i in range(1, count) if holding[i] < largest] or [i for i in range(1, count) if holding[i] < limit]
        mass, left = sum([weights[i] for i in free]), spare
        for i in free:
            addition = min(limit - holding[i], max(1, left * weights[i] // mass), spare)
            holding[i] = holding[i] + addition
            spare = spare - addition
    return np.array(holding)


def normal_values(stream_key, dims, deviation, limit, pieces=(), kind=jnp.bfloat16):
    entries = deviation * jax.random.normal(stream_key, dims, jnp.float32)
    if pieces:
        entries = entries * steps_of(stream_key, dims, pieces, -0.22, 0.18)
    return jnp.clip(entries, -limit, limit).astype(kind)


def setup_inputs(seed: int = 0, part: int = 0) -> dict:
    seeds = jax.random.split(jax.random.key(seed), 14)
    own_keys = jax.random.split(jax.random.fold_in(seeds[13], part), 14)
    hidden_in = normal_values(own_keys[0], (STEPS, PARTICLES, D), 1.0, 6.0, ((1, 8),))
    queries = draw_queries(jax.random.fold_in(jax.random.fold_in(seeds[13], part), 71), part)
    new_keys = normal_values(own_keys[2], (STEPS, PARTICLES, KVH, HD), 1.0, 4.0, ((1, 8), (2, 2)))
    new_values = normal_values(own_keys[3], (STEPS, PARTICLES, KVH, HD), 2.0, 8.0, ((1, 8), (2, 2)))
    cache_keys = draw_cache_keys(jax.random.fold_in(jax.random.fold_in(seeds[13], part), 71), part)
    cache_values = normal_values(own_keys[5], (PARTICLES, KVH, CACHE, HD), 2.0, 8.0, ((0, 8), (1, 2)))
    route_ids_keys = jax.random.split(jax.random.fold_in(own_keys[6], 1), STEPS * PARTICLES // TOK_DEV)
    route_ids_turns = jax.random.permutation(jax.random.fold_in(own_keys[6], 3), STEPS * PARTICLES // TOK_DEV)
    route_ids = jax.vmap(lambda own, number: assign_block(jax.random.fold_in(own_keys[6], 2), own, number, TOK_DEV, EXPERTS, TOPK, CAP, 2))(route_ids_keys, route_ids_turns).reshape((STEPS, PARTICLES, TOPK))
    route_weights = jnp.clip(jnp.exp(math.log(1.0) - 2.3025851 * jax.random.uniform(own_keys[7], (STEPS, PARTICLES, TOPK), jnp.float32) ** steps_of(own_keys[7], (STEPS, PARTICLES, TOPK), ((1, 8),), -0.2, 0.2)), 0.1, 1.0)
    norm_gain = jnp.clip(1.0 + 0.15 * jax.random.normal(seeds[8], (D,), jnp.float32), 0.25, 1.75)
    gate_weight = normal_values(seeds[9], (EXPERTS, D, FF), D ** -0.5, 0.09375, ((0, 8), (2, 2)))
    up_weight = normal_values(seeds[10], (EXPERTS, D, FF), D ** -0.5, 0.09375, ((0, 8), (2, 2)))
    down_weight = normal_values(seeds[11], (EXPERTS, FF, D), FF ** -0.5, 0.21875, ((0, 8), (2, 2)))
    ancestor_counts = draw_ancestor_counts(jax.random.fold_in(jax.random.fold_in(seeds[13], part), 71), part)
    return dict(hidden_in=hidden_in, queries=queries, new_keys=new_keys, new_values=new_values, cache_keys=cache_keys, cache_values=cache_values, route_ids=route_ids, route_weights=route_weights, norm_gain=norm_gain, gate_weight=gate_weight, up_weight=up_weight, down_weight=down_weight, ancestor_counts=ancestor_counts)


epsilon = 1e-06
highest = lax.Precision.HIGHEST

def attention(queries, keys_all, values_all):
    group_size = QH // KVH
    length = CACHE + STEPS
    grouped = queries.astype(jnp.float32).reshape(STEPS, PARTICLES, KVH, group_size, HD)
    scores = jnp.einsum('sphgd,phld->sphgl', grouped, keys_all.astype(jnp.float32), precision=highest) / math.sqrt(HD)
    allowed = lax.broadcasted_iota(jnp.int32, (STEPS, length), 1) <= CACHE + lax.broadcasted_iota(jnp.int32, (STEPS, length), 0)
    scores = jnp.where(allowed[:, None, None, None, :], scores, -1e+30)
    exponent = jnp.exp(scores - lax.optimization_barrier(jnp.max(scores, axis=-1, keepdims=True)))
    probs = (exponent / lax.optimization_barrier(jnp.sum(exponent, axis=-1, keepdims=True))).astype(jnp.bfloat16)
    mixed = jnp.einsum('sphgl,phld->sphgd', probs.astype(jnp.float32), values_all.astype(jnp.float32), precision=highest)
    return mixed.astype(jnp.bfloat16).reshape(STEPS, PARTICLES, QH * HD)

def expert_rows(route_ids):
    blocks = PARTICLES // TOK_DEV
    pair_count = TOK_DEV * TOPK
    chosen = route_ids.reshape(STEPS, blocks, pair_count).astype(jnp.int32)
    expert_hits = (chosen[..., None] == jnp.arange(EXPERTS, dtype=jnp.int32)).astype(jnp.int32)
    position = lax.optimization_barrier(jnp.sum((jnp.cumsum(expert_hits, axis=2) - expert_hits) * expert_hits, axis=-1)).astype(jnp.int32)
    step_ids = lax.broadcasted_iota(jnp.int32, (STEPS, blocks, pair_count), 0)
    block_ids = lax.broadcasted_iota(jnp.int32, (STEPS, blocks, pair_count), 1)
    pair_ids = lax.broadcasted_iota(jnp.int32, (STEPS, blocks, pair_count), 2)
    slot_ids = ((chosen * STEPS + step_ids) * blocks + block_ids) * CAP + position
    token_ids = step_ids * PARTICLES + block_ids * TOK_DEV + pair_ids // TOPK
    return (slot_ids.reshape(-1).astype(jnp.int32), token_ids.reshape(-1).astype(jnp.int32))

def block_sum(split_rows, weight):
    blocks = weight.astype(jnp.float32).reshape(N_GROUP, D // N_GROUP, FF)
    terms = jnp.einsum('rgd,gdf->rgf', split_rows, blocks, precision=highest)
    return lax.optimization_barrier(jnp.sum(lax.optimization_barrier(terms.astype(jnp.bfloat16)).astype(jnp.float32), axis=1))

def mixture(normed, route_ids, route_weights, gate_weight, up_weight, down_weight):
    slot_ids, token_ids = expert_rows(route_ids)
    slot_total = EXPERTS * STEPS * (PARTICLES // TOK_DEV) * CAP
    holder = jnp.zeros((slot_total,), jnp.int32).at[slot_ids].set(token_ids + 1)
    flat_normed = normed.reshape(STEPS * PARTICLES, D)
    rows = flat_normed[jnp.maximum(holder - 1, 0)]
    rows = jnp.where((holder > 0)[:, None], rows, jnp.zeros((), jnp.bfloat16))
    rows = rows.reshape(EXPERTS, slot_total // EXPERTS, D)

    def one_expert(packed):
        block_rows, gate_matrix, up_matrix, down_matrix = packed
        split_rows = block_rows.astype(jnp.float32).reshape(-1, N_GROUP, D // N_GROUP)
        gate_sum = block_sum(split_rows, gate_matrix)
        up_sum = block_sum(split_rows, up_matrix)
        hidden = (jax.nn.silu(gate_sum) * up_sum).astype(jnp.bfloat16)
        return jnp.dot(hidden, down_matrix, preferred_element_type=jnp.float32).astype(jnp.bfloat16)
    outputs = lax.map(one_expert, (rows, gate_weight, up_weight, down_weight))
    outputs = outputs.reshape(slot_total, D)
    picked = outputs[slot_ids].astype(jnp.float32).reshape(STEPS, PARTICLES, TOPK, D)
    route_share = route_weights / lax.optimization_barrier(jnp.sum(route_weights, axis=-1, keepdims=True))
    return lax.optimization_barrier(jnp.sum(route_share[..., None] * picked, axis=2))

def reference(hidden_in, queries, new_keys, new_values, cache_keys, cache_values, route_ids, route_weights, norm_gain, gate_weight, up_weight, down_weight, ancestor_counts):
    keys_all = jnp.concatenate([cache_keys, jnp.transpose(new_keys, (1, 2, 0, 3))], axis=2)
    values_all = jnp.concatenate([cache_values, jnp.transpose(new_values, (1, 2, 0, 3))], axis=2)
    attended = attention(queries, keys_all, values_all)
    residual = hidden_in.astype(jnp.float32) + attended.astype(jnp.float32)
    normed = (residual * lax.rsqrt(lax.optimization_barrier(jnp.mean(residual * residual, axis=-1, keepdims=True)) + epsilon) * norm_gain).astype(jnp.bfloat16)
    expert_mix = mixture(normed, route_ids, route_weights, gate_weight, up_weight, down_weight)
    layer_out = (residual + expert_mix).astype(jnp.bfloat16)
    running = jnp.cumsum(ancestor_counts)
    indices = jnp.arange(PARTICLES, dtype=jnp.int32)
    ancestor = lax.optimization_barrier(jnp.sum((running[None, :] <= indices[:, None]).astype(jnp.int32), axis=1))
    return (layer_out, keys_all[ancestor], values_all[ancestor])
```

```python
import functools
import math

import jax
import jax.numpy as jnp
from jax import lax
from jax.experimental import pallas as pl
from jax.experimental.pallas import tpu as pltpu
from jax.sharding import PartitionSpec as P

REACH = 2
LANES = 128
f32, bf16 = jnp.float32, jnp.bfloat16

epsilon = 1e-06
highest = lax.Precision.HIGHEST


def dot(a, b, dims=((1,), (0,))):
    return lax.dot_general(a, b, (dims, ((), ())), preferred_element_type=f32)


def iota(shape, dim):
    return lax.broadcasted_iota(jnp.int32, shape, dim)


def attend_kernel(
    steps, experts, ids_ref, weights_ref, counts_ref, gain_ref, hidden_ref, q_ref, nk_ref, nv_ref, ck_ref, cv_ref,
    send_ref, residual_ref, near_ref, far_ref, scores_ref,
):
    tokens, heads, width = q_ref.shape[1:]
    kv_heads, cached = ck_ref.shape[1:3]
    group = heads // kv_heads
    columns = heads * width
    part = columns // (steps + 1)
    main = steps * part
    rows = (steps + 1) * tokens
    base = lax.axis_index("tensor") * columns
    fresh = steps * kv_heads
    fresh_rows = -(-fresh // 16) * 16
    scale = 1.0 / math.sqrt(width)

    odd = lax.rem(lax.axis_index("expert"), 2)
    per = REACH * kv_heads

    def halo(out_ref, start):
        for kind, (cache_ref, new_ref) in enumerate(((ck_ref, nk_ref), (cv_ref, nv_ref))):
            for r in range(REACH):
                for h in range(kv_heads):
                    slot = kind * per + r * kv_heads + h
                    out_ref[slot, :cached, :] = cache_ref[start + r, h]
                    new = jnp.concatenate(
                        [new_ref[s, start + r, h : h + 1, :].astype(f32) for s in range(steps)]
                        + [jnp.zeros((16 - steps, width), f32)], axis=0)
                    out_ref[slot, cached:, :] = new.astype(bf16)

    @pl.when(odd == 0)
    def _():
        halo(near_ref, tokens - REACH)
        halo(far_ref, 0)

    @pl.when(odd == 1)
    def _():
        halo(near_ref, 0)
        halo(far_ref, tokens - REACH)

    q_rows = steps * heads
    row = iota((q_rows, kv_heads * cached), 0)
    col = iota((q_rows, kv_heads * cached), 1)
    own_head = lax.div(lax.rem(row, heads), group) == lax.div(col, cached)
    row = iota((q_rows, fresh_rows), 0)
    col = iota((q_rows, fresh_rows), 1)
    own_new = (
        (lax.div(lax.rem(row, heads), group) == lax.rem(col, kv_heads))
        & (lax.div(col, kv_heads) <= lax.div(row, heads))
        & (col < fresh)
    )
    outputs = []
    for p in range(tokens):
        q = jnp.concatenate([q_ref[s, p] for s in range(steps)], axis=0)

        def with_new(new_ref):
            pieces = [new_ref[s, p].astype(f32) for s in range(steps)]
            return jnp.concatenate(pieces + [jnp.zeros((fresh_rows - fresh, width), f32)], axis=0).astype(bf16)

        keys = ck_ref[p].reshape(kv_heads * cached, width)
        values = cv_ref[p].reshape(kv_heads * cached, width)
        old = jnp.where(own_head, dot(q, keys, ((1,), (1,))) * scale, -1e30)
        new = jnp.where(own_new, dot(q, with_new(nk_ref), ((1,), (1,))) * scale, -1e30)
        top = jnp.maximum(jnp.max(old, axis=1, keepdims=True), jnp.max(new, axis=1, keepdims=True))
        old = jnp.exp(old - top)
        new = jnp.exp(new - top)
        total = jnp.sum(old, axis=1, keepdims=True) + jnp.sum(new, axis=1, keepdims=True)
        old = (old / total).astype(bf16)
        new = (new / total).astype(bf16)
        outputs.append((dot(old, values) + dot(new, with_new(nv_ref))).astype(bf16))
    attended = jnp.concatenate(outputs, axis=0)

    tiles = main // width
    count = tokens * q_rows
    target = iota((tiles * rows, count), 0)
    tile, inner = lax.div(target, rows), lax.rem(target, rows)
    is_extra = inner >= steps * tokens
    step = jnp.where(is_extra, lax.div(tile, part // width), lax.div(inner, tokens))
    token = lax.rem(inner, tokens)
    head = jnp.where(is_extra, tiles + lax.rem(tile, part // width), tile)
    chosen = (token * q_rows + step * heads + head) == iota((tiles * rows, count), 1)
    moved = dot(chosen.astype(f32).astype(bf16), attended)
    for s in range(steps):
        residual_ref[s * tokens : (s + 1) * tokens, :] = hidden_ref[s, :, pl.ds(pl.multiple_of(base, LANES), main)].astype(f32)
        residual_ref[steps * tokens :, s * part : (s + 1) * part] = hidden_ref[
            s, :, pl.ds(pl.multiple_of(base + main, LANES), part)
        ].astype(f32)
    residual = residual_ref[...] + jnp.concatenate([moved[j * rows : (j + 1) * rows] for j in range(tiles)], axis=1)
    residual_ref[...] = residual
    gain_main = gain_ref[:, pl.ds(pl.multiple_of(base, LANES), main)]
    gain_last = gain_ref[:, pl.ds(pl.multiple_of(base + main, LANES), part)]
    in_main = iota((rows, main), 0) < steps * tokens
    gain = jnp.where(in_main, gain_main, jnp.concatenate([gain_last] * steps, axis=1))
    send_ref[:, :main] = (residual * gain).astype(bf16)

    squares = residual * residual
    lane = iota((tokens, LANES), 1)
    for s in range(steps):
        scores_ref[s * rows : (s + 1) * rows, :] = jnp.broadcast_to(
            jnp.sum(squares[:, s * part : (s + 1) * part], axis=1, keepdims=True), (rows, LANES))
    whole = sum(scores_ref[s * rows : (s + 1) * rows, :] for s in range(steps))
    scores_ref[steps * rows :, :] = whole
    pieces = []
    for s in range(steps):
        square_sum = (
            scores_ref[steps * rows + s * tokens : steps * rows + (s + 1) * tokens, :]
            + scores_ref[s * rows + steps * tokens : (s + 1) * rows, :]
        )
        ids, weights = ids_ref[s], weights_ref[s]
        share = weights / jnp.sum(weights, axis=1, keepdims=True)
        value = jnp.zeros((tokens, LANES), f32)
        expert = jnp.where(lane < experts, lane, lane - experts)
        for k in range(ids.shape[1]):
            value = jnp.where(ids[:, k : k + 1] == expert, share[:, k : k + 1], value)
        value = jnp.where(lane < 2 * experts, value, square_sum)
        high = value.astype(bf16).astype(f32)
        low = value - high
        piece = jnp.where((lane < experts) | (lane == 2 * experts), high, low)
        piece = jnp.where(lane < 2 * experts + 2, piece, 0.0)
        if s == 0:
            for p in range(tokens):
                here = (lane == 2 * experts + 2) & (iota((tokens, LANES), 0) == p)
                piece = jnp.where(here, counts_ref[p].astype(f32), piece)
        pieces.append(piece)
    pieces.append(jnp.zeros((tokens, LANES), f32))
    send_ref[:, main:] = jnp.concatenate(pieces, axis=0).astype(bf16)


def unpacking(blocks, steps, tokens, s, back):
    rows = (steps + 1) * tokens
    target, source = iota((blocks * rows, blocks * rows), 0), iota((blocks * rows, blocks * rows), 1)
    if back:
        target, source = source, target
    hit = (target + (steps - s) * tokens == source) & (lax.div(lax.rem(target, rows), tokens) == s)
    return hit.astype(f32).astype(bf16)


def hidden_kernel(steps, tokens, experts, own_ref, other_ref, gate_ref, up_ref, out_ref):
    total, padded = own_ref.shape
    rows = (steps + 1) * tokens
    main = padded - LANES
    part = main // steps
    columns = main + part
    local, _, units = gate_ref.shape
    mine = lax.axis_index("tensor")
    blocks = total // rows
    gates, ups = [0.0] * local, [0.0] * local
    unpacks = [unpacking(blocks, steps, tokens, s, False) for s in range(steps)]
    for ref, half in ((own_ref, mine), (other_ref, 1 - mine)):
        features = ref[:, :main]
        extra = sum(dot(unpacks[s], features[:, s * part : (s + 1) * part]) for s in range(steps)).astype(bf16)
        first = pl.multiple_of(half * columns, LANES)
        last = pl.multiple_of(half * columns + main, LANES)
        for e in range(local):
            gates[e] += dot(features, gate_ref[e, pl.ds(first, main), :]) + dot(extra, gate_ref[e, pl.ds(last, part), :])
            ups[e] += dot(features, up_ref[e, pl.ds(first, main), :]) + dot(extra, up_ref[e, pl.ds(last, part), :])
    meta = own_ref[:, main:].astype(f32)
    meta_other = other_ref[:, main:].astype(f32)
    lane = iota(meta.shape, 1)
    valid = lax.rem(iota((total, 1), 0), rows) < steps * tokens
    in_squares = (lane == 2 * experts) | (lane == 2 * experts + 1)
    square_sum = jnp.sum(jnp.where(in_squares, meta + meta_other, 0.0), axis=1, keepdims=True)
    factor = jnp.where(valid, lax.rsqrt(square_sum / (2 * columns) + epsilon), 0.0)
    first_expert = lax.axis_index("expert") * local
    for e in range(local):
        at = first_expert + e
        share = jnp.sum(jnp.where((lane == at) | (lane == at + experts), meta, 0.0), axis=1, keepdims=True)
        gate = (gates[e] * factor).astype(bf16).astype(f32)
        up = (ups[e] * factor).astype(bf16).astype(f32)
        hidden = gate / (1.0 + jnp.exp(-gate)) * up * share
        out_ref[:, e * units : (e + 1) * units] = hidden.astype(bf16)


def down_kernel(steps, tokens, own_ref, other_ref, down_ref, out_ref):
    total, width = own_ref.shape
    local, _, columns = down_ref.shape
    units = width // local
    rows = (steps + 1) * tokens
    part = columns // (steps + 1)
    main = steps * part
    blocks = total // rows
    mine = lax.axis_index("tensor")
    product = 0.0
    for ref, half in ((own_ref, mine), (other_ref, 1 - mine)):
        start = pl.multiple_of(half * units, LANES)
        for e in range(local):
            product += dot(ref[:, e * units : (e + 1) * units], down_ref[e, pl.ds(start, units), :])
    last = product[:, main:].astype(bf16)
    extra = jnp.concatenate([dot(unpacking(blocks, steps, tokens, s, True), last) for s in range(steps)], axis=1)
    in_main = lax.rem(iota((total, main), 0), rows) < steps * tokens
    out_ref[...] = jnp.where(in_main, product[:, :main], extra).astype(out_ref.dtype)


def resample_kernel(steps, counts_ref, near_ref, far_ref, ck_ref, cv_ref, nk_ref, nv_ref, keys_ref, values_ref):
    tokens, kv_heads, cached, width = ck_ref.shape
    devices = counts_ref.shape[0]
    me = lax.axis_index("expert")
    first = me * tokens
    odd = lax.rem(me, 2)
    per = REACH * kv_heads
    running = jnp.int32(0)
    ancestors = [jnp.int32(0)] * tokens
    for d in range(devices):
        k = jnp.bitwise_xor(me, d)
        for p in range(tokens):
            running = running + counts_ref[k, p]
            for i in range(tokens):
                ancestors[i] = ancestors[i] + (running <= first + i).astype(jnp.int32)

    for i in range(tokens):
        offset = ancestors[i] - first

        @pl.when((offset >= 0) & (offset < tokens))
        def _():
            for out_ref, cache_ref, new_ref in ((keys_ref, ck_ref, nk_ref), (values_ref, cv_ref, nv_ref)):
                out_ref[i, :, :cached, :] = cache_ref[offset]
                for s in range(steps):
                    out_ref[i, :, cached + s, :] = new_ref[s, offset]

        def from_halo(ref, at):
            for kind, out_ref in enumerate((keys_ref, values_ref)):
                for h in range(kv_heads):
                    out_ref[i, h, :, :] = ref[kind * per + at * kv_heads + h, : cached + steps, :]

        @pl.when((offset < 0) & (odd == 1))
        def _():
            from_halo(near_ref, offset + REACH)

        @pl.when((offset < 0) & (odd == 0))
        def _():
            from_halo(far_ref, offset + REACH)

        @pl.when((offset >= tokens) & (odd == 0))
        def _():
            from_halo(near_ref, offset - tokens)

        @pl.when((offset >= tokens) & (odd == 1))
        def _():
            from_halo(far_ref, offset - tokens)


def add_kernel(a_ref, b_ref, out_ref):
    out_ref[...] = (a_ref[...] + b_ref[...].astype(f32)).astype(out_ref.dtype)


def total_kernel(count, *refs):
    out_ref = refs[-1]
    value = refs[0][...]
    for ref in refs[1 : count + 1]:
        value = value + ref[...].astype(f32)
    out_ref[...] = value.astype(out_ref.dtype)


def unpack_kernel(own_ref, other_ref, out_ref):
    steps, tokens, model_width = out_ref.shape
    columns = model_width // 2
    main = own_ref.shape[1]
    part = main // steps
    mine = lax.axis_index("tensor")
    for ref, half in ((own_ref, mine), (other_ref, 1 - mine)):
        block = ref[...].astype(f32)
        first = pl.multiple_of(half * columns, LANES)
        last = pl.multiple_of(half * columns + main, LANES)
        for s in range(steps):
            out_ref[s, :, pl.ds(first, main)] = block[s * tokens : (s + 1) * tokens].astype(bf16)
            out_ref[s, :, pl.ds(last, part)] = block[steps * tokens :, s * part : (s + 1) * part].astype(bf16)


VMEM = pl.BlockSpec(memory_space=pltpu.VMEM)
SMEM = pl.BlockSpec(memory_space=pltpu.SMEM)


def call(kernel, out, specs, name, scratch=(), limit=48):
    outs = jax.tree.map(lambda _: VMEM, out)
    return pl.pallas_call(
        kernel, out_shape=out, in_specs=specs, out_specs=outs, scratch_shapes=scratch, name=name,
        compiler_params=pltpu.CompilerParams(vmem_limit_bytes=limit << 20),
    )


def struct(shape, dtype):
    return jax.ShapeDtypeStruct(shape, dtype)


def fast_shards(
    hidden_in, queries, new_keys, new_values, cache_keys, cache_values, route_ids, route_weights, norm_gain,
    gate_weight, up_weight, down_weight, ancestor_counts,
):
    steps, tokens, heads, width = queries.shape
    kv_heads, cached = cache_keys.shape[1:3]
    count = lax.axis_size("expert")
    local, _, units = gate_weight.shape
    experts = local * count
    columns = down_weight.shape[2]
    part = columns // (steps + 1)
    main = steps * part
    rows = (steps + 1) * tokens
    halo = struct((2 * REACH * kv_heads, cached + 16, width), bf16)

    def swap(value, offset):
        return lax.ppermute(value, "expert", [(i, i ^ offset) for i in range(count)])

    def sibling(value):
        return lax.ppermute(value, "tensor", [(0, 1), (1, 0)])

    send, residual, near, far = call(
        functools.partial(attend_kernel, steps, experts),
        (struct((rows, main + LANES), bf16), struct((rows, main), f32), halo, halo),
        [VMEM, VMEM, SMEM] + [VMEM] * 7, "attend", [pltpu.VMEM(((steps + 1) * rows, LANES), f32)],
    )(route_ids, route_weights, ancestor_counts, norm_gain.reshape(1, -1), hidden_in, queries, new_keys, new_values, cache_keys, cache_values)

    even = jnp.concatenate([send] + [swap(send, k) for k in range(2, count, 2)], axis=0)
    near = swap(near, 1)
    odd = swap(even, 1)
    own = jnp.concatenate([even, odd], axis=0)
    other = sibling(own)
    far = lax.ppermute(far, "expert", [(i, ((i + 1) ^ 1) - 1 if 0 < i < count - 1 else i) for i in range(count)])
    hidden = call(
        functools.partial(hidden_kernel, steps, tokens, experts),
        struct((count * rows, local * units), bf16), [VMEM] * 4, "hidden",
    )(own, other, gate_weight, up_weight)
    other_hidden = sibling(hidden)
    half = count // 2 * rows

    def down(first, dtype):
        return call(
            functools.partial(down_kernel, steps, tokens), struct((half, main), dtype), [VMEM] * 3, "down",
        )(hidden[first : first + half], other_hidden[first : first + half], down_weight)

    arrived = swap(down(half, bf16), 1)
    kept = down(0, f32)
    own_block, others = kept[:rows], call(add_kernel, struct((half - rows, main), bf16), [VMEM] * 2, "add")(kept[rows:], arrived[rows:])
    returned = [swap(others[(k // 2 - 1) * rows : k // 2 * rows], k) for k in range(2, count, 2)]
    result = call(functools.partial(total_kernel, len(returned) + 2), struct((rows, main), bf16), [VMEM] * (len(returned) + 3), "total")(
        residual, own_block, arrived[:rows], *returned
    )
    layer_out = call(unpack_kernel, struct((steps, tokens, 2 * columns), bf16), [VMEM] * 2, "unpack")(result, sibling(result))

    counts = own.reshape(count, rows, main + LANES)[:, :tokens, main + 2 * experts + 2].astype(jnp.int32)
    counts = counts.reshape(2, count // 2, tokens).transpose(1, 0, 2).reshape(count, tokens)
    out = struct((tokens, kv_heads, cached + steps, width), bf16)
    keys, values = call(functools.partial(resample_kernel, steps), (out, out), [SMEM] + [VMEM] * 6, "resample")(
        counts, near, far, cache_keys, cache_values, new_keys, new_values
    )
    return layer_out, keys, values


def padded(cells, sides, width):
    for axis, dim in sides:
        count = lax.axis_size(axis)
        ends = count - 1
        head = lax.slice_in_dim(cells, 0, width, axis=dim)
        tail = lax.slice_in_dim(cells, cells.shape[dim] - width, cells.shape[dim], axis=dim)
        cells = jnp.concatenate(
            [
                lax.ppermute(tail, axis, [(i, (i + 1) % count) for i in range(ends)]),
                cells,
                lax.ppermute(head, axis, [((i + 1) % count, i) for i in range(ends)]),
            ],
            axis=dim,
        )
    return cells


def shards(
    hidden_in,
    queries,
    new_keys,
    new_values,
    cache_keys,
    cache_values,
    route_ids,
    route_weights,
    norm_gain,
    gate_weight,
    up_weight,
    down_weight,
    ancestor_counts,
):
    step_count, token_count, query_heads, head_width = queries.shape
    key_heads = cache_keys.shape[1]
    cached = cache_keys.shape[2]
    group_size = query_heads // key_heads
    cache_pair = jnp.stack([cache_keys, cache_values])
    fresh_pair = jnp.transpose(jnp.stack([new_keys, new_values]), (0, 2, 3, 1, 4))
    both_kv = jnp.concatenate([cache_pair, fresh_pair], axis=3)
    length = both_kv.shape[3]
    grouped = queries.reshape(step_count, token_count, key_heads, group_size, head_width)
    scores = jnp.einsum(
        "sphgd,phld->sphgl", grouped, both_kv[0], preferred_element_type=jnp.float32
    ) / math.sqrt(head_width)
    allowed = lax.broadcasted_iota(
        jnp.int32, (step_count, length), 1
    ) <= cached + lax.broadcasted_iota(jnp.int32, (step_count, length), 0)
    scores = jnp.where(allowed[:, None, None, None, :], scores, -1e30)
    exponent = jnp.exp(scores - jnp.max(scores, axis=-1, keepdims=True))
    attn_weights = (exponent / jnp.sum(exponent, axis=-1, keepdims=True)).astype(jnp.bfloat16)
    attended = jnp.einsum(
        "sphgl,phld->sphgd", attn_weights, both_kv[1], preferred_element_type=jnp.float32
    )
    attended = attended.astype(jnp.bfloat16).reshape(
        step_count, token_count, query_heads * head_width
    )
    attended = lax.all_gather(attended, "tensor", axis=2, tiled=True)
    expert_count = lax.axis_size("expert")
    group_count = lax.axis_size("group")
    tensor_count = lax.axis_size("tensor")
    tensor_index = lax.axis_index("tensor")
    expert_local = gate_weight.shape[0]
    experts_all = expert_local * expert_count
    chosen_count = route_ids.shape[2]
    model_width = hidden_in.shape[2]
    column_width = down_weight.shape[2]
    capacity = min(token_count, max(2, 2 * token_count * chosen_count // experts_all))
    pair_count = token_count * chosen_count
    expert_iota = jnp.arange(experts_all, dtype=jnp.int32)
    slot_iota = jnp.arange(capacity, dtype=jnp.int32)
    token_owner = (
        (jnp.arange(pair_count) // chosen_count)[:, None] == jnp.arange(token_count)[None, :]
    ).astype(jnp.float32)
    halves = []
    for step_index in range(step_count):
        residual = hidden_in[step_index].astype(jnp.float32) + attended[step_index].astype(
            jnp.float32
        )
        normed = (
            residual
            * lax.rsqrt(jnp.mean(residual * residual, axis=-1, keepdims=True) + epsilon)
            * norm_gain
        ).astype(jnp.bfloat16)
        chosen = route_ids[step_index].reshape(pair_count)
        route_share = route_weights[step_index] / jnp.sum(
            route_weights[step_index], axis=-1, keepdims=True
        )
        expert_hits = (chosen[:, None] == expert_iota[None, :]).astype(jnp.int32)
        position = jnp.sum((jnp.cumsum(expert_hits, axis=0) - expert_hits) * expert_hits, axis=1)
        slotted = (
            expert_hits[:, :, None]
            * (position[:, None, None] == slot_iota[None, None, :]).astype(jnp.int32)
        ).astype(jnp.float32)
        dispatch = jnp.einsum("rec,rt->ect", slotted, token_owner, precision=highest)
        dispatch = dispatch.reshape(expert_count, expert_local, capacity, token_count).astype(
            jnp.bfloat16
        )
        combine = jnp.einsum(
            "rec,rt,r->tec",
            slotted,
            token_owner,
            route_share.reshape(pair_count),
            precision=highest,
        )
        combine = combine.reshape(token_count, expert_count, expert_local, capacity)
        feature_blocks = normed.reshape(token_count, group_count, model_width // group_count)
        outgoing = jnp.einsum(
            "aict,tgd->agicd", dispatch, feature_blocks, preferred_element_type=jnp.float32
        ).astype(jnp.bfloat16)
        flattened = outgoing.reshape(
            expert_count * group_count, expert_local, capacity, model_width // group_count
        )
        received = lax.all_to_all(
            flattened, ("expert", "group"), split_axis=0, concat_axis=0, tiled=True
        )
        gate_part = jnp.einsum(
            "seki,eif->sekf", received, gate_weight, preferred_element_type=jnp.float32
        ).astype(jnp.bfloat16)
        up_part = jnp.einsum(
            "seki,eif->sekf", received, up_weight, preferred_element_type=jnp.float32
        ).astype(jnp.bfloat16)
        gate_sum = lax.psum(gate_part, "group").astype(jnp.float32)
        up_sum = lax.psum(up_part, "group").astype(jnp.float32)
        hidden = (jax.nn.silu(gate_sum) * up_sum).astype(jnp.bfloat16)
        hidden = lax.all_gather(hidden, "tensor", axis=3, tiled=True)
        answered = jnp.einsum(
            "sekf,efo->seko", hidden, down_weight, preferred_element_type=jnp.float32
        ).astype(jnp.bfloat16)
        returned = lax.all_to_all(
            answered, ("expert", "group"), split_axis=0, concat_axis=0, tiled=True
        )
        returned = returned.reshape(
            expert_count, group_count, expert_local, capacity, column_width
        ).astype(jnp.float32)
        expert_mix = jnp.einsum("taic,agicd->tgd", combine, returned, precision=highest)
        own_columns = lax.dynamic_index_in_dim(
            residual.reshape(token_count, group_count, tensor_count, column_width),
            tensor_index,
            2,
            keepdims=False,
        )
        halves.append((own_columns + expert_mix).astype(jnp.bfloat16))
    stacked = jnp.stack(halves)
    layer_out = lax.all_gather(stacked, "tensor", axis=3, tiled=True).reshape(
        step_count, token_count, model_width
    )
    every_count = lax.all_gather(ancestor_counts, ("expert", "group"), axis=0, tiled=True)
    running = jnp.cumsum(every_count)
    first_index = lax.axis_index(("expert", "group")) * token_count
    own_index = first_index + jnp.arange(token_count, dtype=jnp.int32)
    ancestor = jnp.sum((running[None, :] <= own_index[:, None]).astype(jnp.int32), axis=1)
    widened = padded(both_kv, ((("expert", "group"), 1),), REACH)
    window_index = first_index - REACH + jnp.arange(token_count + 2 * REACH, dtype=jnp.int32)
    selector = (ancestor[:, None] == window_index[None, :]).astype(jnp.bfloat16)
    resampled = jnp.einsum(
        "tw,kwhld->kthld", selector, widened, preferred_element_type=jnp.float32
    ).astype(jnp.bfloat16)
    return (layer_out, resampled[0], resampled[1])


def solution(mesh):
    count = mesh.shape["expert"]
    fast = mesh.shape["group"] == 1 and mesh.shape["tensor"] == 2 and count % 2 == 0 and count & (count - 1) == 0
    in_specs = (
        P(None, ("parts", "expert", "group"), None),
        P(None, ("parts", "expert", "group"), "tensor", None),
        P(None, ("parts", "expert", "group"), "tensor", None),
        P(None, ("parts", "expert", "group"), "tensor", None),
        P(("parts", "expert", "group"), "tensor", None, None),
        P(("parts", "expert", "group"), "tensor", None, None),
        P(None, ("parts", "expert", "group"), None),
        P(None, ("parts", "expert", "group"), None),
        P(),
        P("expert", "group", "tensor"),
        P("expert", "group", "tensor"),
        P("expert", None, ("group", "tensor")),
        P(("parts", "expert", "group")),
    )
    out_specs = (
        P(None, ("parts", "expert", "group"), None),
        P(("parts", "expert", "group"), "tensor", None, None),
        P(("parts", "expert", "group"), "tensor", None, None),
    )
    return jax.shard_map(fast_shards if fast else shards, mesh=mesh, in_specs=in_specs, out_specs=out_specs, check_vma=False)
```

```python
import functools
import math

import jax
import jax.numpy as jnp
from jax import lax
from jax.experimental import pallas as pl
from jax.experimental.pallas import tpu as pltpu
from jax.sharding import PartitionSpec as P

REACH = 2
LANES = 128
PAD = 8
f32, bf16 = jnp.float32, jnp.bfloat16

epsilon = 1e-06
highest = lax.Precision.HIGHEST


def dot(a, b, dims=((1,), (0,))):
    return lax.dot_general(a, b, (dims, ((), ())), preferred_element_type=f32)


def iota(shape, dim):
    return lax.broadcasted_iota(jnp.int32, shape, dim)


def load_kernel(
    steps, ids_in, weights_in, counts_in, gain_in, hidden_in, q_in, nk_in, nv_in, ck_in, cv_in,
    ids_ref, weights_ref, counts_ref, gain_ref, hidden_ref, q_ref, nk_ref, nv_ref, ck_ref, cv_ref, near_ref, far_ref, sems,
):
    pairs = (
        (ck_in, ck_ref), (cv_in, cv_ref), (nk_in, nk_ref), (nv_in, nv_ref), (q_in, q_ref), (hidden_in, hidden_ref),
        (gain_in, gain_ref), (ids_in, ids_ref), (weights_in, weights_ref), (counts_in, counts_ref),
    )
    copies = [pltpu.make_async_copy(source, target, sems.at[n]) for n, (source, target) in enumerate(pairs)]
    for copy in copies:
        copy.start()
    for copy in copies:
        copy.wait()
    tokens, kv_heads, cached, width = ck_ref.shape

    odd = lax.rem(lax.axis_index("expert"), 2)
    per = REACH * kv_heads

    early = near_ref.shape[0]

    def halo(start, kinds, slot):
        for cache_ref, new_ref in kinds:
            for r in range(REACH):
                for h in range(kv_heads):
                    out_ref, at = (near_ref, slot) if slot < early else (far_ref, slot - early)
                    out_ref[at, :cached, :] = cache_ref[start + r, h]
                    new = jnp.concatenate(
                        [new_ref[s, start + r, h : h + 1, :].astype(f32) for s in range(steps)]
                        + [jnp.zeros((PAD - steps, width), f32)], axis=0)
                    out_ref[at, cached:, :] = new.astype(bf16)
                    slot += 1

    keys, values = (ck_ref, nk_ref), (cv_ref, nv_ref)
    tail = tokens - REACH

    @pl.when(odd == 0)
    def _():
        halo(tail, (keys, values), 0)
        halo(0, (keys, values), 2 * per)

    @pl.when(odd == 1)
    def _():
        halo(0, (keys, values), 0)
        halo(tail, (keys, values), 2 * per)


def weight_kernel(after_ref, source, target, token_ref, sems):
    copies = []
    part = source.shape[1] // 2
    for e in range(source.shape[0]):
        for k in range(2):
            at = pl.ds(k * part, part)
            copies.append(pltpu.make_async_copy(source.at[e, at], target.at[e, at], sems.at[len(copies)]))
    for copy in copies:
        copy.start()
    for copy in copies:
        copy.wait()
    token_ref[...] = jnp.zeros_like(token_ref)


def attend_kernel(
    steps, experts, ids_ref, weights_ref, counts_ref, gain_ref, hidden_ref, q_ref, nk_ref, nv_ref, ck_ref, cv_ref,
    send_ref, residual_ref, scores_ref,
):
    tokens, heads, width = q_ref.shape[1:]
    kv_heads, cached = ck_ref.shape[1:3]
    group = heads // kv_heads
    columns = heads * width
    part = columns // (steps + 1)
    main = steps * part
    rows = (steps + 1) * tokens
    base = lax.axis_index("tensor") * columns
    fresh = steps * kv_heads
    fresh_rows = -(-fresh // 16) * 16
    scale = 1.0 / math.sqrt(width)

    q_rows = steps * heads
    row = iota((q_rows, kv_heads * cached), 0)
    col = iota((q_rows, kv_heads * cached), 1)
    own_head = lax.div(lax.rem(row, heads), group) == lax.div(col, cached)
    row = iota((q_rows, fresh_rows), 0)
    col = iota((q_rows, fresh_rows), 1)
    own_new = (
        (lax.div(lax.rem(row, heads), group) == lax.rem(col, kv_heads))
        & (lax.div(col, kv_heads) <= lax.div(row, heads))
        & (col < fresh)
    )
    outputs = []
    for p in range(tokens):
        q = jnp.concatenate([q_ref[s, p] for s in range(steps)], axis=0)

        def with_new(new_ref):
            pieces = [new_ref[s, p].astype(f32) for s in range(steps)]
            return jnp.concatenate(pieces + [jnp.zeros((fresh_rows - fresh, width), f32)], axis=0).astype(bf16)

        keys = ck_ref[p].reshape(kv_heads * cached, width)
        values = cv_ref[p].reshape(kv_heads * cached, width)
        old = jnp.where(own_head, dot(q, keys, ((1,), (1,))) * scale, -1e30)
        new = jnp.where(own_new, dot(q, with_new(nk_ref), ((1,), (1,))) * scale, -1e30)
        top = jnp.maximum(jnp.max(old, axis=1, keepdims=True), jnp.max(new, axis=1, keepdims=True))
        old = jnp.exp(old - top)
        new = jnp.exp(new - top)
        total = jnp.sum(old, axis=1, keepdims=True) + jnp.sum(new, axis=1, keepdims=True)
        old = (old / total).astype(bf16)
        new = (new / total).astype(bf16)
        outputs.append((dot(old, values) + dot(new, with_new(nv_ref))).astype(bf16))
    attended = jnp.concatenate(outputs, axis=0)

    tiles = main // width
    count = tokens * q_rows
    target = iota((tiles * rows, count), 0)
    tile, inner = lax.div(target, rows), lax.rem(target, rows)
    is_extra = inner >= steps * tokens
    step = jnp.where(is_extra, lax.div(tile, part // width), lax.div(inner, tokens))
    token = lax.rem(inner, tokens)
    head = jnp.where(is_extra, tiles + lax.rem(tile, part // width), tile)
    chosen = (token * q_rows + step * heads + head) == iota((tiles * rows, count), 1)
    moved = dot(chosen.astype(f32).astype(bf16), attended)
    for s in range(steps):
        residual_ref[s * tokens : (s + 1) * tokens, :] = hidden_ref[s, :, pl.ds(pl.multiple_of(base, LANES), main)].astype(f32)
        residual_ref[steps * tokens :, s * part : (s + 1) * part] = hidden_ref[
            s, :, pl.ds(pl.multiple_of(base + main, LANES), part)
        ].astype(f32)
    residual = residual_ref[...] + jnp.concatenate([moved[j * rows : (j + 1) * rows] for j in range(tiles)], axis=1)
    residual_ref[...] = residual
    gain_main = gain_ref[:, pl.ds(pl.multiple_of(base, LANES), main)]
    gain_last = gain_ref[:, pl.ds(pl.multiple_of(base + main, LANES), part)]
    in_main = iota((rows, main), 0) < steps * tokens
    gain = jnp.where(in_main, gain_main, jnp.concatenate([gain_last] * steps, axis=1))
    send_ref[:, :main] = (residual * gain).astype(bf16)

    squares = residual * residual
    lane = iota((tokens, LANES), 1)
    for s in range(steps):
        scores_ref[s * rows : (s + 1) * rows, :] = jnp.broadcast_to(
            jnp.sum(squares[:, s * part : (s + 1) * part], axis=1, keepdims=True), (rows, LANES))
    whole = sum(scores_ref[s * rows : (s + 1) * rows, :] for s in range(steps))
    scores_ref[steps * rows :, :] = whole
    pieces = []
    for s in range(steps):
        square_sum = (
            scores_ref[steps * rows + s * tokens : steps * rows + (s + 1) * tokens, :]
            + scores_ref[s * rows + steps * tokens : (s + 1) * rows, :]
        )
        ids, weights = ids_ref[s], weights_ref[s]
        share = weights / jnp.sum(weights, axis=1, keepdims=True)
        value = jnp.zeros((tokens, LANES), f32)
        expert = jnp.where(lane < experts, lane, lane - experts)
        for k in range(ids.shape[1]):
            value = jnp.where(ids[:, k : k + 1] == expert, share[:, k : k + 1], value)
        value = jnp.where(lane < 2 * experts, value, square_sum)
        high = value.astype(bf16).astype(f32)
        low = value - high
        piece = jnp.where((lane < experts) | (lane == 2 * experts), high, low)
        piece = jnp.where(lane < 2 * experts + 2, piece, 0.0)
        if s == 0:
            for p in range(tokens):
                here = (lane == 2 * experts + 2) & (iota((tokens, LANES), 0) == p)
                piece = jnp.where(here, counts_ref[p].astype(f32), piece)
        pieces.append(piece)
    pieces.append(jnp.zeros((tokens, LANES), f32))
    send_ref[:, main:] = jnp.concatenate(pieces, axis=0).astype(bf16)


def unpacking(blocks, steps, tokens, s, back):
    rows = (steps + 1) * tokens
    target, source = iota((blocks * rows, blocks * rows), 0), iota((blocks * rows, blocks * rows), 1)
    if back:
        target, source = source, target
    hit = (target + (steps - s) * tokens == source) & (lax.div(lax.rem(target, rows), tokens) == s)
    return hit.astype(f32).astype(bf16)


def halves(even_ref, odd_ref, at):
    return jnp.concatenate([even_ref[:, at], odd_ref[:, at]], axis=0)


def expert_products(steps, tokens, features, gate_ref, up_ref, half):
    total, main = features.shape
    rows = (steps + 1) * tokens
    part = main // steps
    columns = main + part
    local = gate_ref.shape[0]
    blocks = total // rows
    extra = sum(
        dot(unpacking(blocks, steps, tokens, s, False), features[:, s * part : (s + 1) * part]) for s in range(steps)
    ).astype(bf16)
    first = pl.ds(pl.multiple_of(half * columns, LANES), main)
    last = pl.ds(pl.multiple_of(half * columns + main, LANES), part)
    return [
        dot(features, ref[e, first, :]) + dot(extra, ref[e, last, :]) for ref in (gate_ref, up_ref) for e in range(local)
    ]


def partial_kernel(steps, tokens, after_ref, also_after_ref, even_ref, odd_ref, gate_ref, up_ref, out_ref):
    main = even_ref.shape[1] - LANES
    products = expert_products(steps, tokens, halves(even_ref, odd_ref, slice(0, main)), gate_ref, up_ref, lax.axis_index("tensor"))
    for n, product in enumerate(products):
        out_ref[n] = product


def hidden_kernel(steps, tokens, experts, partial_ref, even_ref, odd_ref, even_other_ref, odd_other_ref, gate_ref, up_ref, out_ref):
    main = even_ref.shape[1] - LANES
    total = 2 * even_ref.shape[0]
    rows = (steps + 1) * tokens
    columns = main + main // steps
    local, _, units = gate_ref.shape
    features = halves(even_other_ref, odd_other_ref, slice(0, main))
    products = expert_products(steps, tokens, features, gate_ref, up_ref, 1 - lax.axis_index("tensor"))
    meta = halves(even_ref, odd_ref, slice(main, None)).astype(f32)
    meta_other = halves(even_other_ref, odd_other_ref, slice(main, None)).astype(f32)
    lane = iota(meta.shape, 1)
    valid = lax.rem(iota((total, 1), 0), rows) < steps * tokens
    in_squares = (lane == 2 * experts) | (lane == 2 * experts + 1)
    square_sum = jnp.sum(jnp.where(in_squares, meta + meta_other, 0.0), axis=1, keepdims=True)
    factor = jnp.where(valid, lax.rsqrt(square_sum / (2 * columns) + epsilon), 0.0)
    first_expert = lax.axis_index("expert") * local
    for e in range(local):
        at = first_expert + e
        share = jnp.sum(jnp.where((lane == at) | (lane == at + experts), meta, 0.0), axis=1, keepdims=True)
        gate = ((partial_ref[e] + products[e]) * factor).astype(bf16).astype(f32)
        up = ((partial_ref[local + e] + products[local + e]) * factor).astype(bf16).astype(f32)
        hidden = gate / (1.0 + jnp.exp(-gate)) * up * share
        out_ref[:, e * units : (e + 1) * units] = hidden.astype(bf16)


def down_kernel(steps, tokens, begin, own_ref, other_ref, down_ref, out_ref):
    total, width = out_ref.shape[0], own_ref.shape[1]
    local, _, columns = down_ref.shape
    units = width // local
    rows = (steps + 1) * tokens
    part = columns // (steps + 1)
    main = steps * part
    blocks = total // rows
    mine = lax.axis_index("tensor")
    product = 0.0
    for ref, half in ((own_ref, mine), (other_ref, 1 - mine)):
        start = pl.multiple_of(half * units, LANES)
        for e in range(local):
            product += dot(ref[begin : begin + total, e * units : (e + 1) * units], down_ref[e, pl.ds(start, units), :])
    last = product[:, main:].astype(bf16)
    extra = jnp.concatenate([dot(unpacking(blocks, steps, tokens, s, True), last) for s in range(steps)], axis=1)
    in_main = lax.rem(iota((total, main), 0), rows) < steps * tokens
    out_ref[...] = jnp.where(in_main, product[:, :main], extra).astype(out_ref.dtype)


def resample_kernel(steps, early, counts_ref, near_ref, relay_ref, ck_ref, cv_ref, nk_ref, nv_ref, keys_ref, values_ref):
    tokens, kv_heads, cached, width = ck_ref.shape
    devices = counts_ref.shape[0]
    me = lax.axis_index("expert")
    first = me * tokens
    odd = lax.rem(me, 2)
    per = REACH * kv_heads
    running = jnp.int32(0)
    ancestors = [jnp.int32(0)] * tokens
    for d in range(devices):
        k = jnp.bitwise_xor(me, d)
        for p in range(tokens):
            running = running + counts_ref[k, p]
            for i in range(tokens):
                ancestors[i] = ancestors[i] + (running <= first + i).astype(jnp.int32)

    for i in range(tokens):
        offset = ancestors[i] - first

        @pl.when((offset >= 0) & (offset < tokens))
        def _():
            for out_ref, cache_ref, new_ref in ((keys_ref, ck_ref, nk_ref), (values_ref, cv_ref, nv_ref)):
                out_ref[i, :cached] = jnp.swapaxes(cache_ref[offset], 0, 1)
                for s in range(steps):
                    out_ref[i, cached + s] = new_ref[s, offset]

        def from_halo(ref, at):
            for kind, out_ref in enumerate((keys_ref, values_ref)):
                slots = ref[pl.ds(kind * per + at * kv_heads, kv_heads)]
                out_ref[i] = jnp.swapaxes(slots[:, : cached + steps], 0, 1)

        left = offset < 0
        near = (left & (odd == 1)) | ((offset >= tokens) & (odd == 0))
        far = (left & (odd == 0)) | ((offset >= tokens) & (odd == 1))
        at = jnp.where(left, offset + REACH, offset - tokens)

        @pl.when(near)
        def _():
            from_halo(near_ref, at)

        @pl.when(far)
        def _():
            from_halo(relay_ref, at)


def add_kernel(a_ref, b_ref, out_ref):
    out_ref[...] = (a_ref[...] + b_ref[...].astype(f32)).astype(out_ref.dtype)


def total_kernel(count, *refs):
    out_ref = refs[-1]
    value = refs[0][...]
    for ref in refs[1 : count + 1]:
        value = value + ref[...].astype(f32)
    out_ref[...] = value.astype(out_ref.dtype)


def unpack_kernel(own_ref, other_ref, out_ref):
    steps, tokens, model_width = out_ref.shape
    columns = model_width // 2
    main = own_ref.shape[1]
    part = main // steps
    mine = lax.axis_index("tensor")
    for ref, half in ((own_ref, mine), (other_ref, 1 - mine)):
        block = ref[...].astype(f32)
        first = pl.multiple_of(half * columns, LANES)
        last = pl.multiple_of(half * columns + main, LANES)
        for s in range(steps):
            out_ref[s, :, pl.ds(first, main)] = block[s * tokens : (s + 1) * tokens].astype(bf16)
            out_ref[s, :, pl.ds(last, part)] = block[steps * tokens :, s * part : (s + 1) * part].astype(bf16)


VMEM = pl.BlockSpec(memory_space=pltpu.VMEM)
SMEM = pl.BlockSpec(memory_space=pltpu.SMEM)
HBM = pl.BlockSpec(memory_space=pltpu.HBM)


def call(kernel, out, specs, name, microseconds, scratch=(), limit=20):
    outs = jax.tree.map(lambda _: VMEM, out)
    return pl.pallas_call(
        kernel, out_shape=out, in_specs=specs, out_specs=outs, scratch_shapes=scratch, name=name,
        cost_estimate=pl.CostEstimate(flops=0, bytes_accessed=int(microseconds * 3.5e6), transcendentals=0),
        compiler_params=pltpu.CompilerParams(vmem_limit_bytes=limit << 20),
    )


def struct(shape, dtype):
    return jax.ShapeDtypeStruct(shape, dtype)


def in_hbm(value):
    return pltpu.with_memory_space_constraint(value, pltpu.HBM)


def fast_shards(
    hidden_in, queries, new_keys, new_values, cache_keys, cache_values, route_ids, route_weights, norm_gain,
    gate_weight, up_weight, down_weight, ancestor_counts,
):
    steps, tokens, heads, width = queries.shape
    kv_heads, cached = cache_keys.shape[1:3]
    count = lax.axis_size("expert")
    local, _, units = gate_weight.shape
    experts = local * count
    columns = down_weight.shape[2]
    part = columns // (steps + 1)
    main = steps * part
    rows = (steps + 1) * tokens
    per = REACH * kv_heads
    early = 2 * per + per // 2
    halos = [pltpu.VMEM((slots, cached + PAD, width), bf16) for slots in (early, 4 * per - early)]

    def swap(value, offset):
        return lax.ppermute(value, "expert", [(i, i ^ offset) for i in range(count)])

    def sibling(value):
        return lax.ppermute(value, "tensor", [(0, 1), (1, 0)])

    inputs = (route_ids, route_weights, ancestor_counts, norm_gain.reshape(1, -1), hidden_in, queries, new_keys, new_values, cache_keys, cache_values)
    spaces = [pltpu.SMEM if value is ancestor_counts else pltpu.VMEM for value in inputs]
    loaded = pl.pallas_call(
        functools.partial(load_kernel, steps),
        out_shape=[space(value.shape, value.dtype) for space, value in zip(spaces, inputs)] + halos,
        in_specs=[HBM] * len(inputs), out_specs=[pl.BlockSpec(memory_space=space) for space in spaces] + [VMEM] * 2,
        scratch_shapes=[pltpu.SemaphoreType.DMA((len(inputs),))], name="load",
        compiler_params=pltpu.CompilerParams(vmem_limit_bytes=20 << 20),
    )(*(in_hbm(value) for value in inputs))
    *loaded, near, far = loaded
    near = swap(near, 1)
    new_keys, new_values, cache_keys, cache_values = loaded[6:]
    send, residual = call(
        functools.partial(attend_kernel, steps, experts),
        (struct((rows, main + LANES), bf16), struct((rows, main), f32)),
        [VMEM, VMEM, SMEM] + [VMEM] * 7, "attend", 2.3, [pltpu.VMEM(((steps + 1) * rows, LANES), f32)],
    )(*loaded)

    def fetch(after, weight, name):
        return pl.pallas_call(
            weight_kernel, out_shape=[pltpu.VMEM(weight.shape, weight.dtype), pltpu.VMEM((8, LANES), f32)],
            in_specs=[VMEM, HBM], out_specs=[VMEM] * 2, scratch_shapes=[pltpu.SemaphoreType.DMA((2 * local,))], name=name,
            cost_estimate=pl.CostEstimate(flops=0, bytes_accessed=7_000_000, transcendentals=0),
            compiler_params=pltpu.CompilerParams(vmem_limit_bytes=16 << 20),
        )(after, in_hbm(weight))

    gate, token = fetch(residual, gate_weight, "gate")
    even = jnp.concatenate([send] + [swap(send, k) for k in range(2, count, 2)], axis=0)
    even, near, token = lax.optimization_barrier((even, near, token))
    odd = swap(even, 1)
    even_other = sibling(even)
    up, token_up = fetch(even, up_weight, "up")
    odd, token_up, far = lax.optimization_barrier((odd, token_up, far))
    relayed = swap(far, 1)
    odd_other = sibling(odd)
    partial = call(
        functools.partial(partial_kernel, steps, tokens), struct((2 * local, count * rows, units), f32), [VMEM] * 6, "partial", 0.01,
    )(token, token_up, even, odd, gate, up)
    hidden = call(
        functools.partial(hidden_kernel, steps, tokens, experts),
        struct((count * rows, local * units), bf16), [VMEM] * 7, "hidden", 0.01,
    )(partial, even, odd, even_other, odd_other, gate, up)
    other_hidden = sibling(hidden)
    half = count // 2 * rows

    def down(first, dtype):
        return call(
            functools.partial(down_kernel, steps, tokens, first), struct((half, main), dtype), [VMEM] * 3, "down", 0.01,
        )(hidden, other_hidden, down_weight)

    leaving, relayed = lax.optimization_barrier((down(half, bf16), relayed))
    arrived = swap(leaving, 1)
    ring = [(i, min(i + 2, count - 1) if i % 2 == 0 else max(i - 2, 0)) for i in range(count)]
    far = lax.ppermute(jnp.concatenate([near[2 * per :], relayed], axis=0), "expert", ring)
    kept = down(0, f32)
    own_block, others = kept[:rows], call(add_kernel, struct((half - rows, main), bf16), [VMEM] * 2, "add", 0.1)(kept[rows:], arrived[rows:])

    counts = jnp.stack([even, odd], 0).reshape(2, count // 2, rows, main + LANES)[:, :, :tokens, main + 2 * experts + 2].astype(jnp.int32)
    counts = counts.transpose(1, 0, 2).reshape(count, tokens)
    out = struct((tokens, cached + steps, kv_heads, width), bf16)
    keys, values = call(functools.partial(resample_kernel, steps, early), (out, out), [SMEM] + [VMEM] * 6, "resample", 2.2)(
        counts, near, far, cache_keys, cache_values, new_keys, new_values
    )
    returned = [swap(others[(k // 2 - 1) * rows : k // 2 * rows], k) for k in range(2, count, 2)]
    keys, values, *returned = lax.optimization_barrier((keys, values, *returned))
    result = call(functools.partial(total_kernel, len(returned) + 2), struct((rows, main), bf16), [VMEM] * (len(returned) + 3), "total", 0.1)(
        residual, own_block, arrived[:rows], *returned
    )
    layer_out = call(unpack_kernel, struct((steps, tokens, 2 * columns), bf16), [VMEM] * 2, "unpack", 0.5)(result, sibling(result))
    return layer_out, keys.transpose(0, 2, 1, 3), values.transpose(0, 2, 1, 3)


def padded(cells, sides, width):
    for axis, dim in sides:
        count = lax.axis_size(axis)
        ends = count - 1
        head = lax.slice_in_dim(cells, 0, width, axis=dim)
        tail = lax.slice_in_dim(cells, cells.shape[dim] - width, cells.shape[dim], axis=dim)
        cells = jnp.concatenate(
            [
                lax.ppermute(tail, axis, [(i, (i + 1) % count) for i in range(ends)]),
                cells,
                lax.ppermute(head, axis, [((i + 1) % count, i) for i in range(ends)]),
            ],
            axis=dim,
        )
    return cells


def shards(
    hidden_in,
    queries,
    new_keys,
    new_values,
    cache_keys,
    cache_values,
    route_ids,
    route_weights,
    norm_gain,
    gate_weight,
    up_weight,
    down_weight,
    ancestor_counts,
):
    step_count, token_count, query_heads, head_width = queries.shape
    key_heads = cache_keys.shape[1]
    cached = cache_keys.shape[2]
    group_size = query_heads // key_heads
    cache_pair = jnp.stack([cache_keys, cache_values])
    fresh_pair = jnp.transpose(jnp.stack([new_keys, new_values]), (0, 2, 3, 1, 4))
    both_kv = jnp.concatenate([cache_pair, fresh_pair], axis=3)
    length = both_kv.shape[3]
    grouped = queries.reshape(step_count, token_count, key_heads, group_size, head_width)
    scores = jnp.einsum(
        "sphgd,phld->sphgl", grouped, both_kv[0], preferred_element_type=jnp.float32
    ) / math.sqrt(head_width)
    allowed = lax.broadcasted_iota(
        jnp.int32, (step_count, length), 1
    ) <= cached + lax.broadcasted_iota(jnp.int32, (step_count, length), 0)
    scores = jnp.where(allowed[:, None, None, None, :], scores, -1e30)
    exponent = jnp.exp(scores - jnp.max(scores, axis=-1, keepdims=True))
    attn_weights = (exponent / jnp.sum(exponent, axis=-1, keepdims=True)).astype(jnp.bfloat16)
    attended = jnp.einsum(
        "sphgl,phld->sphgd", attn_weights, both_kv[1], preferred_element_type=jnp.float32
    )
    attended = attended.astype(jnp.bfloat16).reshape(
        step_count, token_count, query_heads * head_width
    )
    attended = lax.all_gather(attended, "tensor", axis=2, tiled=True)
    expert_count = lax.axis_size("expert")
    group_count = lax.axis_size("group")
    tensor_count = lax.axis_size("tensor")
    tensor_index = lax.axis_index("tensor")
    expert_local = gate_weight.shape[0]
    experts_all = expert_local * expert_count
    chosen_count = route_ids.shape[2]
    model_width = hidden_in.shape[2]
    column_width = down_weight.shape[2]
    capacity = min(token_count, max(2, 2 * token_count * chosen_count // experts_all))
    pair_count = token_count * chosen_count
    expert_iota = jnp.arange(experts_all, dtype=jnp.int32)
    slot_iota = jnp.arange(capacity, dtype=jnp.int32)
    token_owner = (
        (jnp.arange(pair_count) // chosen_count)[:, None] == jnp.arange(token_count)[None, :]
    ).astype(jnp.float32)
    halves = []
    for step_index in range(step_count):
        residual = hidden_in[step_index].astype(jnp.float32) + attended[step_index].astype(
            jnp.float32
        )
        normed = (
            residual
            * lax.rsqrt(jnp.mean(residual * residual, axis=-1, keepdims=True) + epsilon)
            * norm_gain
        ).astype(jnp.bfloat16)
        chosen = route_ids[step_index].reshape(pair_count)
        route_share = route_weights[step_index] / jnp.sum(
            route_weights[step_index], axis=-1, keepdims=True
        )
        expert_hits = (chosen[:, None] == expert_iota[None, :]).astype(jnp.int32)
        position = jnp.sum((jnp.cumsum(expert_hits, axis=0) - expert_hits) * expert_hits, axis=1)
        slotted = (
            expert_hits[:, :, None]
            * (position[:, None, None] == slot_iota[None, None, :]).astype(jnp.int32)
        ).astype(jnp.float32)
        dispatch = jnp.einsum("rec,rt->ect", slotted, token_owner, precision=highest)
        dispatch = dispatch.reshape(expert_count, expert_local, capacity, token_count).astype(
            jnp.bfloat16
        )
        combine = jnp.einsum(
            "rec,rt,r->tec",
            slotted,
            token_owner,
            route_share.reshape(pair_count),
            precision=highest,
        )
        combine = combine.reshape(token_count, expert_count, expert_local, capacity)
        feature_blocks = normed.reshape(token_count, group_count, model_width // group_count)
        outgoing = jnp.einsum(
            "aict,tgd->agicd", dispatch, feature_blocks, preferred_element_type=jnp.float32
        ).astype(jnp.bfloat16)
        flattened = outgoing.reshape(
            expert_count * group_count, expert_local, capacity, model_width // group_count
        )
        received = lax.all_to_all(
            flattened, ("expert", "group"), split_axis=0, concat_axis=0, tiled=True
        )
        gate_part = jnp.einsum(
            "seki,eif->sekf", received, gate_weight, preferred_element_type=jnp.float32
        ).astype(jnp.bfloat16)
        up_part = jnp.einsum(
            "seki,eif->sekf", received, up_weight, preferred_element_type=jnp.float32
        ).astype(jnp.bfloat16)
        gate_sum = lax.psum(gate_part, "group").astype(jnp.float32)
        up_sum = lax.psum(up_part, "group").astype(jnp.float32)
        hidden = (jax.nn.silu(gate_sum) * up_sum).astype(jnp.bfloat16)
        hidden = lax.all_gather(hidden, "tensor", axis=3, tiled=True)
        answered = jnp.einsum(
            "sekf,efo->seko", hidden, down_weight, preferred_element_type=jnp.float32
        ).astype(jnp.bfloat16)
        returned = lax.all_to_all(
            answered, ("expert", "group"), split_axis=0, concat_axis=0, tiled=True
        )
        returned = returned.reshape(
            expert_count, group_count, expert_local, capacity, column_width
        ).astype(jnp.float32)
        expert_mix = jnp.einsum("taic,agicd->tgd", combine, returned, precision=highest)
        own_columns = lax.dynamic_index_in_dim(
            residual.reshape(token_count, group_count, tensor_count, column_width),
            tensor_index,
            2,
            keepdims=False,
        )
        halves.append((own_columns + expert_mix).astype(jnp.bfloat16))
    stacked = jnp.stack(halves)
    layer_out = lax.all_gather(stacked, "tensor", axis=3, tiled=True).reshape(
        step_count, token_count, model_width
    )
    every_count = lax.all_gather(ancestor_counts, ("expert", "group"), axis=0, tiled=True)
    running = jnp.cumsum(every_count)
    first_index = lax.axis_index(("expert", "group")) * token_count
    own_index = first_index + jnp.arange(token_count, dtype=jnp.int32)
    ancestor = jnp.sum((running[None, :] <= own_index[:, None]).astype(jnp.int32), axis=1)
    widened = padded(both_kv, ((("expert", "group"), 1),), REACH)
    window_index = first_index - REACH + jnp.arange(token_count + 2 * REACH, dtype=jnp.int32)
    selector = (ancestor[:, None] == window_index[None, :]).astype(jnp.bfloat16)
    resampled = jnp.einsum(
        "tw,kwhld->kthld", selector, widened, preferred_element_type=jnp.float32
    ).astype(jnp.bfloat16)
    return (layer_out, resampled[0], resampled[1])


def solution(mesh):
    count = mesh.shape["expert"]
    fast = mesh.shape["group"] == 1 and mesh.shape["tensor"] == 2 and count % 2 == 0 and count & (count - 1) == 0
    in_specs = (
        P(None, ("parts", "expert", "group"), None),
        P(None, ("parts", "expert", "group"), "tensor", None),
        P(None, ("parts", "expert", "group"), "tensor", None),
        P(None, ("parts", "expert", "group"), "tensor", None),
        P(("parts", "expert", "group"), "tensor", None, None),
        P(("parts", "expert", "group"), "tensor", None, None),
        P(None, ("parts", "expert", "group"), None),
        P(None, ("parts", "expert", "group"), None),
        P(),
        P("expert", "group", "tensor"),
        P("expert", "group", "tensor"),
        P("expert", None, ("group", "tensor")),
        P(("parts", "expert", "group")),
    )
    out_specs = (
        P(None, ("parts", "expert", "group"), None),
        P(("parts", "expert", "group"), "tensor", None, None),
        P(("parts", "expert", "group"), "tensor", None, None),
    )
    return jax.shard_map(fast_shards if fast else shards, mesh=mesh, in_specs=in_specs, out_specs=out_specs, check_vma=False)
```

```python
import functools
import math

import jax
import jax.numpy as jnp
from jax import lax
from jax.experimental import pallas as pl
from jax.experimental.pallas import tpu as pltpu
from jax.sharding import PartitionSpec as P

REACH = 2
LANES = 128
PAD = 8
f32, bf16 = jnp.float32, jnp.bfloat16

epsilon = 1e-06
highest = lax.Precision.HIGHEST


def dot(a, b, dims=((1,), (0,))):
    return lax.dot_general(a, b, (dims, ((), ())), preferred_element_type=f32)


def iota(shape, dim):
    return lax.broadcasted_iota(jnp.int32, shape, dim)


def load_kernel(
    steps, ids_in, weights_in, counts_in, gain_in, hidden_in, q_in, nk_in, nv_in, ck_in, cv_in,
    ids_ref, weights_ref, counts_ref, gain_ref, hidden_ref, q_ref, nk_ref, nv_ref, ck_ref, cv_ref, near_ref, far_ref, sems,
):
    pairs = (
        (ck_in, ck_ref), (cv_in, cv_ref), (nk_in, nk_ref), (nv_in, nv_ref), (q_in, q_ref), (hidden_in, hidden_ref),
        (gain_in, gain_ref), (ids_in, ids_ref), (weights_in, weights_ref), (counts_in, counts_ref),
    )
    copies = [pltpu.make_async_copy(source, target, sems.at[n]) for n, (source, target) in enumerate(pairs)]
    for copy in copies:
        copy.start()
    for copy in copies:
        copy.wait()
    tokens, kv_heads, cached, width = ck_ref.shape

    odd = lax.rem(lax.axis_index("expert"), 2)
    per = REACH * kv_heads

    early = near_ref.shape[0]

    def halo(start, kinds, slot):
        for cache_ref, new_ref in kinds:
            for r in range(REACH):
                for h in range(kv_heads):
                    out_ref, at = (near_ref, slot) if slot < early else (far_ref, slot - early)
                    out_ref[at, :cached, :] = cache_ref[start + r, h]
                    new = jnp.concatenate(
                        [new_ref[s, start + r, h : h + 1, :].astype(f32) for s in range(steps)]
                        + [jnp.zeros((PAD - steps, width), f32)], axis=0)
                    out_ref[at, cached:, :] = new.astype(bf16)
                    slot += 1

    keys, values = (ck_ref, nk_ref), (cv_ref, nv_ref)
    tail = tokens - REACH

    @pl.when(odd == 0)
    def _():
        halo(tail, (keys, values), 0)
        halo(0, (keys, values), 2 * per)

    @pl.when(odd == 1)
    def _():
        halo(0, (keys, values), 0)
        halo(tail, (keys, values), 2 * per)


def weight_kernel(after_ref, source, target, token_ref, sems):
    copies = []
    part = source.shape[1] // 2
    for e in range(source.shape[0]):
        for k in range(2):
            at = pl.ds(k * part, part)
            copies.append(pltpu.make_async_copy(source.at[e, at], target.at[e, at], sems.at[len(copies)]))
    for copy in copies:
        copy.start()
    for copy in copies:
        copy.wait()
    token_ref[...] = jnp.zeros_like(token_ref)


def attend_kernel(
    steps, experts, ids_ref, weights_ref, counts_ref, gain_ref, hidden_ref, q_ref, nk_ref, nv_ref, ck_ref, cv_ref,
    send_ref, residual_ref, scores_ref,
):
    tokens, heads, width = q_ref.shape[1:]
    kv_heads, cached = ck_ref.shape[1:3]
    group = heads // kv_heads
    columns = heads * width
    part = columns // (steps + 1)
    main = steps * part
    rows = (steps + 1) * tokens
    base = lax.axis_index("tensor") * columns
    fresh = steps * kv_heads
    fresh_rows = -(-fresh // 16) * 16
    scale = 1.0 / math.sqrt(width)

    q_rows = steps * heads
    row = iota((q_rows, kv_heads * cached), 0)
    col = iota((q_rows, kv_heads * cached), 1)
    own_head = lax.div(lax.rem(row, heads), group) == lax.div(col, cached)
    row = iota((q_rows, fresh_rows), 0)
    col = iota((q_rows, fresh_rows), 1)
    own_new = (
        (lax.div(lax.rem(row, heads), group) == lax.rem(col, kv_heads))
        & (lax.div(col, kv_heads) <= lax.div(row, heads))
        & (col < fresh)
    )
    outputs = []
    for p in range(tokens):
        q = jnp.concatenate([q_ref[s, p] for s in range(steps)], axis=0)

        def with_new(new_ref):
            pieces = [new_ref[s, p].astype(f32) for s in range(steps)]
            return jnp.concatenate(pieces + [jnp.zeros((fresh_rows - fresh, width), f32)], axis=0).astype(bf16)

        keys = ck_ref[p].reshape(kv_heads * cached, width)
        values = cv_ref[p].reshape(kv_heads * cached, width)
        old = jnp.where(own_head, dot(q, keys, ((1,), (1,))) * scale, -1e30)
        new = jnp.where(own_new, dot(q, with_new(nk_ref), ((1,), (1,))) * scale, -1e30)
        top = jnp.maximum(jnp.max(old, axis=1, keepdims=True), jnp.max(new, axis=1, keepdims=True))
        old = jnp.exp(old - top)
        new = jnp.exp(new - top)
        total = jnp.sum(old, axis=1, keepdims=True) + jnp.sum(new, axis=1, keepdims=True)
        old = (old / total).astype(bf16)
        new = (new / total).astype(bf16)
        outputs.append((dot(old, values) + dot(new, with_new(nv_ref))).astype(bf16))
    attended = jnp.concatenate(outputs, axis=0)

    tiles = main // width
    count = tokens * q_rows
    target = iota((tiles * rows, count), 0)
    tile, inner = lax.div(target, rows), lax.rem(target, rows)
    is_extra = inner >= steps * tokens
    step = jnp.where(is_extra, lax.div(tile, part // width), lax.div(inner, tokens))
    token = lax.rem(inner, tokens)
    head = jnp.where(is_extra, tiles + lax.rem(tile, part // width), tile)
    chosen = (token * q_rows + step * heads + head) == iota((tiles * rows, count), 1)
    moved = dot(chosen.astype(f32).astype(bf16), attended)
    for s in range(steps):
        residual_ref[s * tokens : (s + 1) * tokens, :] = hidden_ref[s, :, pl.ds(pl.multiple_of(base, LANES), main)].astype(f32)
        residual_ref[steps * tokens :, s * part : (s + 1) * part] = hidden_ref[
            s, :, pl.ds(pl.multiple_of(base + main, LANES), part)
        ].astype(f32)
    residual = residual_ref[...] + jnp.concatenate([moved[j * rows : (j + 1) * rows] for j in range(tiles)], axis=1)
    residual_ref[...] = residual
    gain_main = gain_ref[:, pl.ds(pl.multiple_of(base, LANES), main)]
    gain_last = gain_ref[:, pl.ds(pl.multiple_of(base + main, LANES), part)]
    in_main = iota((rows, main), 0) < steps * tokens
    gain = jnp.where(in_main, gain_main, jnp.concatenate([gain_last] * steps, axis=1))
    send_ref[:, :main] = (residual * gain).astype(bf16)

    squares = residual * residual
    lane = iota((tokens, LANES), 1)
    for s in range(steps):
        scores_ref[s * rows : (s + 1) * rows, :] = jnp.broadcast_to(
            jnp.sum(squares[:, s * part : (s + 1) * part], axis=1, keepdims=True), (rows, LANES))
    whole = sum(scores_ref[s * rows : (s + 1) * rows, :] for s in range(steps))
    scores_ref[steps * rows :, :] = whole
    pieces = []
    for s in range(steps):
        square_sum = (
            scores_ref[steps * rows + s * tokens : steps * rows + (s + 1) * tokens, :]
            + scores_ref[s * rows + steps * tokens : (s + 1) * rows, :]
        )
        ids, weights = ids_ref[s], weights_ref[s]
        share = weights / jnp.sum(weights, axis=1, keepdims=True)
        value = jnp.zeros((tokens, LANES), f32)
        expert = jnp.where(lane < experts, lane, lane - experts)
        for k in range(ids.shape[1]):
            value = jnp.where(ids[:, k : k + 1] == expert, share[:, k : k + 1], value)
        value = jnp.where(lane < 2 * experts, value, square_sum)
        high = value.astype(bf16).astype(f32)
        low = value - high
        piece = jnp.where((lane < experts) | (lane == 2 * experts), high, low)
        piece = jnp.where(lane < 2 * experts + 2, piece, 0.0)
        if s == 0:
            for p in range(tokens):
                here = (lane == 2 * experts + 2) & (iota((tokens, LANES), 0) == p)
                piece = jnp.where(here, counts_ref[p].astype(f32), piece)
        pieces.append(piece)
    pieces.append(jnp.zeros((tokens, LANES), f32))
    send_ref[:, main:] = jnp.concatenate(pieces, axis=0).astype(bf16)


def unpacking(blocks, steps, tokens, s, back):
    rows = (steps + 1) * tokens
    target, source = iota((blocks * rows, blocks * rows), 0), iota((blocks * rows, blocks * rows), 1)
    if back:
        target, source = source, target
    hit = (target + (steps - s) * tokens == source) & (lax.div(lax.rem(target, rows), tokens) == s)
    return hit.astype(f32).astype(bf16)


def halves(even_ref, odd_ref, at):
    return jnp.concatenate([even_ref[:, at], odd_ref[:, at]], axis=0)


def expert_products(steps, tokens, features, gate_ref, up_ref, half):
    total, main = features.shape
    rows = (steps + 1) * tokens
    part = main // steps
    columns = main + part
    local = gate_ref.shape[0]
    blocks = total // rows
    extra = sum(
        dot(unpacking(blocks, steps, tokens, s, False), features[:, s * part : (s + 1) * part]) for s in range(steps)
    ).astype(bf16)
    first = pl.ds(pl.multiple_of(half * columns, LANES), main)
    last = pl.ds(pl.multiple_of(half * columns + main, LANES), part)
    return [
        dot(features, ref[e, first, :]) + dot(extra, ref[e, last, :]) for ref in (gate_ref, up_ref) for e in range(local)
    ]


def partial_kernel(steps, tokens, after_ref, also_after_ref, even_ref, odd_ref, gate_ref, up_ref, out_ref):
    main = even_ref.shape[1] - LANES
    products = expert_products(steps, tokens, halves(even_ref, odd_ref, slice(0, main)), gate_ref, up_ref, lax.axis_index("tensor"))
    for n, product in enumerate(products):
        out_ref[n] = product


def hidden_kernel(steps, tokens, experts, partial_ref, even_ref, odd_ref, even_other_ref, odd_other_ref, gate_ref, up_ref, out_ref):
    main = even_ref.shape[1] - LANES
    total = 2 * even_ref.shape[0]
    rows = (steps + 1) * tokens
    columns = main + main // steps
    local, _, units = gate_ref.shape
    features = halves(even_other_ref, odd_other_ref, slice(0, main))
    products = expert_products(steps, tokens, features, gate_ref, up_ref, 1 - lax.axis_index("tensor"))
    meta = halves(even_ref, odd_ref, slice(main, None)).astype(f32)
    meta_other = halves(even_other_ref, odd_other_ref, slice(main, None)).astype(f32)
    lane = iota(meta.shape, 1)
    valid = lax.rem(iota((total, 1), 0), rows) < steps * tokens
    in_squares = (lane == 2 * experts) | (lane == 2 * experts + 1)
    square_sum = jnp.sum(jnp.where(in_squares, meta + meta_other, 0.0), axis=1, keepdims=True)
    factor = jnp.where(valid, lax.rsqrt(square_sum / (2 * columns) + epsilon), 0.0)
    first_expert = lax.axis_index("expert") * local
    for e in range(local):
        at = first_expert + e
        share = jnp.sum(jnp.where((lane == at) | (lane == at + experts), meta, 0.0), axis=1, keepdims=True)
        gate = ((partial_ref[e] + products[e]) * factor).astype(bf16).astype(f32)
        up = ((partial_ref[local + e] + products[local + e]) * factor).astype(bf16).astype(f32)
        hidden = gate / (1.0 + jnp.exp(-gate)) * up * share
        out_ref[:, e * units : (e + 1) * units] = hidden.astype(bf16)


def down_kernel(steps, tokens, own_ref, other_ref, down_ref, kept_ref, leaving_ref):
    total, width = own_ref.shape
    local, _, columns = down_ref.shape
    units = width // local
    rows = (steps + 1) * tokens
    part = columns // (steps + 1)
    main = steps * part
    mine = lax.axis_index("tensor")
    product = 0.0
    for ref, half in ((own_ref, mine), (other_ref, 1 - mine)):
        start = pl.multiple_of(half * units, LANES)
        for e in range(local):
            product += dot(ref[:, e * units : (e + 1) * units], down_ref[e, pl.ds(start, units), :])
    last = product[:, main:].astype(bf16)
    extra = jnp.concatenate([dot(unpacking(total // rows, steps, tokens, s, True), last) for s in range(steps)], axis=1)
    in_main = lax.rem(iota((total, main), 0), rows) < steps * tokens
    product = jnp.where(in_main, product[:, :main], extra)
    kept_ref[...] = product[: total // 2]
    leaving_ref[...] = product[total // 2 :].astype(bf16)


def resample_kernel(steps, early, counts_ref, near_ref, relay_ref, ck_ref, cv_ref, nk_ref, nv_ref, keys_ref, values_ref):
    tokens, kv_heads, cached, width = ck_ref.shape
    devices = counts_ref.shape[0]
    me = lax.axis_index("expert")
    first = me * tokens
    odd = lax.rem(me, 2)
    per = REACH * kv_heads
    running = jnp.int32(0)
    ancestors = [jnp.int32(0)] * tokens
    for d in range(devices):
        k = jnp.bitwise_xor(me, d)
        for p in range(tokens):
            running = running + counts_ref[k, p]
            for i in range(tokens):
                ancestors[i] = ancestors[i] + (running <= first + i).astype(jnp.int32)

    for i in range(tokens):
        offset = ancestors[i] - first

        @pl.when((offset >= 0) & (offset < tokens))
        def _():
            for out_ref, cache_ref, new_ref in ((keys_ref, ck_ref, nk_ref), (values_ref, cv_ref, nv_ref)):
                out_ref[i, :cached] = jnp.swapaxes(cache_ref[offset], 0, 1)
                for s in range(steps):
                    out_ref[i, cached + s] = new_ref[s, offset]

        def from_halo(ref, at):
            for kind, out_ref in enumerate((keys_ref, values_ref)):
                slots = ref[pl.ds(kind * per + at * kv_heads, kv_heads)]
                out_ref[i] = jnp.swapaxes(slots[:, : cached + steps], 0, 1)

        left = offset < 0
        near = (left & (odd == 1)) | ((offset >= tokens) & (odd == 0))
        far = (left & (odd == 0)) | ((offset >= tokens) & (odd == 1))
        at = jnp.where(left, offset + REACH, offset - tokens)

        @pl.when(near)
        def _():
            from_halo(near_ref, at)

        @pl.when(far)
        def _():
            from_halo(relay_ref, at)


def add_kernel(a_ref, b_ref, out_ref):
    out_ref[...] = (a_ref[...] + b_ref[...].astype(f32)).astype(out_ref.dtype)


def total_kernel(count, *refs):
    out_ref = refs[-1]
    value = refs[0][...]
    for ref in refs[1 : count + 1]:
        value = value + ref[...].astype(f32)
    out_ref[...] = value.astype(out_ref.dtype)


def unpack_kernel(own_ref, other_ref, out_ref):
    steps, tokens, model_width = out_ref.shape
    columns = model_width // 2
    main = own_ref.shape[1]
    part = main // steps
    mine = lax.axis_index("tensor")
    for ref, half in ((own_ref, mine), (other_ref, 1 - mine)):
        block = ref[...].astype(f32)
        first = pl.multiple_of(half * columns, LANES)
        last = pl.multiple_of(half * columns + main, LANES)
        for s in range(steps):
            out_ref[s, :, pl.ds(first, main)] = block[s * tokens : (s + 1) * tokens].astype(bf16)
            out_ref[s, :, pl.ds(last, part)] = block[steps * tokens :, s * part : (s + 1) * part].astype(bf16)


VMEM = pl.BlockSpec(memory_space=pltpu.VMEM)
SMEM = pl.BlockSpec(memory_space=pltpu.SMEM)
HBM = pl.BlockSpec(memory_space=pltpu.HBM)


def call(kernel, out, specs, name, microseconds, scratch=(), limit=20):
    outs = jax.tree.map(lambda _: VMEM, out)
    return pl.pallas_call(
        kernel, out_shape=out, in_specs=specs, out_specs=outs, scratch_shapes=scratch, name=name,
        cost_estimate=pl.CostEstimate(flops=0, bytes_accessed=int(microseconds * 3.5e6), transcendentals=0),
        compiler_params=pltpu.CompilerParams(vmem_limit_bytes=limit << 20),
    )


def struct(shape, dtype):
    return jax.ShapeDtypeStruct(shape, dtype)


def in_hbm(value):
    return pltpu.with_memory_space_constraint(value, pltpu.HBM)


def fast_shards(
    hidden_in, queries, new_keys, new_values, cache_keys, cache_values, route_ids, route_weights, norm_gain,
    gate_weight, up_weight, down_weight, ancestor_counts,
):
    steps, tokens, heads, width = queries.shape
    kv_heads, cached = cache_keys.shape[1:3]
    count = lax.axis_size("expert")
    local, _, units = gate_weight.shape
    experts = local * count
    columns = down_weight.shape[2]
    part = columns // (steps + 1)
    main = steps * part
    rows = (steps + 1) * tokens
    per = REACH * kv_heads
    early = 2 * per + per // 2
    halos = [pltpu.VMEM((slots, cached + PAD, width), bf16) for slots in (early, 4 * per - early)]

    def swap(value, offset):
        return lax.ppermute(value, "expert", [(i, i ^ offset) for i in range(count)])

    def sibling(value):
        return lax.ppermute(value, "tensor", [(0, 1), (1, 0)])

    inputs = (route_ids, route_weights, ancestor_counts, norm_gain.reshape(1, -1), hidden_in, queries, new_keys, new_values, cache_keys, cache_values)
    spaces = [pltpu.SMEM if value is ancestor_counts else pltpu.VMEM for value in inputs]
    loaded = pl.pallas_call(
        functools.partial(load_kernel, steps),
        out_shape=[space(value.shape, value.dtype) for space, value in zip(spaces, inputs)] + halos,
        in_specs=[HBM] * len(inputs), out_specs=[pl.BlockSpec(memory_space=space) for space in spaces] + [VMEM] * 2,
        scratch_shapes=[pltpu.SemaphoreType.DMA((len(inputs),))], name="load",
        compiler_params=pltpu.CompilerParams(vmem_limit_bytes=20 << 20),
    )(*(in_hbm(value) for value in inputs))
    *loaded, near, far = loaded
    near = swap(near, 1)
    new_keys, new_values, cache_keys, cache_values = loaded[6:]
    send, residual = call(
        functools.partial(attend_kernel, steps, experts),
        (struct((rows, main + LANES), bf16), struct((rows, main), f32)),
        [VMEM, VMEM, SMEM] + [VMEM] * 7, "attend", 2.3, [pltpu.VMEM(((steps + 1) * rows, LANES), f32)],
    )(*loaded)

    def fetch(after, weight, name):
        return pl.pallas_call(
            weight_kernel, out_shape=[pltpu.VMEM(weight.shape, weight.dtype), pltpu.VMEM((8, LANES), f32)],
            in_specs=[VMEM, HBM], out_specs=[VMEM] * 2, scratch_shapes=[pltpu.SemaphoreType.DMA((2 * local,))], name=name,
            cost_estimate=pl.CostEstimate(flops=0, bytes_accessed=7_000_000, transcendentals=0),
            compiler_params=pltpu.CompilerParams(vmem_limit_bytes=16 << 20),
        )(after, in_hbm(weight))

    gate, token = fetch(residual, gate_weight, "gate")
    even = jnp.concatenate([send] + [swap(send, k) for k in range(2, count, 2)], axis=0)
    even, near, token = lax.optimization_barrier((even, near, token))
    odd = swap(even, 1)
    even_other = sibling(even)
    up, token_up = fetch(even, up_weight, "up")
    odd, token_up, far = lax.optimization_barrier((odd, token_up, far))
    relayed = swap(far, 1)
    odd_other = sibling(odd)
    partial = call(
        functools.partial(partial_kernel, steps, tokens), struct((2 * local, count * rows, units), f32), [VMEM] * 6, "partial", 0.01,
    )(token, token_up, even, odd, gate, up)
    hidden = call(
        functools.partial(hidden_kernel, steps, tokens, experts),
        struct((count * rows, local * units), bf16), [VMEM] * 7, "hidden", 0.01,
    )(partial, even, odd, even_other, odd_other, gate, up)
    other_hidden = sibling(hidden)
    half = count // 2 * rows

    kept, leaving = call(
        functools.partial(down_kernel, steps, tokens), (struct((half, main), f32), struct((half, main), bf16)), [VMEM] * 3, "down", 0.01,
    )(hidden, other_hidden, down_weight)
    leaving, relayed = lax.optimization_barrier((leaving, relayed))
    arrived = swap(leaving, 1)
    ring = [(i, i + 2 if i % 2 == 0 else i - 2) for i in range(count) if (i < count - 2 if i % 2 == 0 else i > 1)]
    far = lax.ppermute(jnp.concatenate([near[2 * per :], relayed], axis=0), "expert", ring)
    own_block, others = kept[:rows], call(add_kernel, struct((half - rows, main), bf16), [VMEM] * 2, "add", 0.1)(kept[rows:], arrived[rows:])

    counts = jnp.stack([even, odd], 0).reshape(2, count // 2, rows, main + LANES)[:, :, :tokens, main + 2 * experts + 2].astype(jnp.int32)
    counts = counts.transpose(1, 0, 2).reshape(count, tokens)
    out = struct((tokens, cached + steps, kv_heads, width), bf16)
    keys, values = call(functools.partial(resample_kernel, steps, early), (out, out), [SMEM] + [VMEM] * 6, "resample", 2.2)(
        counts, near, far, cache_keys, cache_values, new_keys, new_values
    )
    returned = [swap(others[(k // 2 - 1) * rows : k // 2 * rows], k) for k in range(2, count, 2)]
    keys, values, *returned = lax.optimization_barrier((keys, values, *returned))
    result = call(functools.partial(total_kernel, len(returned) + 2), struct((rows, main), bf16), [VMEM] * (len(returned) + 3), "total", 0.1)(
        residual, own_block, arrived[:rows], *returned
    )
    layer_out = call(unpack_kernel, struct((steps, tokens, 2 * columns), bf16), [VMEM] * 2, "unpack", 0.5)(result, sibling(result))
    return layer_out, keys.transpose(0, 2, 1, 3), values.transpose(0, 2, 1, 3)


def padded(cells, sides, width):
    for axis, dim in sides:
        count = lax.axis_size(axis)
        ends = count - 1
        head = lax.slice_in_dim(cells, 0, width, axis=dim)
        tail = lax.slice_in_dim(cells, cells.shape[dim] - width, cells.shape[dim], axis=dim)
        cells = jnp.concatenate(
            [
                lax.ppermute(tail, axis, [(i, (i + 1) % count) for i in range(ends)]),
                cells,
                lax.ppermute(head, axis, [((i + 1) % count, i) for i in range(ends)]),
            ],
            axis=dim,
        )
    return cells


def shards(
    hidden_in,
    queries,
    new_keys,
    new_values,
    cache_keys,
    cache_values,
    route_ids,
    route_weights,
    norm_gain,
    gate_weight,
    up_weight,
    down_weight,
    ancestor_counts,
):
    step_count, token_count, query_heads, head_width = queries.shape
    key_heads = cache_keys.shape[1]
    cached = cache_keys.shape[2]
    group_size = query_heads // key_heads
    cache_pair = jnp.stack([cache_keys, cache_values])
    fresh_pair = jnp.transpose(jnp.stack([new_keys, new_values]), (0, 2, 3, 1, 4))
    both_kv = jnp.concatenate([cache_pair, fresh_pair], axis=3)
    length = both_kv.shape[3]
    grouped = queries.reshape(step_count, token_count, key_heads, group_size, head_width)
    scores = jnp.einsum(
        "sphgd,phld->sphgl", grouped, both_kv[0], preferred_element_type=jnp.float32
    ) / math.sqrt(head_width)
    allowed = lax.broadcasted_iota(
        jnp.int32, (step_count, length), 1
    ) <= cached + lax.broadcasted_iota(jnp.int32, (step_count, length), 0)
    scores = jnp.where(allowed[:, None, None, None, :], scores, -1e30)
    exponent = jnp.exp(scores - jnp.max(scores, axis=-1, keepdims=True))
    attn_weights = (exponent / jnp.sum(exponent, axis=-1, keepdims=True)).astype(jnp.bfloat16)
    attended = jnp.einsum(
        "sphgl,phld->sphgd", attn_weights, both_kv[1], preferred_element_type=jnp.float32
    )
    attended = attended.astype(jnp.bfloat16).reshape(
        step_count, token_count, query_heads * head_width
    )
    attended = lax.all_gather(attended, "tensor", axis=2, tiled=True)
    expert_count = lax.axis_size("expert")
    group_count = lax.axis_size("group")
    tensor_count = lax.axis_size("tensor")
    tensor_index = lax.axis_index("tensor")
    expert_local = gate_weight.shape[0]
    experts_all = expert_local * expert_count
    chosen_count = route_ids.shape[2]
    model_width = hidden_in.shape[2]
    column_width = down_weight.shape[2]
    capacity = min(token_count, max(2, 2 * token_count * chosen_count // experts_all))
    pair_count = token_count * chosen_count
    expert_iota = jnp.arange(experts_all, dtype=jnp.int32)
    slot_iota = jnp.arange(capacity, dtype=jnp.int32)
    token_owner = (
        (jnp.arange(pair_count) // chosen_count)[:, None] == jnp.arange(token_count)[None, :]
    ).astype(jnp.float32)
    halves = []
    for step_index in range(step_count):
        residual = hidden_in[step_index].astype(jnp.float32) + attended[step_index].astype(
            jnp.float32
        )
        normed = (
            residual
            * lax.rsqrt(jnp.mean(residual * residual, axis=-1, keepdims=True) + epsilon)
            * norm_gain
        ).astype(jnp.bfloat16)
        chosen = route_ids[step_index].reshape(pair_count)
        route_share = route_weights[step_index] / jnp.sum(
            route_weights[step_index], axis=-1, keepdims=True
        )
        expert_hits = (chosen[:, None] == expert_iota[None, :]).astype(jnp.int32)
        position = jnp.sum((jnp.cumsum(expert_hits, axis=0) - expert_hits) * expert_hits, axis=1)
        slotted = (
            expert_hits[:, :, None]
            * (position[:, None, None] == slot_iota[None, None, :]).astype(jnp.int32)
        ).astype(jnp.float32)
        dispatch = jnp.einsum("rec,rt->ect", slotted, token_owner, precision=highest)
        dispatch = dispatch.reshape(expert_count, expert_local, capacity, token_count).astype(
            jnp.bfloat16
        )
        combine = jnp.einsum(
            "rec,rt,r->tec",
            slotted,
            token_owner,
            route_share.reshape(pair_count),
            precision=highest,
        )
        combine = combine.reshape(token_count, expert_count, expert_local, capacity)
        feature_blocks = normed.reshape(token_count, group_count, model_width // group_count)
        outgoing = jnp.einsum(
            "aict,tgd->agicd", dispatch, feature_blocks, preferred_element_type=jnp.float32
        ).astype(jnp.bfloat16)
        flattened = outgoing.reshape(
            expert_count * group_count, expert_local, capacity, model_width // group_count
        )
        received = lax.all_to_all(
            flattened, ("expert", "group"), split_axis=0, concat_axis=0, tiled=True
        )
        gate_part = jnp.einsum(
            "seki,eif->sekf", received, gate_weight, preferred_element_type=jnp.float32
        ).astype(jnp.bfloat16)
        up_part = jnp.einsum(
            "seki,eif->sekf", received, up_weight, preferred_element_type=jnp.float32
        ).astype(jnp.bfloat16)
        gate_sum = lax.psum(gate_part, "group").astype(jnp.float32)
        up_sum = lax.psum(up_part, "group").astype(jnp.float32)
        hidden = (jax.nn.silu(gate_sum) * up_sum).astype(jnp.bfloat16)
        hidden = lax.all_gather(hidden, "tensor", axis=3, tiled=True)
        answered = jnp.einsum(
            "sekf,efo->seko", hidden, down_weight, preferred_element_type=jnp.float32
        ).astype(jnp.bfloat16)
        returned = lax.all_to_all(
            answered, ("expert", "group"), split_axis=0, concat_axis=0, tiled=True
        )
        returned = returned.reshape(
            expert_count, group_count, expert_local, capacity, column_width
        ).astype(jnp.float32)
        expert_mix = jnp.einsum("taic,agicd->tgd", combine, returned, precision=highest)
        own_columns = lax.dynamic_index_in_dim(
            residual.reshape(token_count, group_count, tensor_count, column_width),
            tensor_index,
            2,
            keepdims=False,
        )
        halves.append((own_columns + expert_mix).astype(jnp.bfloat16))
    stacked = jnp.stack(halves)
    layer_out = lax.all_gather(stacked, "tensor", axis=3, tiled=True).reshape(
        step_count, token_count, model_width
    )
    every_count = lax.all_gather(ancestor_counts, ("expert", "group"), axis=0, tiled=True)
    running = jnp.cumsum(every_count)
    first_index = lax.axis_index(("expert", "group")) * token_count
    own_index = first_index + jnp.arange(token_count, dtype=jnp.int32)
    ancestor = jnp.sum((running[None, :] <= own_index[:, None]).astype(jnp.int32), axis=1)
    widened = padded(both_kv, ((("expert", "group"), 1),), REACH)
    window_index = first_index - REACH + jnp.arange(token_count + 2 * REACH, dtype=jnp.int32)
    selector = (ancestor[:, None] == window_index[None, :]).astype(jnp.bfloat16)
    resampled = jnp.einsum(
        "tw,kwhld->kthld", selector, widened, preferred_element_type=jnp.float32
    ).astype(jnp.bfloat16)
    return (layer_out, resampled[0], resampled[1])


def solution(mesh):
    count = mesh.shape["expert"]
    fast = mesh.shape["group"] == 1 and mesh.shape["tensor"] == 2 and count % 2 == 0 and count & (count - 1) == 0
    in_specs = (
        P(None, ("parts", "expert", "group"), None),
        P(None, ("parts", "expert", "group"), "tensor", None),
        P(None, ("parts", "expert", "group"), "tensor", None),
        P(None, ("parts", "expert", "group"), "tensor", None),
        P(("parts", "expert", "group"), "tensor", None, None),
        P(("parts", "expert", "group"), "tensor", None, None),
        P(None, ("parts", "expert", "group"), None),
        P(None, ("parts", "expert", "group"), None),
        P(),
        P("expert", "group", "tensor"),
        P("expert", "group", "tensor"),
        P("expert", None, ("group", "tensor")),
        P(("parts", "expert", "group")),
    )
    out_specs = (
        P(None, ("parts", "expert", "group"), None),
        P(("parts", "expert", "group"), "tensor", None, None),
        P(("parts", "expert", "group"), "tensor", None, None),
    )
    return jax.shard_map(fast_shards if fast else shards, mesh=mesh, in_specs=in_specs, out_specs=out_specs, check_vma=False)
```

```python
import functools
import math

import jax
import jax.numpy as jnp
from jax import lax
from jax.experimental import pallas as pl
from jax.experimental.pallas import tpu as pltpu
from jax.sharding import PartitionSpec as P

REACH = 2
LANES = 128
PAD = 8
f32, bf16 = jnp.float32, jnp.bfloat16

epsilon = 1e-06
highest = lax.Precision.HIGHEST


def dot(a, b, dims=((1,), (0,))):
    return lax.dot_general(a, b, (dims, ((), ())), preferred_element_type=f32)


def iota(shape, dim):
    return lax.broadcasted_iota(jnp.int32, shape, dim)


def packing(steps, tokens, heads):
    rows, per_part = (steps + 1) * tokens, heads // (steps + 1)
    tiles, count = steps * per_part, tokens * steps * heads
    target = iota((tiles * rows, count), 0)
    tile, inner = lax.div(target, rows), lax.rem(target, rows)
    is_extra = inner >= steps * tokens
    step = jnp.where(is_extra, lax.div(tile, per_part), lax.div(inner, tokens))
    token = lax.rem(inner, tokens)
    head = jnp.where(is_extra, tiles + lax.rem(tile, per_part), tile)
    chosen = (token * steps + step) * heads + head == iota((tiles * rows, count), 1)
    return chosen.astype(f32).astype(bf16)


def load_kernel(
    steps, ids_in, weights_in, counts_in, gain_in, hidden_in, q_in, nk_in, nv_in, ck_in, cv_in,
    ids_ref, weights_ref, counts_ref, gain_ref, hidden_ref, q_ref, nk_ref, nv_ref, ck_ref, cv_ref, chosen_ref, near_ref, far_ref, sems,
):
    pairs = (
        (ck_in, ck_ref), (cv_in, cv_ref), (nk_in, nk_ref), (nv_in, nv_ref), (q_in, q_ref), (hidden_in, hidden_ref),
        (gain_in, gain_ref), (ids_in, ids_ref), (weights_in, weights_ref), (counts_in, counts_ref),
    )
    copies = [pltpu.make_async_copy(source, target, sems.at[n]) for n, (source, target) in enumerate(pairs)]
    for copy in copies:
        copy.start()
    tokens, kv_heads, cached, width = ck_ref.shape
    chosen_ref[...] = packing(steps, tokens, q_ref.shape[2])
    for copy in copies:
        copy.wait()

    odd = lax.rem(lax.axis_index("expert"), 2)
    per = REACH * kv_heads

    early = near_ref.shape[0]

    def halo(start, kinds, slot):
        for cache_ref, new_ref in kinds:
            for r in range(REACH):
                for h in range(kv_heads):
                    out_ref, at = (near_ref, slot) if slot < early else (far_ref, slot - early)
                    out_ref[at, :cached, :] = cache_ref[start + r, h]
                    new = jnp.concatenate(
                        [new_ref[s, start + r, h : h + 1, :].astype(f32) for s in range(steps)]
                        + [jnp.zeros((PAD - steps, width), f32)], axis=0)
                    out_ref[at, cached:, :] = new.astype(bf16)
                    slot += 1

    keys, values = (ck_ref, nk_ref), (cv_ref, nv_ref)
    tail = tokens - REACH

    @pl.when(odd == 0)
    def _():
        halo(tail, (keys, values), 0)
        halo(0, (keys, values), 2 * per)

    @pl.when(odd == 1)
    def _():
        halo(0, (keys, values), 0)
        halo(tail, (keys, values), 2 * per)


def weight_kernel(after_ref, source, target, token_ref, sems):
    copies = []
    part = source.shape[1] // 2
    for e in range(source.shape[0]):
        for k in range(2):
            at = pl.ds(k * part, part)
            copies.append(pltpu.make_async_copy(source.at[e, at], target.at[e, at], sems.at[len(copies)]))
    for copy in copies:
        copy.start()
    for copy in copies:
        copy.wait()
    token_ref[...] = jnp.zeros_like(token_ref)


def attend_kernel(
    steps, experts, ids_ref, weights_ref, counts_ref, gain_ref, hidden_ref, q_ref, nk_ref, nv_ref, ck_ref, cv_ref, chosen_ref,
    send_ref, residual_ref, scores_ref,
):
    tokens, heads, width = q_ref.shape[1:]
    kv_heads, cached = ck_ref.shape[1:3]
    group = heads // kv_heads
    columns = heads * width
    part = columns // (steps + 1)
    main = steps * part
    rows = (steps + 1) * tokens
    base = lax.axis_index("tensor") * columns
    fresh = steps * kv_heads
    fresh_rows = -(-fresh // 16) * 16
    scale = 1.0 / math.sqrt(width)

    q_rows = steps * heads
    row = iota((q_rows, kv_heads * cached), 0)
    col = iota((q_rows, kv_heads * cached), 1)
    own_head = lax.div(lax.rem(row, heads), group) == lax.div(col, cached)
    row = iota((q_rows, fresh_rows), 0)
    col = iota((q_rows, fresh_rows), 1)
    own_new = (
        (lax.div(lax.rem(row, heads), group) == lax.rem(col, kv_heads))
        & (lax.div(col, kv_heads) <= lax.div(row, heads))
        & (col < fresh)
    )
    def with_new(new_ref, p):
        pieces = [new_ref[s, p].astype(f32) for s in range(steps)]
        return jnp.concatenate(pieces + [jnp.zeros((fresh_rows - fresh, width), f32)], axis=0).astype(bf16)

    every = range(tokens)
    q = [jnp.concatenate([q_ref[s, p] for s in range(steps)], axis=0) for p in every]
    old = [dot(q[p], ck_ref[p].reshape(kv_heads * cached, width), ((1,), (1,))) for p in every]
    new = [dot(q[p], with_new(nk_ref, p), ((1,), (1,))) for p in every]
    old = [jnp.where(own_head, x * scale, -1e30) for x in old]
    new = [jnp.where(own_new, x * scale, -1e30) for x in new]
    top = [jnp.maximum(jnp.max(old[p], axis=1, keepdims=True), jnp.max(new[p], axis=1, keepdims=True)) for p in every]
    old = [jnp.exp(old[p] - top[p]) for p in every]
    new = [jnp.exp(new[p] - top[p]) for p in every]
    inverse = [1.0 / (jnp.sum(old[p], axis=1, keepdims=True) + jnp.sum(new[p], axis=1, keepdims=True)) for p in every]
    old = [(old[p] * inverse[p]).astype(bf16) for p in every]
    new = [(new[p] * inverse[p]).astype(bf16) for p in every]
    attended = jnp.concatenate([
        (dot(old[p], cv_ref[p].reshape(kv_heads * cached, width)) + dot(new[p], with_new(nv_ref, p))).astype(bf16) for p in every
    ], axis=0)

    tiles = main // width
    moved = dot(chosen_ref[...], attended)
    for s in range(steps):
        residual_ref[s * tokens : (s + 1) * tokens, :] = hidden_ref[s, :, pl.ds(pl.multiple_of(base, LANES), main)].astype(f32)
        residual_ref[steps * tokens :, s * part : (s + 1) * part] = hidden_ref[
            s, :, pl.ds(pl.multiple_of(base + main, LANES), part)
        ].astype(f32)
    residual = residual_ref[...] + jnp.concatenate([moved[j * rows : (j + 1) * rows] for j in range(tiles)], axis=1)
    residual_ref[...] = residual
    gain_main = gain_ref[:, pl.ds(pl.multiple_of(base, LANES), main)]
    gain_last = gain_ref[:, pl.ds(pl.multiple_of(base + main, LANES), part)]
    in_main = iota((rows, main), 0) < steps * tokens
    gain = jnp.where(in_main, gain_main, jnp.concatenate([gain_last] * steps, axis=1))
    send_ref[:, :main] = (residual * gain).astype(bf16)

    squares = residual * residual
    lane = iota((tokens, LANES), 1)
    for s in range(steps):
        scores_ref[s * rows : (s + 1) * rows, :] = jnp.broadcast_to(
            jnp.sum(squares[:, s * part : (s + 1) * part], axis=1, keepdims=True), (rows, LANES))
    whole = sum(scores_ref[s * rows : (s + 1) * rows, :] for s in range(steps))
    scores_ref[steps * rows :, :] = whole
    pieces = []
    for s in range(steps):
        square_sum = (
            scores_ref[steps * rows + s * tokens : steps * rows + (s + 1) * tokens, :]
            + scores_ref[s * rows + steps * tokens : (s + 1) * rows, :]
        )
        ids, weights = ids_ref[s], weights_ref[s]
        share = weights / jnp.sum(weights, axis=1, keepdims=True)
        value = jnp.zeros((tokens, LANES), f32)
        expert = jnp.where(lane < experts, lane, lane - experts)
        for k in range(ids.shape[1]):
            value = jnp.where(ids[:, k : k + 1] == expert, share[:, k : k + 1], value)
        value = jnp.where(lane < 2 * experts, value, square_sum)
        high = value.astype(bf16).astype(f32)
        low = value - high
        piece = jnp.where((lane < experts) | (lane == 2 * experts), high, low)
        piece = jnp.where(lane < 2 * experts + 2, piece, 0.0)
        if s == 0:
            for p in range(tokens):
                here = (lane == 2 * experts + 2) & (iota((tokens, LANES), 0) == p)
                piece = jnp.where(here, counts_ref[p].astype(f32), piece)
        pieces.append(piece)
    pieces.append(jnp.zeros((tokens, LANES), f32))
    send_ref[:, main:] = jnp.concatenate(pieces, axis=0).astype(bf16)


def unpacking(blocks, steps, tokens, s, back):
    rows = (steps + 1) * tokens
    target, source = iota((blocks * rows, blocks * rows), 0), iota((blocks * rows, blocks * rows), 1)
    if back:
        target, source = source, target
    hit = (target + (steps - s) * tokens == source) & (lax.div(lax.rem(target, rows), tokens) == s)
    return hit.astype(f32).astype(bf16)


def halves(even_ref, odd_ref, at):
    return jnp.concatenate([even_ref[:, at], odd_ref[:, at]], axis=0)


def expert_products(steps, tokens, features, gate_ref, up_ref, half):
    total, main = features.shape
    rows = (steps + 1) * tokens
    part = main // steps
    columns = main + part
    local = gate_ref.shape[0]
    blocks = total // rows
    extra = sum(
        dot(unpacking(blocks, steps, tokens, s, False), features[:, s * part : (s + 1) * part]) for s in range(steps)
    ).astype(bf16)
    first = pl.ds(pl.multiple_of(half * columns, LANES), main)
    last = pl.ds(pl.multiple_of(half * columns + main, LANES), part)
    return [
        dot(features, ref[e, first, :]) + dot(extra, ref[e, last, :]) for ref in (gate_ref, up_ref) for e in range(local)
    ]


def partial_kernel(steps, tokens, after_ref, also_after_ref, even_ref, odd_ref, gate_ref, up_ref, out_ref):
    main = even_ref.shape[1] - LANES
    products = expert_products(steps, tokens, halves(even_ref, odd_ref, slice(0, main)), gate_ref, up_ref, lax.axis_index("tensor"))
    for n, product in enumerate(products):
        out_ref[n] = product


def hidden_kernel(steps, tokens, experts, partial_ref, even_ref, odd_ref, even_other_ref, odd_other_ref, gate_ref, up_ref, out_ref):
    main = even_ref.shape[1] - LANES
    total = 2 * even_ref.shape[0]
    rows = (steps + 1) * tokens
    columns = main + main // steps
    local, _, units = gate_ref.shape
    features = halves(even_other_ref, odd_other_ref, slice(0, main))
    products = expert_products(steps, tokens, features, gate_ref, up_ref, 1 - lax.axis_index("tensor"))
    meta = halves(even_ref, odd_ref, slice(main, None)).astype(f32)
    meta_other = halves(even_other_ref, odd_other_ref, slice(main, None)).astype(f32)
    lane = iota(meta.shape, 1)
    valid = lax.rem(iota((total, 1), 0), rows) < steps * tokens
    in_squares = (lane == 2 * experts) | (lane == 2 * experts + 1)
    square_sum = jnp.sum(jnp.where(in_squares, meta + meta_other, 0.0), axis=1, keepdims=True)
    factor = jnp.where(valid, lax.rsqrt(square_sum / (2 * columns) + epsilon), 0.0)
    first_expert = lax.axis_index("expert") * local
    for e in range(local):
        at = first_expert + e
        share = jnp.sum(jnp.where((lane == at) | (lane == at + experts), meta, 0.0), axis=1, keepdims=True)
        gate = ((partial_ref[e] + products[e]) * factor).astype(bf16).astype(f32)
        up = ((partial_ref[local + e] + products[local + e]) * factor).astype(bf16).astype(f32)
        hidden = gate / (1.0 + jnp.exp(-gate)) * up * share
        out_ref[:, e * units : (e + 1) * units] = hidden.astype(bf16)


def down_kernel(steps, tokens, own_ref, other_ref, down_ref, kept_ref, leaving_ref):
    total, width = own_ref.shape
    local, _, columns = down_ref.shape
    units = width // local
    rows = (steps + 1) * tokens
    part = columns // (steps + 1)
    main = steps * part
    mine = lax.axis_index("tensor")
    product = 0.0
    for ref, half in ((own_ref, mine), (other_ref, 1 - mine)):
        start = pl.multiple_of(half * units, LANES)
        for e in range(local):
            product += dot(ref[:, e * units : (e + 1) * units], down_ref[e, pl.ds(start, units), :])
    last = product[:, main:].astype(bf16)
    extra = jnp.concatenate([dot(unpacking(total // rows, steps, tokens, s, True), last) for s in range(steps)], axis=1)
    in_main = lax.rem(iota((total, main), 0), rows) < steps * tokens
    product = jnp.where(in_main, product[:, :main], extra)
    kept_ref[...] = product[: total // 2]
    leaving_ref[...] = product[total // 2 :].astype(bf16)


def resample_kernel(steps, early, counts_ref, near_ref, relay_ref, ck_ref, cv_ref, nk_ref, nv_ref, keys_ref, values_ref):
    tokens, kv_heads, cached, width = ck_ref.shape
    devices = counts_ref.shape[0]
    me = lax.axis_index("expert")
    first = me * tokens
    odd = lax.rem(me, 2)
    per = REACH * kv_heads
    running = jnp.int32(0)
    ancestors = [jnp.int32(0)] * tokens
    for d in range(devices):
        k = jnp.bitwise_xor(me, d)
        for p in range(tokens):
            running = running + counts_ref[k, p]
            for i in range(tokens):
                ancestors[i] = ancestors[i] + (running <= first + i).astype(jnp.int32)

    for i in range(tokens):
        offset = ancestors[i] - first

        @pl.when((offset >= 0) & (offset < tokens))
        def _():
            for out_ref, cache_ref, new_ref in ((keys_ref, ck_ref, nk_ref), (values_ref, cv_ref, nv_ref)):
                out_ref[i, :cached] = jnp.swapaxes(cache_ref[offset], 0, 1)
                for s in range(steps):
                    out_ref[i, cached + s] = new_ref[s, offset]

        def from_halo(ref, at):
            for kind, out_ref in enumerate((keys_ref, values_ref)):
                slots = ref[pl.ds(kind * per + at * kv_heads, kv_heads)]
                out_ref[i] = jnp.swapaxes(slots[:, : cached + steps], 0, 1)

        left = offset < 0
        near = (left & (odd == 1)) | ((offset >= tokens) & (odd == 0))
        far = (left & (odd == 0)) | ((offset >= tokens) & (odd == 1))
        at = jnp.where(left, offset + REACH, offset - tokens)

        @pl.when(near)
        def _():
            from_halo(near_ref, at)

        @pl.when(far)
        def _():
            from_halo(relay_ref, at)


def add_kernel(a_ref, b_ref, out_ref):
    out_ref[...] = (a_ref[...] + b_ref[...].astype(f32)).astype(out_ref.dtype)


def total_kernel(count, *refs):
    out_ref = refs[-1]
    value = refs[0][...]
    for ref in refs[1 : count + 1]:
        value = value + ref[...].astype(f32)
    out_ref[...] = value.astype(out_ref.dtype)


def unpack_kernel(own_ref, other_ref, out_ref):
    steps, tokens, model_width = out_ref.shape
    columns = model_width // 2
    main = own_ref.shape[1]
    part = main // steps
    mine = lax.axis_index("tensor")
    for ref, half in ((own_ref, mine), (other_ref, 1 - mine)):
        block = ref[...].astype(f32)
        first = pl.multiple_of(half * columns, LANES)
        last = pl.multiple_of(half * columns + main, LANES)
        for s in range(steps):
            out_ref[s, :, pl.ds(first, main)] = block[s * tokens : (s + 1) * tokens].astype(bf16)
            out_ref[s, :, pl.ds(last, part)] = block[steps * tokens :, s * part : (s + 1) * part].astype(bf16)


VMEM = pl.BlockSpec(memory_space=pltpu.VMEM)
SMEM = pl.BlockSpec(memory_space=pltpu.SMEM)
HBM = pl.BlockSpec(memory_space=pltpu.HBM)


def call(kernel, out, specs, name, microseconds, scratch=(), limit=20):
    outs = jax.tree.map(lambda _: VMEM, out)
    return pl.pallas_call(
        kernel, out_shape=out, in_specs=specs, out_specs=outs, scratch_shapes=scratch, name=name,
        cost_estimate=pl.CostEstimate(flops=0, bytes_accessed=int(microseconds * 3.5e6), transcendentals=0),
        compiler_params=pltpu.CompilerParams(vmem_limit_bytes=limit << 20),
    )


def struct(shape, dtype):
    return jax.ShapeDtypeStruct(shape, dtype)


def in_hbm(value):
    return pltpu.with_memory_space_constraint(value, pltpu.HBM)


def fast_shards(
    hidden_in, queries, new_keys, new_values, cache_keys, cache_values, route_ids, route_weights, norm_gain,
    gate_weight, up_weight, down_weight, ancestor_counts,
):
    steps, tokens, heads, width = queries.shape
    kv_heads, cached = cache_keys.shape[1:3]
    count = lax.axis_size("expert")
    local, _, units = gate_weight.shape
    experts = local * count
    columns = down_weight.shape[2]
    part = columns // (steps + 1)
    main = steps * part
    rows = (steps + 1) * tokens
    per = REACH * kv_heads
    early = 2 * per + per // 2
    square = steps * tokens * heads
    chosen = pltpu.VMEM((square, square), bf16)
    halos = [pltpu.VMEM((slots, cached + PAD, width), bf16) for slots in (early, 4 * per - early)]

    def swap(value, offset):
        return lax.ppermute(value, "expert", [(i, i ^ offset) for i in range(count)])

    def sibling(value):
        return lax.ppermute(value, "tensor", [(0, 1), (1, 0)])

    inputs = (route_ids, route_weights, ancestor_counts, norm_gain.reshape(1, -1), hidden_in, queries, new_keys, new_values, cache_keys, cache_values)
    spaces = [pltpu.SMEM if value is ancestor_counts else pltpu.VMEM for value in inputs]
    loaded = pl.pallas_call(
        functools.partial(load_kernel, steps),
        out_shape=[space(value.shape, value.dtype) for space, value in zip(spaces, inputs)] + [chosen] + halos,
        in_specs=[HBM] * len(inputs), out_specs=[pl.BlockSpec(memory_space=space) for space in spaces] + [VMEM] * 3,
        scratch_shapes=[pltpu.SemaphoreType.DMA((len(inputs),))], name="load",
        compiler_params=pltpu.CompilerParams(vmem_limit_bytes=20 << 20),
    )(*(in_hbm(value) for value in inputs))
    *loaded, near, far = loaded
    near = swap(near, 1)
    new_keys, new_values, cache_keys, cache_values = loaded[6:10]
    send, residual = call(
        functools.partial(attend_kernel, steps, experts),
        (struct((rows, main + LANES), bf16), struct((rows, main), f32)),
        [VMEM, VMEM, SMEM] + [VMEM] * 8, "attend", 2.3, [pltpu.VMEM(((steps + 1) * rows, LANES), f32)],
    )(*loaded)

    far_first = range(count - 2, 0, -2)
    def fetch(after, weight, name):
        return pl.pallas_call(
            weight_kernel, out_shape=[pltpu.VMEM(weight.shape, weight.dtype), pltpu.VMEM((8, LANES), f32)],
            in_specs=[VMEM, HBM], out_specs=[VMEM] * 2, scratch_shapes=[pltpu.SemaphoreType.DMA((2 * local,))], name=name,
            cost_estimate=pl.CostEstimate(flops=0, bytes_accessed=7_000_000, transcendentals=0),
            compiler_params=pltpu.CompilerParams(vmem_limit_bytes=16 << 20),
        )(after, in_hbm(weight))

    gate, token = fetch(residual, gate_weight, "gate")
    even = jnp.concatenate([send] + [swap(send, k) for k in far_first], axis=0)
    even, near, token = lax.optimization_barrier((even, near, token))
    odd = swap(even, 1)
    even_other = sibling(even)
    up, token_up = fetch(even, up_weight, "up")
    odd, token_up, far = lax.optimization_barrier((odd, token_up, far))
    relayed = swap(far, 1)
    odd_other = sibling(odd)
    partial = call(
        functools.partial(partial_kernel, steps, tokens), struct((2 * local, count * rows, units), f32), [VMEM] * 6, "partial", 0.01,
    )(token, token_up, even, odd, gate, up)
    hidden = call(
        functools.partial(hidden_kernel, steps, tokens, experts),
        struct((count * rows, local * units), bf16), [VMEM] * 7, "hidden", 0.01,
    )(partial, even, odd, even_other, odd_other, gate, up)
    other_hidden = sibling(hidden)
    half = count // 2 * rows

    kept, leaving = call(
        functools.partial(down_kernel, steps, tokens), (struct((half, main), f32), struct((half, main), bf16)), [VMEM] * 3, "down", 0.01,
    )(hidden, other_hidden, down_weight)
    leaving, relayed = lax.optimization_barrier((leaving, relayed))
    arrived = swap(leaving, 1)
    ring = [(i, i + 2 if i % 2 == 0 else i - 2) for i in range(count) if (i < count - 2 if i % 2 == 0 else i > 1)]
    far = lax.ppermute(jnp.concatenate([near[2 * per :], relayed], axis=0), "expert", ring)
    own_block, others = kept[:rows], call(add_kernel, struct((half - rows, main), bf16), [VMEM] * 2, "add", 0.1)(kept[rows:], arrived[rows:])

    counts = [block.reshape(count // 2, rows, main + LANES)[:, :tokens, main + 2 * experts + 2].astype(jnp.int32) for block in (even, odd)]
    place = [0, *far_first]
    counts = jnp.stack([counts[k % 2][place.index(k - k % 2)] for k in range(count)])
    out = struct((tokens, cached + steps, kv_heads, width), bf16)
    keys, values = call(functools.partial(resample_kernel, steps, early), (out, out), [SMEM] + [VMEM] * 6, "resample", 2.2)(
        counts, near, far, cache_keys, cache_values, new_keys, new_values
    )
    returned = [swap(others[n * rows : (n + 1) * rows], k) for n, k in enumerate(far_first)]
    keys, values, *returned = lax.optimization_barrier((keys, values, *returned))
    result = call(functools.partial(total_kernel, len(returned) + 2), struct((rows, main), bf16), [VMEM] * (len(returned) + 3), "total", 0.1)(
        residual, own_block, arrived[:rows], *returned
    )
    layer_out = call(unpack_kernel, struct((steps, tokens, 2 * columns), bf16), [VMEM] * 2, "unpack", 0.5)(result, sibling(result))
    return layer_out, keys.transpose(0, 2, 1, 3), values.transpose(0, 2, 1, 3)


def padded(cells, sides, width):
    for axis, dim in sides:
        count = lax.axis_size(axis)
        ends = count - 1
        head = lax.slice_in_dim(cells, 0, width, axis=dim)
        tail = lax.slice_in_dim(cells, cells.shape[dim] - width, cells.shape[dim], axis=dim)
        cells = jnp.concatenate(
            [
                lax.ppermute(tail, axis, [(i, (i + 1) % count) for i in range(ends)]),
                cells,
                lax.ppermute(head, axis, [((i + 1) % count, i) for i in range(ends)]),
            ],
            axis=dim,
        )
    return cells


def shards(
    hidden_in,
    queries,
    new_keys,
    new_values,
    cache_keys,
    cache_values,
    route_ids,
    route_weights,
    norm_gain,
    gate_weight,
    up_weight,
    down_weight,
    ancestor_counts,
):
    step_count, token_count, query_heads, head_width = queries.shape
    key_heads = cache_keys.shape[1]
    cached = cache_keys.shape[2]
    group_size = query_heads // key_heads
    cache_pair = jnp.stack([cache_keys, cache_values])
    fresh_pair = jnp.transpose(jnp.stack([new_keys, new_values]), (0, 2, 3, 1, 4))
    both_kv = jnp.concatenate([cache_pair, fresh_pair], axis=3)
    length = both_kv.shape[3]
    grouped = queries.reshape(step_count, token_count, key_heads, group_size, head_width)
    scores = jnp.einsum(
        "sphgd,phld->sphgl", grouped, both_kv[0], preferred_element_type=jnp.float32
    ) / math.sqrt(head_width)
    allowed = lax.broadcasted_iota(
        jnp.int32, (step_count, length), 1
    ) <= cached + lax.broadcasted_iota(jnp.int32, (step_count, length), 0)
    scores = jnp.where(allowed[:, None, None, None, :], scores, -1e30)
    exponent = jnp.exp(scores - jnp.max(scores, axis=-1, keepdims=True))
    attn_weights = (exponent / jnp.sum(exponent, axis=-1, keepdims=True)).astype(jnp.bfloat16)
    attended = jnp.einsum(
        "sphgl,phld->sphgd", attn_weights, both_kv[1], preferred_element_type=jnp.float32
    )
    attended = attended.astype(jnp.bfloat16).reshape(
        step_count, token_count, query_heads * head_width
    )
    attended = lax.all_gather(attended, "tensor", axis=2, tiled=True)
    expert_count = lax.axis_size("expert")
    group_count = lax.axis_size("group")
    tensor_count = lax.axis_size("tensor")
    tensor_index = lax.axis_index("tensor")
    expert_local = gate_weight.shape[0]
    experts_all = expert_local * expert_count
    chosen_count = route_ids.shape[2]
    model_width = hidden_in.shape[2]
    column_width = down_weight.shape[2]
    capacity = min(token_count, max(2, 2 * token_count * chosen_count // experts_all))
    pair_count = token_count * chosen_count
    expert_iota = jnp.arange(experts_all, dtype=jnp.int32)
    slot_iota = jnp.arange(capacity, dtype=jnp.int32)
    token_owner = (
        (jnp.arange(pair_count) // chosen_count)[:, None] == jnp.arange(token_count)[None, :]
    ).astype(jnp.float32)
    halves = []
    for step_index in range(step_count):
        residual = hidden_in[step_index].astype(jnp.float32) + attended[step_index].astype(
            jnp.float32
        )
        normed = (
            residual
            * lax.rsqrt(jnp.mean(residual * residual, axis=-1, keepdims=True) + epsilon)
            * norm_gain
        ).astype(jnp.bfloat16)
        chosen = route_ids[step_index].reshape(pair_count)
        route_share = route_weights[step_index] / jnp.sum(
            route_weights[step_index], axis=-1, keepdims=True
        )
        expert_hits = (chosen[:, None] == expert_iota[None, :]).astype(jnp.int32)
        position = jnp.sum((jnp.cumsum(expert_hits, axis=0) - expert_hits) * expert_hits, axis=1)
        slotted = (
            expert_hits[:, :, None]
            * (position[:, None, None] == slot_iota[None, None, :]).astype(jnp.int32)
        ).astype(jnp.float32)
        dispatch = jnp.einsum("rec,rt->ect", slotted, token_owner, precision=highest)
        dispatch = dispatch.reshape(expert_count, expert_local, capacity, token_count).astype(
            jnp.bfloat16
        )
        combine = jnp.einsum(
            "rec,rt,r->tec",
            slotted,
            token_owner,
            route_share.reshape(pair_count),
            precision=highest,
        )
        combine = combine.reshape(token_count, expert_count, expert_local, capacity)
        feature_blocks = normed.reshape(token_count, group_count, model_width // group_count)
        outgoing = jnp.einsum(
            "aict,tgd->agicd", dispatch, feature_blocks, preferred_element_type=jnp.float32
        ).astype(jnp.bfloat16)
        flattened = outgoing.reshape(
            expert_count * group_count, expert_local, capacity, model_width // group_count
        )
        received = lax.all_to_all(
            flattened, ("expert", "group"), split_axis=0, concat_axis=0, tiled=True
        )
        gate_part = jnp.einsum(
            "seki,eif->sekf", received, gate_weight, preferred_element_type=jnp.float32
        ).astype(jnp.bfloat16)
        up_part = jnp.einsum(
            "seki,eif->sekf", received, up_weight, preferred_element_type=jnp.float32
        ).astype(jnp.bfloat16)
        gate_sum = lax.psum(gate_part, "group").astype(jnp.float32)
        up_sum = lax.psum(up_part, "group").astype(jnp.float32)
        hidden = (jax.nn.silu(gate_sum) * up_sum).astype(jnp.bfloat16)
        hidden = lax.all_gather(hidden, "tensor", axis=3, tiled=True)
        answered = jnp.einsum(
            "sekf,efo->seko", hidden, down_weight, preferred_element_type=jnp.float32
        ).astype(jnp.bfloat16)
        returned = lax.all_to_all(
            answered, ("expert", "group"), split_axis=0, concat_axis=0, tiled=True
        )
        returned = returned.reshape(
            expert_count, group_count, expert_local, capacity, column_width
        ).astype(jnp.float32)
        expert_mix = jnp.einsum("taic,agicd->tgd", combine, returned, precision=highest)
        own_columns = lax.dynamic_index_in_dim(
            residual.reshape(token_count, group_count, tensor_count, column_width),
            tensor_index,
            2,
            keepdims=False,
        )
        halves.append((own_columns + expert_mix).astype(jnp.bfloat16))
    stacked = jnp.stack(halves)
    layer_out = lax.all_gather(stacked, "tensor", axis=3, tiled=True).reshape(
        step_count, token_count, model_width
    )
    every_count = lax.all_gather(ancestor_counts, ("expert", "group"), axis=0, tiled=True)
    running = jnp.cumsum(every_count)
    first_index = lax.axis_index(("expert", "group")) * token_count
    own_index = first_index + jnp.arange(token_count, dtype=jnp.int32)
    ancestor = jnp.sum((running[None, :] <= own_index[:, None]).astype(jnp.int32), axis=1)
    widened = padded(both_kv, ((("expert", "group"), 1),), REACH)
    window_index = first_index - REACH + jnp.arange(token_count + 2 * REACH, dtype=jnp.int32)
    selector = (ancestor[:, None] == window_index[None, :]).astype(jnp.bfloat16)
    resampled = jnp.einsum(
        "tw,kwhld->kthld", selector, widened, preferred_element_type=jnp.float32
    ).astype(jnp.bfloat16)
    return (layer_out, resampled[0], resampled[1])


def solution(mesh):
    count = mesh.shape["expert"]
    fast = mesh.shape["group"] == 1 and mesh.shape["tensor"] == 2 and count % 2 == 0 and count & (count - 1) == 0
    in_specs = (
        P(None, ("parts", "expert", "group"), None),
        P(None, ("parts", "expert", "group"), "tensor", None),
        P(None, ("parts", "expert", "group"), "tensor", None),
        P(None, ("parts", "expert", "group"), "tensor", None),
        P(("parts", "expert", "group"), "tensor", None, None),
        P(("parts", "expert", "group"), "tensor", None, None),
        P(None, ("parts", "expert", "group"), None),
        P(None, ("parts", "expert", "group"), None),
        P(),
        P("expert", "group", "tensor"),
        P("expert", "group", "tensor"),
        P("expert", None, ("group", "tensor")),
        P(("parts", "expert", "group")),
    )
    out_specs = (
        P(None, ("parts", "expert", "group"), None),
        P(("parts", "expert", "group"), "tensor", None, None),
        P(("parts", "expert", "group"), "tensor", None, None),
    )
    return jax.shard_map(fast_shards if fast else shards, mesh=mesh, in_specs=in_specs, out_specs=out_specs, check_vma=False)
```

```python
import functools
import math

import jax
import jax.numpy as jnp
from jax import lax
from jax.experimental import pallas as pl
from jax.experimental.pallas import tpu as pltpu
from jax.sharding import PartitionSpec as P

REACH = 2
LANES = 128
PAD = 8
f32, bf16 = jnp.float32, jnp.bfloat16

epsilon = 1e-06
highest = lax.Precision.HIGHEST


def dot(a, b, dims=((1,), (0,))):
    return lax.dot_general(a, b, (dims, ((), ())), preferred_element_type=f32)


def iota(shape, dim):
    return lax.broadcasted_iota(jnp.int32, shape, dim)


def packing(steps, tokens, heads):
    rows, per_part = (steps + 1) * tokens, heads // (steps + 1)
    tiles, count = steps * per_part, tokens * steps * heads
    target = iota((tiles * rows, count), 0)
    tile, inner = lax.div(target, rows), lax.rem(target, rows)
    is_extra = inner >= steps * tokens
    step = jnp.where(is_extra, lax.div(tile, per_part), lax.div(inner, tokens))
    token = lax.rem(inner, tokens)
    head = jnp.where(is_extra, tiles + lax.rem(tile, per_part), tile)
    chosen = (token * steps + step) * heads + head == iota((tiles * rows, count), 1)
    return chosen.astype(f32).astype(bf16)


def load_kernel(
    steps, ids_in, weights_in, counts_in, gain_in, hidden_in, q_in, nk_in, nv_in, ck_in, cv_in,
    ids_ref, weights_ref, counts_ref, gain_ref, hidden_ref, q_ref, nk_ref, nv_ref, ck_ref, cv_ref, chosen_ref, near_ref, far_ref, sems,
):
    pairs = (
        (ck_in, ck_ref), (cv_in, cv_ref), (nk_in, nk_ref), (nv_in, nv_ref), (q_in, q_ref), (hidden_in, hidden_ref),
        (gain_in, gain_ref), (ids_in, ids_ref), (weights_in, weights_ref), (counts_in, counts_ref),
    )
    copies = [pltpu.make_async_copy(source, target, sems.at[n]) for n, (source, target) in enumerate(pairs)]
    for copy in copies:
        copy.start()
    tokens, kv_heads, cached, width = ck_ref.shape
    chosen_ref[...] = packing(steps, tokens, q_ref.shape[2])
    for copy in copies:
        copy.wait()

    odd = lax.rem(lax.axis_index("expert"), 2)
    per = REACH * kv_heads

    early = near_ref.shape[0]

    def halo(start, kinds, slot):
        for cache_ref, new_ref in kinds:
            for r in range(REACH):
                for h in range(kv_heads):
                    out_ref, at = (near_ref, slot) if slot < early else (far_ref, slot - early)
                    out_ref[at, :cached, :] = cache_ref[start + r, h]
                    new = jnp.concatenate(
                        [new_ref[s, start + r, h : h + 1, :].astype(f32) for s in range(steps)]
                        + [jnp.zeros((PAD - steps, width), f32)], axis=0)
                    out_ref[at, cached:, :] = new.astype(bf16)
                    slot += 1

    keys, values = (ck_ref, nk_ref), (cv_ref, nv_ref)
    tail = tokens - REACH

    @pl.when(odd == 0)
    def _():
        halo(tail, (keys, values), 0)
        halo(0, (keys, values), 2 * per)

    @pl.when(odd == 1)
    def _():
        halo(0, (keys, values), 0)
        halo(tail, (keys, values), 2 * per)


def weight_kernel(after_ref, source, target, token_ref, sems):
    copies = []
    part = source.shape[1] // 2
    for e in range(source.shape[0]):
        for k in range(2):
            at = pl.ds(k * part, part)
            copies.append(pltpu.make_async_copy(source.at[e, at], target.at[e, at], sems.at[len(copies)]))
    for copy in copies:
        copy.start()
    for copy in copies:
        copy.wait()
    token_ref[...] = jnp.zeros_like(token_ref)


def attend_kernel(
    steps, experts, ids_ref, weights_ref, counts_ref, gain_ref, hidden_ref, q_ref, nk_ref, nv_ref, ck_ref, cv_ref, chosen_ref,
    send_ref, residual_ref, scores_ref,
):
    tokens, heads, width = q_ref.shape[1:]
    kv_heads, cached = ck_ref.shape[1:3]
    group = heads // kv_heads
    columns = heads * width
    part = columns // (steps + 1)
    main = steps * part
    rows = (steps + 1) * tokens
    base = lax.axis_index("tensor") * columns
    fresh = steps * kv_heads
    fresh_rows = -(-fresh // 16) * 16
    scale = 1.0 / math.sqrt(width)

    q_rows = steps * heads
    row = iota((q_rows, kv_heads * cached), 0)
    col = iota((q_rows, kv_heads * cached), 1)
    own_head = lax.div(lax.rem(row, heads), group) == lax.div(col, cached)
    row = iota((q_rows, fresh_rows), 0)
    col = iota((q_rows, fresh_rows), 1)
    own_new = (
        (lax.div(lax.rem(row, heads), group) == lax.rem(col, kv_heads))
        & (lax.div(col, kv_heads) <= lax.div(row, heads))
        & (col < fresh)
    )
    def with_new(new_ref, p):
        pieces = [new_ref[s, p].astype(f32) for s in range(steps)]
        return jnp.concatenate(pieces + [jnp.zeros((fresh_rows - fresh, width), f32)], axis=0).astype(bf16)

    every = range(tokens)
    q = [jnp.concatenate([q_ref[s, p] for s in range(steps)], axis=0) for p in every]
    old = [dot(q[p], ck_ref[p].reshape(kv_heads * cached, width), ((1,), (1,))) for p in every]
    new = [dot(q[p], with_new(nk_ref, p), ((1,), (1,))) for p in every]
    old = [jnp.where(own_head, x * scale, -1e30) for x in old]
    new = [jnp.where(own_new, x * scale, -1e30) for x in new]
    top = [jnp.maximum(jnp.max(old[p], axis=1, keepdims=True), jnp.max(new[p], axis=1, keepdims=True)) for p in every]
    old = [jnp.exp(old[p] - top[p]) for p in every]
    new = [jnp.exp(new[p] - top[p]) for p in every]
    inverse = [1.0 / (jnp.sum(old[p], axis=1, keepdims=True) + jnp.sum(new[p], axis=1, keepdims=True)) for p in every]
    old = [(old[p] * inverse[p]).astype(bf16) for p in every]
    new = [(new[p] * inverse[p]).astype(bf16) for p in every]
    attended = jnp.concatenate([
        (dot(old[p], cv_ref[p].reshape(kv_heads * cached, width)) + dot(new[p], with_new(nv_ref, p))).astype(bf16) for p in every
    ], axis=0)

    tiles = main // width
    moved = dot(chosen_ref[...], attended)
    for s in range(steps):
        residual_ref[s * tokens : (s + 1) * tokens, :] = hidden_ref[s, :, pl.ds(pl.multiple_of(base, LANES), main)].astype(f32)
        residual_ref[steps * tokens :, s * part : (s + 1) * part] = hidden_ref[
            s, :, pl.ds(pl.multiple_of(base + main, LANES), part)
        ].astype(f32)
    residual = residual_ref[...] + jnp.concatenate([moved[j * rows : (j + 1) * rows] for j in range(tiles)], axis=1)
    residual_ref[...] = residual
    gain_main = gain_ref[:, pl.ds(pl.multiple_of(base, LANES), main)]
    gain_last = gain_ref[:, pl.ds(pl.multiple_of(base + main, LANES), part)]
    in_main = iota((rows, main), 0) < steps * tokens
    gain = jnp.where(in_main, gain_main, jnp.concatenate([gain_last] * steps, axis=1))
    send_ref[:, :main] = (residual * gain).astype(bf16)

    squares = residual * residual
    lane = iota((tokens, LANES), 1)
    for s in range(steps):
        scores_ref[s * rows : (s + 1) * rows, :] = jnp.broadcast_to(
            jnp.sum(squares[:, s * part : (s + 1) * part], axis=1, keepdims=True), (rows, LANES))
    whole = sum(scores_ref[s * rows : (s + 1) * rows, :] for s in range(steps))
    scores_ref[steps * rows :, :] = whole
    pieces = []
    for s in range(steps):
        square_sum = (
            scores_ref[steps * rows + s * tokens : steps * rows + (s + 1) * tokens, :]
            + scores_ref[s * rows + steps * tokens : (s + 1) * rows, :]
        )
        ids, weights = ids_ref[s], weights_ref[s]
        share = weights / jnp.sum(weights, axis=1, keepdims=True)
        value = jnp.zeros((tokens, LANES), f32)
        expert = jnp.where(lane < experts, lane, lane - experts)
        for k in range(ids.shape[1]):
            value = jnp.where(ids[:, k : k + 1] == expert, share[:, k : k + 1], value)
        value = jnp.where(lane < 2 * experts, value, square_sum)
        high = value.astype(bf16).astype(f32)
        low = value - high
        piece = jnp.where((lane < experts) | (lane == 2 * experts), high, low)
        piece = jnp.where(lane < 2 * experts + 2, piece, 0.0)
        if s == 0:
            for p in range(tokens):
                here = (lane == 2 * experts + 2) & (iota((tokens, LANES), 0) == p)
                piece = jnp.where(here, counts_ref[p].astype(f32), piece)
        pieces.append(piece)
    pieces.append(jnp.zeros((tokens, LANES), f32))
    send_ref[:, main:] = jnp.concatenate(pieces, axis=0).astype(bf16)


def unpacked(packed, steps, tokens):
    rows, part = (steps + 1) * tokens, packed.shape[1] // steps
    cube = packed.reshape(packed.shape[0] // rows, rows, packed.shape[1])
    step = lax.div(iota((1, rows, part), 1), tokens)
    last = jnp.zeros((cube.shape[0], rows, part), f32)
    for s in range(steps):
        last = jnp.where(step == s, pltpu.roll(cube[:, :, s * part : (s + 1) * part], rows - (steps - s) * tokens, 1), last)
    return last.reshape(packed.shape[0], part)


def packed(plain, steps, tokens):
    rows, part = (steps + 1) * tokens, plain.shape[1] // (steps + 1)
    main = steps * part
    cube = plain.reshape(plain.shape[0] // rows, rows, plain.shape[1])
    last = cube[:, :, main:]
    extra = jnp.concatenate([pltpu.roll(last, (steps - s) * tokens, 1) for s in range(steps)], axis=2)
    in_main = iota((1, rows, main), 1) < steps * tokens
    return jnp.where(in_main, cube[:, :, :main], extra).reshape(plain.shape[0], main)


def halves(even_ref, odd_ref, at):
    return jnp.concatenate([even_ref[:, at], odd_ref[:, at]], axis=0)


def expert_products(steps, tokens, features, gate_ref, up_ref, half):
    main = features.shape[1]
    part = main // steps
    columns = main + part
    local = gate_ref.shape[0]
    extra = unpacked(features.astype(f32), steps, tokens).astype(bf16)
    first = pl.ds(pl.multiple_of(half * columns, LANES), main)
    last = pl.ds(pl.multiple_of(half * columns + main, LANES), part)
    return [
        dot(features, ref[e, first, :]) + dot(extra, ref[e, last, :]) for ref in (gate_ref, up_ref) for e in range(local)
    ]


def partial_kernel(steps, tokens, after_ref, also_after_ref, even_ref, odd_ref, gate_ref, up_ref, out_ref):
    main = even_ref.shape[1] - LANES
    products = expert_products(steps, tokens, halves(even_ref, odd_ref, slice(0, main)), gate_ref, up_ref, lax.axis_index("tensor"))
    for n, product in enumerate(products):
        out_ref[n] = product


def hidden_kernel(steps, tokens, experts, partial_ref, even_ref, odd_ref, even_other_ref, odd_other_ref, gate_ref, up_ref, out_ref):
    main = even_ref.shape[1] - LANES
    total = 2 * even_ref.shape[0]
    rows = (steps + 1) * tokens
    columns = main + main // steps
    local, _, units = gate_ref.shape
    features = halves(even_other_ref, odd_other_ref, slice(0, main))
    products = expert_products(steps, tokens, features, gate_ref, up_ref, 1 - lax.axis_index("tensor"))
    meta = halves(even_ref, odd_ref, slice(main, None)).astype(f32)
    meta_other = halves(even_other_ref, odd_other_ref, slice(main, None)).astype(f32)
    lane = iota(meta.shape, 1)
    valid = lax.rem(iota((total, 1), 0), rows) < steps * tokens
    in_squares = (lane == 2 * experts) | (lane == 2 * experts + 1)
    square_sum = jnp.sum(jnp.where(in_squares, meta + meta_other, 0.0), axis=1, keepdims=True)
    factor = jnp.where(valid, lax.rsqrt(square_sum / (2 * columns) + epsilon), 0.0)
    first_expert = lax.axis_index("expert") * local
    for e in range(local):
        at = first_expert + e
        share = jnp.sum(jnp.where((lane == at) | (lane == at + experts), meta, 0.0), axis=1, keepdims=True)
        gate = ((partial_ref[e] + products[e]) * factor).astype(bf16).astype(f32)
        up = ((partial_ref[local + e] + products[local + e]) * factor).astype(bf16).astype(f32)
        hidden = gate / (1.0 + jnp.exp(-gate)) * up * share
        out_ref[:, e * units : (e + 1) * units] = hidden.astype(bf16)


def down_kernel(steps, tokens, own_ref, other_ref, down_ref, kept_ref, leaving_ref):
    total, width = own_ref.shape
    local, _, columns = down_ref.shape
    units = width // local
    mine = lax.axis_index("tensor")
    product = 0.0
    for ref, half in ((own_ref, mine), (other_ref, 1 - mine)):
        start = pl.multiple_of(half * units, LANES)
        for e in range(local):
            product += dot(ref[:, e * units : (e + 1) * units], down_ref[e, pl.ds(start, units), :])
    product = packed(product, steps, tokens)
    kept_ref[...] = product[: total // 2]
    leaving_ref[...] = product[total // 2 :].astype(bf16)


def resample_kernel(steps, early, counts_ref, near_ref, relay_ref, ck_ref, cv_ref, nk_ref, nv_ref, keys_ref, values_ref):
    tokens, kv_heads, cached, width = ck_ref.shape
    devices = counts_ref.shape[0]
    me = lax.axis_index("expert")
    first = me * tokens
    odd = lax.rem(me, 2)
    per = REACH * kv_heads
    running = jnp.int32(0)
    ancestors = [jnp.int32(0)] * tokens
    for d in range(devices):
        k = jnp.bitwise_xor(me, d)
        for p in range(tokens):
            running = running + counts_ref[k, p]
            for i in range(tokens):
                ancestors[i] = ancestors[i] + (running <= first + i).astype(jnp.int32)

    for i in range(tokens):
        offset = ancestors[i] - first

        @pl.when((offset >= 0) & (offset < tokens))
        def _():
            for out_ref, cache_ref, new_ref in ((keys_ref, ck_ref, nk_ref), (values_ref, cv_ref, nv_ref)):
                out_ref[i, :cached] = jnp.swapaxes(cache_ref[offset], 0, 1)
                for s in range(steps):
                    out_ref[i, cached + s] = new_ref[s, offset]

        def from_halo(ref, at):
            for kind, out_ref in enumerate((keys_ref, values_ref)):
                slots = ref[pl.ds(kind * per + at * kv_heads, kv_heads)]
                out_ref[i] = jnp.swapaxes(slots[:, : cached + steps], 0, 1)

        left = offset < 0
        near = (left & (odd == 1)) | ((offset >= tokens) & (odd == 0))
        far = (left & (odd == 0)) | ((offset >= tokens) & (odd == 1))
        at = jnp.where(left, offset + REACH, offset - tokens)

        @pl.when(near)
        def _():
            from_halo(near_ref, at)

        @pl.when(far)
        def _():
            from_halo(relay_ref, at)


def add_kernel(a_ref, b_ref, out_ref):
    out_ref[...] = (a_ref[...] + b_ref[...].astype(f32)).astype(out_ref.dtype)


def total_kernel(count, *refs):
    out_ref = refs[-1]
    value = refs[0][...]
    for ref in refs[1 : count + 1]:
        value = value + ref[...].astype(f32)
    out_ref[...] = value.astype(out_ref.dtype)


def unpack_kernel(own_ref, other_ref, out_ref):
    steps, tokens, model_width = out_ref.shape
    columns = model_width // 2
    main = own_ref.shape[1]
    part = main // steps
    mine = lax.axis_index("tensor")
    for ref, half in ((own_ref, mine), (other_ref, 1 - mine)):
        block = ref[...].astype(f32)
        first = pl.multiple_of(half * columns, LANES)
        last = pl.multiple_of(half * columns + main, LANES)
        for s in range(steps):
            out_ref[s, :, pl.ds(first, main)] = block[s * tokens : (s + 1) * tokens].astype(bf16)
            out_ref[s, :, pl.ds(last, part)] = block[steps * tokens :, s * part : (s + 1) * part].astype(bf16)


VMEM = pl.BlockSpec(memory_space=pltpu.VMEM)
SMEM = pl.BlockSpec(memory_space=pltpu.SMEM)
HBM = pl.BlockSpec(memory_space=pltpu.HBM)


def call(kernel, out, specs, name, microseconds, scratch=(), limit=20):
    outs = jax.tree.map(lambda _: VMEM, out)
    return pl.pallas_call(
        kernel, out_shape=out, in_specs=specs, out_specs=outs, scratch_shapes=scratch, name=name,
        cost_estimate=pl.CostEstimate(flops=0, bytes_accessed=int(microseconds * 3.5e6), transcendentals=0),
        compiler_params=pltpu.CompilerParams(vmem_limit_bytes=limit << 20),
    )


def struct(shape, dtype):
    return jax.ShapeDtypeStruct(shape, dtype)


def in_hbm(value):
    return pltpu.with_memory_space_constraint(value, pltpu.HBM)


def fast_shards(
    hidden_in, queries, new_keys, new_values, cache_keys, cache_values, route_ids, route_weights, norm_gain,
    gate_weight, up_weight, down_weight, ancestor_counts,
):
    steps, tokens, heads, width = queries.shape
    kv_heads, cached = cache_keys.shape[1:3]
    count = lax.axis_size("expert")
    local, _, units = gate_weight.shape
    experts = local * count
    columns = down_weight.shape[2]
    part = columns // (steps + 1)
    main = steps * part
    rows = (steps + 1) * tokens
    per = REACH * kv_heads
    early = 2 * per + per // 2
    square = steps * tokens * heads
    chosen = pltpu.VMEM((square, square), bf16)
    halos = [pltpu.VMEM((slots, cached + PAD, width), bf16) for slots in (early, 4 * per - early)]

    def swap(value, offset):
        return lax.ppermute(value, "expert", [(i, i ^ offset) for i in range(count)])

    def sibling(value):
        return lax.ppermute(value, "tensor", [(0, 1), (1, 0)])

    inputs = (route_ids, route_weights, ancestor_counts, norm_gain.reshape(1, -1), hidden_in, queries, new_keys, new_values, cache_keys, cache_values)
    spaces = [pltpu.SMEM if value is ancestor_counts else pltpu.VMEM for value in inputs]
    loaded = pl.pallas_call(
        functools.partial(load_kernel, steps),
        out_shape=[space(value.shape, value.dtype) for space, value in zip(spaces, inputs)] + [chosen] + halos,
        in_specs=[HBM] * len(inputs), out_specs=[pl.BlockSpec(memory_space=space) for space in spaces] + [VMEM] * 3,
        scratch_shapes=[pltpu.SemaphoreType.DMA((len(inputs),))], name="load",
        compiler_params=pltpu.CompilerParams(vmem_limit_bytes=20 << 20),
    )(*(in_hbm(value) for value in inputs))
    *loaded, near, far = loaded
    near = swap(near, 1)
    new_keys, new_values, cache_keys, cache_values = loaded[6:10]
    send, residual = call(
        functools.partial(attend_kernel, steps, experts),
        (struct((rows, main + LANES), bf16), struct((rows, main), f32)),
        [VMEM, VMEM, SMEM] + [VMEM] * 8, "attend", 2.3, [pltpu.VMEM(((steps + 1) * rows, LANES), f32)],
    )(*loaded)

    far_first = range(count - 2, 0, -2)
    def fetch(after, weight, name):
        return pl.pallas_call(
            weight_kernel, out_shape=[pltpu.VMEM(weight.shape, weight.dtype), pltpu.VMEM((8, LANES), f32)],
            in_specs=[VMEM, HBM], out_specs=[VMEM] * 2, scratch_shapes=[pltpu.SemaphoreType.DMA((2 * local,))], name=name,
            cost_estimate=pl.CostEstimate(flops=0, bytes_accessed=7_000_000, transcendentals=0),
            compiler_params=pltpu.CompilerParams(vmem_limit_bytes=16 << 20),
        )(after, in_hbm(weight))

    gate, token = fetch(residual, gate_weight, "gate")
    even = jnp.concatenate([send] + [swap(send, k) for k in far_first], axis=0)
    even, near, token = lax.optimization_barrier((even, near, token))
    odd = swap(even, 1)
    even_other = sibling(even)
    up, token_up = fetch(even, up_weight, "up")
    odd, token_up, far = lax.optimization_barrier((odd, token_up, far))
    relayed = swap(far, 1)
    odd_other = sibling(odd)
    partial = call(
        functools.partial(partial_kernel, steps, tokens), struct((2 * local, count * rows, units), f32), [VMEM] * 6, "partial", 0.01,
    )(token, token_up, even, odd, gate, up)
    hidden = call(
        functools.partial(hidden_kernel, steps, tokens, experts),
        struct((count * rows, local * units), bf16), [VMEM] * 7, "hidden", 0.01,
    )(partial, even, odd, even_other, odd_other, gate, up)
    other_hidden = sibling(hidden)
    half = count // 2 * rows

    kept, leaving = call(
        functools.partial(down_kernel, steps, tokens), (struct((half, main), f32), struct((half, main), bf16)), [VMEM] * 3, "down", 0.01,
    )(hidden, other_hidden, down_weight)
    leaving, relayed = lax.optimization_barrier((leaving, relayed))
    arrived = swap(leaving, 1)
    ring = [(i, i + 2 if i % 2 == 0 else i - 2) for i in range(count) if (i < count - 2 if i % 2 == 0 else i > 1)]
    far = lax.ppermute(jnp.concatenate([near[2 * per :], relayed], axis=0), "expert", ring)
    own_block, others = kept[:rows], call(add_kernel, struct((half - rows, main), bf16), [VMEM] * 2, "add", 0.1)(kept[rows:], arrived[rows:])

    counts = [block.reshape(count // 2, rows, main + LANES)[:, :tokens, main + 2 * experts + 2].astype(jnp.int32) for block in (even, odd)]
    place = [0, *far_first]
    counts = jnp.stack([counts[k % 2][place.index(k - k % 2)] for k in range(count)])
    out = struct((tokens, cached + steps, kv_heads, width), bf16)
    keys, values = call(functools.partial(resample_kernel, steps, early), (out, out), [SMEM] + [VMEM] * 6, "resample", 2.2)(
        counts, near, far, cache_keys, cache_values, new_keys, new_values
    )
    returned = [swap(others[n * rows : (n + 1) * rows], k) for n, k in enumerate(far_first)]
    keys, values, *returned = lax.optimization_barrier((keys, values, *returned))
    result = call(functools.partial(total_kernel, len(returned) + 2), struct((rows, main), bf16), [VMEM] * (len(returned) + 3), "total", 0.1)(
        residual, own_block, arrived[:rows], *returned
    )
    layer_out = call(unpack_kernel, struct((steps, tokens, 2 * columns), bf16), [VMEM] * 2, "unpack", 0.5)(result, sibling(result))
    return layer_out, keys.transpose(0, 2, 1, 3), values.transpose(0, 2, 1, 3)


def padded(cells, sides, width):
    for axis, dim in sides:
        count = lax.axis_size(axis)
        ends = count - 1
        head = lax.slice_in_dim(cells, 0, width, axis=dim)
        tail = lax.slice_in_dim(cells, cells.shape[dim] - width, cells.shape[dim], axis=dim)
        cells = jnp.concatenate(
            [
                lax.ppermute(tail, axis, [(i, (i + 1) % count) for i in range(ends)]),
                cells,
                lax.ppermute(head, axis, [((i + 1) % count, i) for i in range(ends)]),
            ],
            axis=dim,
        )
    return cells


def shards(
    hidden_in,
    queries,
    new_keys,
    new_values,
    cache_keys,
    cache_values,
    route_ids,
    route_weights,
    norm_gain,
    gate_weight,
    up_weight,
    down_weight,
    ancestor_counts,
):
    step_count, token_count, query_heads, head_width = queries.shape
    key_heads = cache_keys.shape[1]
    cached = cache_keys.shape[2]
    group_size = query_heads // key_heads
    cache_pair = jnp.stack([cache_keys, cache_values])
    fresh_pair = jnp.transpose(jnp.stack([new_keys, new_values]), (0, 2, 3, 1, 4))
    both_kv = jnp.concatenate([cache_pair, fresh_pair], axis=3)
    length = both_kv.shape[3]
    grouped = queries.reshape(step_count, token_count, key_heads, group_size, head_width)
    scores = jnp.einsum(
        "sphgd,phld->sphgl", grouped, both_kv[0], preferred_element_type=jnp.float32
    ) / math.sqrt(head_width)
    allowed = lax.broadcasted_iota(
        jnp.int32, (step_count, length), 1
    ) <= cached + lax.broadcasted_iota(jnp.int32, (step_count, length), 0)
    scores = jnp.where(allowed[:, None, None, None, :], scores, -1e30)
    exponent = jnp.exp(scores - jnp.max(scores, axis=-1, keepdims=True))
    attn_weights = (exponent / jnp.sum(exponent, axis=-1, keepdims=True)).astype(jnp.bfloat16)
    attended = jnp.einsum(
        "sphgl,phld->sphgd", attn_weights, both_kv[1], preferred_element_type=jnp.float32
    )
    attended = attended.astype(jnp.bfloat16).reshape(
        step_count, token_count, query_heads * head_width
    )
    attended = lax.all_gather(attended, "tensor", axis=2, tiled=True)
    expert_count = lax.axis_size("expert")
    group_count = lax.axis_size("group")
    tensor_count = lax.axis_size("tensor")
    tensor_index = lax.axis_index("tensor")
    expert_local = gate_weight.shape[0]
    experts_all = expert_local * expert_count
    chosen_count = route_ids.shape[2]
    model_width = hidden_in.shape[2]
    column_width = down_weight.shape[2]
    capacity = min(token_count, max(2, 2 * token_count * chosen_count // experts_all))
    pair_count = token_count * chosen_count
    expert_iota = jnp.arange(experts_all, dtype=jnp.int32)
    slot_iota = jnp.arange(capacity, dtype=jnp.int32)
    token_owner = (
        (jnp.arange(pair_count) // chosen_count)[:, None] == jnp.arange(token_count)[None, :]
    ).astype(jnp.float32)
    halves = []
    for step_index in range(step_count):
        residual = hidden_in[step_index].astype(jnp.float32) + attended[step_index].astype(
            jnp.float32
        )
        normed = (
            residual
            * lax.rsqrt(jnp.mean(residual * residual, axis=-1, keepdims=True) + epsilon)
            * norm_gain
        ).astype(jnp.bfloat16)
        chosen = route_ids[step_index].reshape(pair_count)
        route_share = route_weights[step_index] / jnp.sum(
            route_weights[step_index], axis=-1, keepdims=True
        )
        expert_hits = (chosen[:, None] == expert_iota[None, :]).astype(jnp.int32)
        position = jnp.sum((jnp.cumsum(expert_hits, axis=0) - expert_hits) * expert_hits, axis=1)
        slotted = (
            expert_hits[:, :, None]
            * (position[:, None, None] == slot_iota[None, None, :]).astype(jnp.int32)
        ).astype(jnp.float32)
        dispatch = jnp.einsum("rec,rt->ect", slotted, token_owner, precision=highest)
        dispatch = dispatch.reshape(expert_count, expert_local, capacity, token_count).astype(
            jnp.bfloat16
        )
        combine = jnp.einsum(
            "rec,rt,r->tec",
            slotted,
            token_owner,
            route_share.reshape(pair_count),
            precision=highest,
        )
        combine = combine.reshape(token_count, expert_count, expert_local, capacity)
        feature_blocks = normed.reshape(token_count, group_count, model_width // group_count)
        outgoing = jnp.einsum(
            "aict,tgd->agicd", dispatch, feature_blocks, preferred_element_type=jnp.float32
        ).astype(jnp.bfloat16)
        flattened = outgoing.reshape(
            expert_count * group_count, expert_local, capacity, model_width // group_count
        )
        received = lax.all_to_all(
            flattened, ("expert", "group"), split_axis=0, concat_axis=0, tiled=True
        )
        gate_part = jnp.einsum(
            "seki,eif->sekf", received, gate_weight, preferred_element_type=jnp.float32
        ).astype(jnp.bfloat16)
        up_part = jnp.einsum(
            "seki,eif->sekf", received, up_weight, preferred_element_type=jnp.float32
        ).astype(jnp.bfloat16)
        gate_sum = lax.psum(gate_part, "group").astype(jnp.float32)
        up_sum = lax.psum(up_part, "group").astype(jnp.float32)
        hidden = (jax.nn.silu(gate_sum) * up_sum).astype(jnp.bfloat16)
        hidden = lax.all_gather(hidden, "tensor", axis=3, tiled=True)
        answered = jnp.einsum(
            "sekf,efo->seko", hidden, down_weight, preferred_element_type=jnp.float32
        ).astype(jnp.bfloat16)
        returned = lax.all_to_all(
            answered, ("expert", "group"), split_axis=0, concat_axis=0, tiled=True
        )
        returned = returned.reshape(
            expert_count, group_count, expert_local, capacity, column_width
        ).astype(jnp.float32)
        expert_mix = jnp.einsum("taic,agicd->tgd", combine, returned, precision=highest)
        own_columns = lax.dynamic_index_in_dim(
            residual.reshape(token_count, group_count, tensor_count, column_width),
            tensor_index,
            2,
            keepdims=False,
        )
        halves.append((own_columns + expert_mix).astype(jnp.bfloat16))
    stacked = jnp.stack(halves)
    layer_out = lax.all_gather(stacked, "tensor", axis=3, tiled=True).reshape(
        step_count, token_count, model_width
    )
    every_count = lax.all_gather(ancestor_counts, ("expert", "group"), axis=0, tiled=True)
    running = jnp.cumsum(every_count)
    first_index = lax.axis_index(("expert", "group")) * token_count
    own_index = first_index + jnp.arange(token_count, dtype=jnp.int32)
    ancestor = jnp.sum((running[None, :] <= own_index[:, None]).astype(jnp.int32), axis=1)
    widened = padded(both_kv, ((("expert", "group"), 1),), REACH)
    window_index = first_index - REACH + jnp.arange(token_count + 2 * REACH, dtype=jnp.int32)
    selector = (ancestor[:, None] == window_index[None, :]).astype(jnp.bfloat16)
    resampled = jnp.einsum(
        "tw,kwhld->kthld", selector, widened, preferred_element_type=jnp.float32
    ).astype(jnp.bfloat16)
    return (layer_out, resampled[0], resampled[1])


def solution(mesh):
    count = mesh.shape["expert"]
    fast = mesh.shape["group"] == 1 and mesh.shape["tensor"] == 2 and count % 2 == 0 and count & (count - 1) == 0
    in_specs = (
        P(None, ("parts", "expert", "group"), None),
        P(None, ("parts", "expert", "group"), "tensor", None),
        P(None, ("parts", "expert", "group"), "tensor", None),
        P(None, ("parts", "expert", "group"), "tensor", None),
        P(("parts", "expert", "group"), "tensor", None, None),
        P(("parts", "expert", "group"), "tensor", None, None),
        P(None, ("parts", "expert", "group"), None),
        P(None, ("parts", "expert", "group"), None),
        P(),
        P("expert", "group", "tensor"),
        P("expert", "group", "tensor"),
        P("expert", None, ("group", "tensor")),
        P(("parts", "expert", "group")),
    )
    out_specs = (
        P(None, ("parts", "expert", "group"), None),
        P(("parts", "expert", "group"), "tensor", None, None),
        P(("parts", "expert", "group"), "tensor", None, None),
    )
    return jax.shard_map(fast_shards if fast else shards, mesh=mesh, in_specs=in_specs, out_specs=out_specs, check_vma=False)
```

```python
import functools
import math

import jax
import jax.numpy as jnp
from jax import lax
from jax.experimental import pallas as pl
from jax.experimental.pallas import tpu as pltpu
from jax.sharding import PartitionSpec as P

REACH = 2
LANES = 128
f32, bf16 = jnp.float32, jnp.bfloat16

epsilon = 1e-06
highest = lax.Precision.HIGHEST


def dot(a, b, dims=((1,), (0,))):
    return lax.dot_general(a, b, (dims, ((), ())), preferred_element_type=f32)


def iota(shape, dim):
    return lax.broadcasted_iota(jnp.int32, shape, dim)


def packing(steps, tokens, heads):
    rows, per_part = (steps + 1) * tokens, heads // (steps + 1)
    tiles, count = steps * per_part, tokens * steps * heads
    target = iota((tiles * rows, count), 0)
    tile, inner = lax.div(target, rows), lax.rem(target, rows)
    is_extra = inner >= steps * tokens
    step = jnp.where(is_extra, lax.div(tile, per_part), lax.div(inner, tokens))
    token = lax.rem(inner, tokens)
    head = jnp.where(is_extra, tiles + lax.rem(tile, per_part), tile)
    chosen = (token * steps + step) * heads + head == iota((tiles * rows, count), 1)
    return chosen.astype(f32).astype(bf16)


def load_kernel(
    steps, ids_in, weights_in, counts_in, gain_in, hidden_in, q_in, nk_in, nv_in, ck_in, cv_in,
    ids_ref, weights_ref, counts_ref, gain_ref, hidden_ref, q_ref, nk_ref, nv_ref, ck_ref, cv_ref, chosen_ref, near_ref, far_ref, sems,
):
    pairs = (
        (ck_in, ck_ref), (cv_in, cv_ref), (nk_in, nk_ref), (nv_in, nv_ref), (q_in, q_ref), (hidden_in, hidden_ref),
        (gain_in, gain_ref), (ids_in, ids_ref), (weights_in, weights_ref), (counts_in, counts_ref),
    )
    copies = [pltpu.make_async_copy(source, target, sems.at[n]) for n, (source, target) in enumerate(pairs)]
    for copy in copies:
        copy.start()
    tokens, kv_heads, cached, width = ck_ref.shape
    chosen_ref[...] = packing(steps, tokens, q_ref.shape[2])
    for copy in copies:
        copy.wait()

    odd = lax.rem(lax.axis_index("expert"), 2)
    per = REACH * kv_heads

    early = 2 * per + per // 2

    def halo(start, kinds, slot):
        for cache_ref, new_ref in kinds:
            for r in range(REACH):
                for h in range(kv_heads):
                    out_ref, at = (near_ref, slot) if slot < early else (far_ref, slot - early)
                    out_ref[at * cached : (at + 1) * cached, :] = cache_ref[start + r, h]
                    yield from (new_ref[s, start + r, h : h + 1, :].astype(f32) for s in range(steps))
                    slot += 1

    def fill(near, far):
        rows = [*halo(near, (keys, values), 0), *halo(far, (keys, values), 2 * per)]
        for out_ref, own in ((near_ref, rows[: early * steps]), (far_ref, rows[early * steps :])):
            below = out_ref.shape[0] - len(own) // steps * cached
            block = jnp.concatenate(own + [jnp.zeros((below - len(own), width), f32)], axis=0)
            out_ref[out_ref.shape[0] - below :, :] = block.astype(bf16)

    keys, values = (ck_ref, nk_ref), (cv_ref, nv_ref)
    tail = tokens - REACH

    @pl.when(odd == 0)
    def _():
        fill(tail, 0)

    @pl.when(odd == 1)
    def _():
        fill(0, tail)


def weight_kernel(after_ref, source, own_ref, other_ref, token_ref, sems):
    half = own_ref.shape[1]
    mine = lax.axis_index("tensor")
    copies = []
    for target, place in ((own_ref, mine), (other_ref, 1 - mine)):
        rows = pl.ds(pl.multiple_of(place * half, LANES), half)
        for e in range(source.shape[0]):
            copies.append(pltpu.make_async_copy(source.at[e, rows], target.at[e], sems.at[len(copies)]))
    for copy in copies:
        copy.start()
    for copy in copies:
        copy.wait()
    token_ref[...] = jnp.zeros_like(token_ref)


def attend_kernel(
    steps, experts, ids_ref, weights_ref, counts_ref, gain_ref, hidden_ref, q_ref, nk_ref, nv_ref, ck_ref, cv_ref, chosen_ref,
    send_ref, residual_ref, scores_ref,
):
    tokens, heads, width = q_ref.shape[1:]
    kv_heads, cached = ck_ref.shape[1:3]
    group = heads // kv_heads
    columns = heads * width
    part = columns // (steps + 1)
    main = steps * part
    rows = (steps + 1) * tokens
    base = lax.axis_index("tensor") * columns
    fresh = steps * kv_heads
    fresh_rows = -(-fresh // 16) * 16
    scale = 1.0 / math.sqrt(width)

    q_rows = steps * heads
    row = iota((q_rows, kv_heads * cached), 0)
    col = iota((q_rows, kv_heads * cached), 1)
    own_head = lax.div(lax.rem(row, heads), group) == lax.div(col, cached)
    row = iota((q_rows, fresh_rows), 0)
    col = iota((q_rows, fresh_rows), 1)
    own_new = (
        (lax.div(lax.rem(row, heads), group) == lax.rem(col, kv_heads))
        & (lax.div(col, kv_heads) <= lax.div(row, heads))
        & (col < fresh)
    )
    def with_new(new_ref, p):
        pieces = [new_ref[s, p].astype(f32) for s in range(steps)]
        return jnp.concatenate(pieces + [jnp.zeros((fresh_rows - fresh, width), f32)], axis=0).astype(bf16)

    every = range(tokens)
    q = [jnp.concatenate([q_ref[s, p] for s in range(steps)], axis=0) for p in every]
    old = [dot(q[p], ck_ref[p].reshape(kv_heads * cached, width), ((1,), (1,))) for p in every]
    new = [dot(q[p], with_new(nk_ref, p), ((1,), (1,))) for p in every]
    old = [jnp.where(own_head, x * scale, -1e30) for x in old]
    new = [jnp.where(own_new, x * scale, -1e30) for x in new]
    top = [jnp.maximum(jnp.max(old[p], axis=1, keepdims=True), jnp.max(new[p], axis=1, keepdims=True)) for p in every]
    old = [jnp.exp(old[p] - top[p]) for p in every]
    new = [jnp.exp(new[p] - top[p]) for p in every]
    inverse = [1.0 / (jnp.sum(old[p], axis=1, keepdims=True) + jnp.sum(new[p], axis=1, keepdims=True)) for p in every]
    old = [(old[p] * inverse[p]).astype(bf16) for p in every]
    new = [(new[p] * inverse[p]).astype(bf16) for p in every]
    attended = jnp.concatenate([
        (dot(old[p], cv_ref[p].reshape(kv_heads * cached, width)) + dot(new[p], with_new(nv_ref, p))).astype(bf16) for p in every
    ], axis=0)

    tiles = main // width
    moved = dot(chosen_ref[...], attended)
    for s in range(steps):
        residual_ref[s * tokens : (s + 1) * tokens, :] = hidden_ref[s, :, pl.ds(pl.multiple_of(base, LANES), main)].astype(f32)
        residual_ref[steps * tokens :, s * part : (s + 1) * part] = hidden_ref[
            s, :, pl.ds(pl.multiple_of(base + main, LANES), part)
        ].astype(f32)
    residual = residual_ref[...] + jnp.concatenate([moved[j * rows : (j + 1) * rows] for j in range(tiles)], axis=1)
    residual_ref[...] = residual
    gain_main = gain_ref[:, pl.ds(pl.multiple_of(base, LANES), main)]
    gain_last = gain_ref[:, pl.ds(pl.multiple_of(base + main, LANES), part)]
    in_main = iota((rows, main), 0) < steps * tokens
    gain = jnp.where(in_main, gain_main, jnp.concatenate([gain_last] * steps, axis=1))
    send_ref[:, :main] = (residual * gain).astype(bf16)

    squares = residual * residual
    lane = iota((tokens, LANES), 1)
    for s in range(steps):
        scores_ref[s * rows : (s + 1) * rows, :] = jnp.broadcast_to(
            jnp.sum(squares[:, s * part : (s + 1) * part], axis=1, keepdims=True), (rows, LANES))
    whole = sum(scores_ref[s * rows : (s + 1) * rows, :] for s in range(steps))
    scores_ref[steps * rows :, :] = whole
    pieces = []
    for s in range(steps):
        square_sum = (
            scores_ref[steps * rows + s * tokens : steps * rows + (s + 1) * tokens, :]
            + scores_ref[s * rows + steps * tokens : (s + 1) * rows, :]
        )
        ids, weights = ids_ref[s], weights_ref[s]
        share = weights / jnp.sum(weights, axis=1, keepdims=True)
        value = jnp.zeros((tokens, LANES), f32)
        expert = jnp.where(lane < experts, lane, lane - experts)
        for k in range(ids.shape[1]):
            value = jnp.where(ids[:, k : k + 1] == expert, share[:, k : k + 1], value)
        value = jnp.where(lane < 2 * experts, value, square_sum)
        high = value.astype(bf16).astype(f32)
        low = value - high
        piece = jnp.where((lane < experts) | (lane == 2 * experts), high, low)
        piece = jnp.where(lane < 2 * experts + 2, piece, 0.0)
        if s == 0:
            for p in range(tokens):
                here = (lane == 2 * experts + 2) & (iota((tokens, LANES), 0) == p)
                piece = jnp.where(here, counts_ref[p].astype(f32), piece)
        pieces.append(piece)
    pieces.append(jnp.zeros((tokens, LANES), f32))
    send_ref[:, main:] = jnp.concatenate(pieces, axis=0).astype(bf16)


def unpacked(packed, steps, tokens):
    rows, part = (steps + 1) * tokens, packed.shape[1] // steps
    cube = packed.reshape(packed.shape[0] // rows, rows, packed.shape[1])
    step = lax.div(iota((1, rows, part), 1), tokens)
    last = jnp.zeros((cube.shape[0], rows, part), f32)
    for s in range(steps):
        last = jnp.where(step == s, pltpu.roll(cube[:, :, s * part : (s + 1) * part], rows - (steps - s) * tokens, 1), last)
    return last.reshape(packed.shape[0], part)


def packed(plain, steps, tokens):
    rows, part = (steps + 1) * tokens, plain.shape[1] // (steps + 1)
    main = steps * part
    cube = plain.reshape(plain.shape[0] // rows, rows, plain.shape[1])
    last = cube[:, :, main:]
    extra = jnp.concatenate([pltpu.roll(last, (steps - s) * tokens, 1) for s in range(steps)], axis=2)
    in_main = iota((1, rows, main), 1) < steps * tokens
    return jnp.where(in_main, cube[:, :, :main], extra).reshape(plain.shape[0], main)


def halves(even_ref, odd_ref, at):
    return jnp.concatenate([even_ref[:, at], odd_ref[:, at]], axis=0)


def expert_products(steps, tokens, features, gate_ref, up_ref):
    main = features.shape[1]
    local = gate_ref.shape[0]
    extra = unpacked(features.astype(f32), steps, tokens).astype(bf16)
    return [
        dot(features, ref[e, :main, :]) + dot(extra, ref[e, main:, :]) for ref in (gate_ref, up_ref) for e in range(local)
    ]


def partial_kernel(steps, tokens, after_ref, also_after_ref, even_ref, odd_ref, gate_ref, up_ref, out_ref):
    main = even_ref.shape[1] - LANES
    products = expert_products(steps, tokens, halves(even_ref, odd_ref, slice(0, main)), gate_ref, up_ref)
    for n, product in enumerate(products):
        out_ref[n] = product


def hidden_kernel(steps, tokens, experts, partial_ref, even_ref, odd_ref, even_other_ref, odd_other_ref, gate_ref, up_ref, out_ref):
    main = even_ref.shape[1] - LANES
    total = 2 * even_ref.shape[0]
    rows = (steps + 1) * tokens
    columns = main + main // steps
    local, _, units = gate_ref.shape
    features = halves(even_other_ref, odd_other_ref, slice(0, main))
    products = expert_products(steps, tokens, features, gate_ref, up_ref)
    meta = halves(even_ref, odd_ref, slice(main, None)).astype(f32)
    meta_other = halves(even_other_ref, odd_other_ref, slice(main, None)).astype(f32)
    lane = iota(meta.shape, 1)
    valid = lax.rem(iota((total, 1), 0), rows) < steps * tokens
    in_squares = (lane == 2 * experts) | (lane == 2 * experts + 1)
    square_sum = jnp.sum(jnp.where(in_squares, meta + meta_other, 0.0), axis=1, keepdims=True)
    factor = jnp.where(valid, lax.rsqrt(square_sum / (2 * columns) + epsilon), 0.0)
    first_expert = lax.axis_index("expert") * local
    for e in range(local):
        at = first_expert + e
        share = jnp.sum(jnp.where((lane == at) | (lane == at + experts), meta, 0.0), axis=1, keepdims=True)
        gate = ((partial_ref[e] + products[e]) * factor).astype(bf16).astype(f32)
        up = ((partial_ref[local + e] + products[local + e]) * factor).astype(bf16).astype(f32)
        hidden = gate / (1.0 + jnp.exp(-gate)) * up * share
        out_ref[:, e * units : (e + 1) * units] = hidden.astype(bf16)


def down_kernel(steps, tokens, own_ref, other_ref, down_ref, kept_ref, leaving_ref):
    total, width = own_ref.shape
    local, _, columns = down_ref.shape
    units = width // local
    mine = lax.axis_index("tensor")
    product = 0.0
    for ref, half in ((own_ref, mine), (other_ref, 1 - mine)):
        start = pl.multiple_of(half * units, LANES)
        for e in range(local):
            product += dot(ref[:, e * units : (e + 1) * units], down_ref[e, pl.ds(start, units), :])
    product = packed(product, steps, tokens)
    kept_ref[...] = product[: total // 2]
    leaving_ref[...] = product[total // 2 :].astype(bf16)


def join_kernel(near_ref, rest_ref, out_ref):
    ahead = out_ref.shape[0] - rest_ref.shape[0]
    out_ref[:ahead, :] = near_ref[near_ref.shape[0] - ahead :, :]
    out_ref[ahead:, :] = rest_ref[...]


def resample_kernel(steps, early, counts_ref, near_ref, relay_ref, ck_ref, cv_ref, nk_ref, nv_ref, keys_ref, values_ref):
    tokens, kv_heads, cached, width = ck_ref.shape
    devices = counts_ref.shape[0]
    me = lax.axis_index("expert")
    first = me * tokens
    odd = lax.rem(me, 2)
    per = REACH * kv_heads
    running = jnp.int32(0)
    ancestors = [jnp.int32(0)] * tokens
    for d in range(devices):
        k = jnp.bitwise_xor(me, d)
        for p in range(tokens):
            running = running + counts_ref[k, p]
            for i in range(tokens):
                ancestors[i] = ancestors[i] + (running <= first + i).astype(jnp.int32)

    for i in range(tokens):
        offset = ancestors[i] - first

        @pl.when((offset >= 0) & (offset < tokens))
        def _():
            for out_ref, cache_ref, new_ref in ((keys_ref, ck_ref, nk_ref), (values_ref, cv_ref, nv_ref)):
                out_ref[i, :cached] = jnp.swapaxes(cache_ref[offset], 0, 1)
                for s in range(steps):
                    out_ref[i, cached + s] = new_ref[s, offset]

        def near_rows(slot):
            return slot * cached, early * cached + slot * steps

        def far_rows(slot):
            ahead = early - 2 * per
            if slot < ahead:
                return slot * cached, ahead * cached + (2 * per + slot) * steps
            begin = near_ref.shape[0] - 2 * per * cached
            return begin + (slot - ahead) * cached, begin + (2 * per - ahead) * cached + (slot - ahead) * steps

        def from_halo(ref, rows_of, at):
            for kind, out_ref in enumerate((keys_ref, values_ref)):
                places = [rows_of(kind * per + at * kv_heads + h) for h in range(kv_heads)]
                first_row, first_new = places[0]
                block = ref[first_row : first_row + kv_heads * cached, :].reshape(kv_heads, cached, width)
                out_ref[i, :cached] = jnp.swapaxes(block, 0, 1)
                aligned = first_new // 16 * 16
                fresh = ref[aligned : aligned + 32, :].astype(f32) if aligned + 32 <= ref.shape[0] else ref[ref.shape[0] - 32 :, :].astype(f32)
                aligned = min(aligned, ref.shape[0] - 32)
                for s in range(steps):
                    pair = [fresh[place + s - aligned : place + s - aligned + 1] for _, place in places]
                    out_ref[i, cached + s] = jnp.concatenate(pair, axis=0).astype(bf16)

        left, right = offset < 0, offset >= tokens
        near = (left & (odd == 1)) | (right & (odd == 0))
        far = (left & (odd == 0)) | (right & (odd == 1))
        at = jnp.where(left, offset + REACH, offset - tokens)
        for n in range(REACH):

            @pl.when(near & (at == n))
            def _():
                from_halo(near_ref, near_rows, n)

            @pl.when(far & (at == n))
            def _():
                from_halo(relay_ref, far_rows, n)


def add_kernel(a_ref, b_ref, out_ref):
    out_ref[...] = (a_ref[...] + b_ref[...].astype(f32)).astype(out_ref.dtype)


def total_kernel(count, *refs):
    out_ref = refs[-1]
    value = refs[0][...]
    for ref in refs[1 : count + 1]:
        value = value + ref[...].astype(f32)
    out_ref[...] = value.astype(out_ref.dtype)


def unpack_kernel(own_ref, other_ref, out_ref):
    steps, tokens, model_width = out_ref.shape
    columns = model_width // 2
    main = own_ref.shape[1]
    part = main // steps
    mine = lax.axis_index("tensor")
    for ref, half in ((own_ref, mine), (other_ref, 1 - mine)):
        block = ref[...].astype(f32)
        first = pl.multiple_of(half * columns, LANES)
        last = pl.multiple_of(half * columns + main, LANES)
        for s in range(steps):
            out_ref[s, :, pl.ds(first, main)] = block[s * tokens : (s + 1) * tokens].astype(bf16)
            out_ref[s, :, pl.ds(last, part)] = block[steps * tokens :, s * part : (s + 1) * part].astype(bf16)


VMEM = pl.BlockSpec(memory_space=pltpu.VMEM)
SMEM = pl.BlockSpec(memory_space=pltpu.SMEM)
HBM = pl.BlockSpec(memory_space=pltpu.HBM)


def call(kernel, out, specs, name, microseconds, scratch=(), limit=20):
    outs = jax.tree.map(lambda _: VMEM, out)
    return pl.pallas_call(
        kernel, out_shape=out, in_specs=specs, out_specs=outs, scratch_shapes=scratch, name=name,
        cost_estimate=pl.CostEstimate(flops=0, bytes_accessed=int(microseconds * 3.5e6), transcendentals=0),
        compiler_params=pltpu.CompilerParams(vmem_limit_bytes=limit << 20),
    )


def struct(shape, dtype):
    return jax.ShapeDtypeStruct(shape, dtype)


def in_hbm(value):
    return pltpu.with_memory_space_constraint(value, pltpu.HBM)


def fast_shards(
    hidden_in, queries, new_keys, new_values, cache_keys, cache_values, route_ids, route_weights, norm_gain,
    gate_weight, up_weight, down_weight, ancestor_counts,
):
    steps, tokens, heads, width = queries.shape
    kv_heads, cached = cache_keys.shape[1:3]
    count = lax.axis_size("expert")
    local, _, units = gate_weight.shape
    experts = local * count
    columns = down_weight.shape[2]
    part = columns // (steps + 1)
    main = steps * part
    rows = (steps + 1) * tokens
    per = REACH * kv_heads
    early = 2 * per + per // 2
    square = steps * tokens * heads
    chosen = pltpu.VMEM((square, square), bf16)
    halos = [pltpu.VMEM((slots * cached + -(-slots * steps // 16) * 16, width), bf16) for slots in (early, 4 * per - early)]

    def swap(value, offset):
        return lax.ppermute(value, "expert", [(i, i ^ offset) for i in range(count)])

    def sibling(value):
        return lax.ppermute(value, "tensor", [(0, 1), (1, 0)])

    inputs = (route_ids, route_weights, ancestor_counts, norm_gain.reshape(1, -1), hidden_in, queries, new_keys, new_values, cache_keys, cache_values)
    spaces = [pltpu.SMEM if value is ancestor_counts else pltpu.VMEM for value in inputs]
    loaded = pl.pallas_call(
        functools.partial(load_kernel, steps),
        out_shape=[space(value.shape, value.dtype) for space, value in zip(spaces, inputs)] + [chosen] + halos,
        in_specs=[HBM] * len(inputs), out_specs=[pl.BlockSpec(memory_space=space) for space in spaces] + [VMEM] * 3,
        scratch_shapes=[pltpu.SemaphoreType.DMA((len(inputs),))], name="load",
        compiler_params=pltpu.CompilerParams(vmem_limit_bytes=20 << 20),
    )(*(in_hbm(value) for value in inputs))
    *loaded, near, far = loaded
    near = swap(near, 1)
    new_keys, new_values, cache_keys, cache_values = loaded[6:10]
    send, residual = call(
        functools.partial(attend_kernel, steps, experts),
        (struct((rows, main + LANES), bf16), struct((rows, main), f32)),
        [VMEM, VMEM, SMEM] + [VMEM] * 8, "attend", 2.3, [pltpu.VMEM(((steps + 1) * rows, LANES), f32)],
    )(*loaded)

    far_first = range(count - 2, 0, -2)
    def fetch(after, weight, name):
        half = pltpu.VMEM((local, columns, units), weight.dtype)
        return pl.pallas_call(
            weight_kernel, out_shape=[half, half, pltpu.VMEM((8, LANES), f32)],
            in_specs=[VMEM, HBM], out_specs=[VMEM] * 3, scratch_shapes=[pltpu.SemaphoreType.DMA((2 * local,))], name=name,
            cost_estimate=pl.CostEstimate(flops=0, bytes_accessed=7_000_000, transcendentals=0),
            compiler_params=pltpu.CompilerParams(vmem_limit_bytes=16 << 20),
        )(after, in_hbm(weight))

    gate_own, gate_other, token = fetch(residual, gate_weight, "gate")
    even = jnp.concatenate([send] + [swap(send, k) for k in far_first], axis=0)
    even, near, token = lax.optimization_barrier((even, near, token))
    odd = swap(even, 1)
    even_other = sibling(even)
    up_own, up_other, token_up = fetch(even, up_weight, "up")
    odd, token_up, far = lax.optimization_barrier((odd, token_up, far))
    relayed = swap(far, 1)
    odd_other = sibling(odd)
    partial = call(
        functools.partial(partial_kernel, steps, tokens), struct((2 * local, count * rows, units), f32), [VMEM] * 6, "partial", 0.01,
    )(token, token_up, even, odd, gate_own, up_own)
    hidden = call(
        functools.partial(hidden_kernel, steps, tokens, experts),
        struct((count * rows, local * units), bf16), [VMEM] * 7, "hidden", 0.01,
    )(partial, even, odd, even_other, odd_other, gate_other, up_other)
    other_hidden = sibling(hidden)
    half = count // 2 * rows

    kept, leaving = call(
        functools.partial(down_kernel, steps, tokens), (struct((half, main), f32), struct((half, main), bf16)), [VMEM] * 3, "down", 0.01,
    )(hidden, other_hidden, down_weight)
    leaving, relayed = lax.optimization_barrier((leaving, relayed))
    arrived = swap(leaving, 1)
    ring = [(i, i + 2 if i % 2 == 0 else i - 2) for i in range(count) if (i < count - 2 if i % 2 == 0 else i > 1)]
    joined = struct((near.shape[0] - 2 * per * cached + relayed.shape[0], width), bf16)
    far = lax.ppermute(call(join_kernel, joined, [VMEM] * 2, "join", 0.1)(near, relayed), "expert", ring)
    own_block, others = kept[:rows], call(add_kernel, struct((half - rows, main), bf16), [VMEM] * 2, "add", 0.1)(kept[rows:], arrived[rows:])

    counts = [block.reshape(count // 2, rows, main + LANES)[:, :tokens, main + 2 * experts + 2].astype(jnp.int32) for block in (even, odd)]
    place = [0, *far_first]
    counts = jnp.stack([counts[k % 2][place.index(k - k % 2)] for k in range(count)])
    out = struct((tokens, cached + steps, kv_heads, width), bf16)
    keys, values = call(functools.partial(resample_kernel, steps, early), (out, out), [SMEM] + [VMEM] * 6, "resample", 2.2)(
        counts, near, far, cache_keys, cache_values, new_keys, new_values
    )
    returned = [swap(others[n * rows : (n + 1) * rows], k) for n, k in enumerate(far_first)]
    keys, values, *returned = lax.optimization_barrier((keys, values, *returned))
    result = call(functools.partial(total_kernel, len(returned) + 2), struct((rows, main), bf16), [VMEM] * (len(returned) + 3), "total", 0.1)(
        residual, own_block, arrived[:rows], *returned
    )
    layer_out = call(unpack_kernel, struct((steps, tokens, 2 * columns), bf16), [VMEM] * 2, "unpack", 0.5)(result, sibling(result))
    return layer_out, keys.transpose(0, 2, 1, 3), values.transpose(0, 2, 1, 3)


def padded(cells, sides, width):
    for axis, dim in sides:
        count = lax.axis_size(axis)
        ends = count - 1
        head = lax.slice_in_dim(cells, 0, width, axis=dim)
        tail = lax.slice_in_dim(cells, cells.shape[dim] - width, cells.shape[dim], axis=dim)
        cells = jnp.concatenate(
            [
                lax.ppermute(tail, axis, [(i, (i + 1) % count) for i in range(ends)]),
                cells,
                lax.ppermute(head, axis, [((i + 1) % count, i) for i in range(ends)]),
            ],
            axis=dim,
        )
    return cells


def shards(
    hidden_in,
    queries,
    new_keys,
    new_values,
    cache_keys,
    cache_values,
    route_ids,
    route_weights,
    norm_gain,
    gate_weight,
    up_weight,
    down_weight,
    ancestor_counts,
):
    step_count, token_count, query_heads, head_width = queries.shape
    key_heads = cache_keys.shape[1]
    cached = cache_keys.shape[2]
    group_size = query_heads // key_heads
    cache_pair = jnp.stack([cache_keys, cache_values])
    fresh_pair = jnp.transpose(jnp.stack([new_keys, new_values]), (0, 2, 3, 1, 4))
    both_kv = jnp.concatenate([cache_pair, fresh_pair], axis=3)
    length = both_kv.shape[3]
    grouped = queries.reshape(step_count, token_count, key_heads, group_size, head_width)
    scores = jnp.einsum(
        "sphgd,phld->sphgl", grouped, both_kv[0], preferred_element_type=jnp.float32
    ) / math.sqrt(head_width)
    allowed = lax.broadcasted_iota(
        jnp.int32, (step_count, length), 1
    ) <= cached + lax.broadcasted_iota(jnp.int32, (step_count, length), 0)
    scores = jnp.where(allowed[:, None, None, None, :], scores, -1e30)
    exponent = jnp.exp(scores - jnp.max(scores, axis=-1, keepdims=True))
    attn_weights = (exponent / jnp.sum(exponent, axis=-1, keepdims=True)).astype(jnp.bfloat16)
    attended = jnp.einsum(
        "sphgl,phld->sphgd", attn_weights, both_kv[1], preferred_element_type=jnp.float32
    )
    attended = attended.astype(jnp.bfloat16).reshape(
        step_count, token_count, query_heads * head_width
    )
    attended = lax.all_gather(attended, "tensor", axis=2, tiled=True)
    expert_count = lax.axis_size("expert")
    group_count = lax.axis_size("group")
    tensor_count = lax.axis_size("tensor")
    tensor_index = lax.axis_index("tensor")
    expert_local = gate_weight.shape[0]
    experts_all = expert_local * expert_count
    chosen_count = route_ids.shape[2]
    model_width = hidden_in.shape[2]
    column_width = down_weight.shape[2]
    capacity = min(token_count, max(2, 2 * token_count * chosen_count // experts_all))
    pair_count = token_count * chosen_count
    expert_iota = jnp.arange(experts_all, dtype=jnp.int32)
    slot_iota = jnp.arange(capacity, dtype=jnp.int32)
    token_owner = (
        (jnp.arange(pair_count) // chosen_count)[:, None] == jnp.arange(token_count)[None, :]
    ).astype(jnp.float32)
    halves = []
    for step_index in range(step_count):
        residual = hidden_in[step_index].astype(jnp.float32) + attended[step_index].astype(
            jnp.float32
        )
        normed = (
            residual
            * lax.rsqrt(jnp.mean(residual * residual, axis=-1, keepdims=True) + epsilon)
            * norm_gain
        ).astype(jnp.bfloat16)
        chosen = route_ids[step_index].reshape(pair_count)
        route_share = route_weights[step_index] / jnp.sum(
            route_weights[step_index], axis=-1, keepdims=True
        )
        expert_hits = (chosen[:, None] == expert_iota[None, :]).astype(jnp.int32)
        position = jnp.sum((jnp.cumsum(expert_hits, axis=0) - expert_hits) * expert_hits, axis=1)
        slotted = (
            expert_hits[:, :, None]
            * (position[:, None, None] == slot_iota[None, None, :]).astype(jnp.int32)
        ).astype(jnp.float32)
        dispatch = jnp.einsum("rec,rt->ect", slotted, token_owner, precision=highest)
        dispatch = dispatch.reshape(expert_count, expert_local, capacity, token_count).astype(
            jnp.bfloat16
        )
        combine = jnp.einsum(
            "rec,rt,r->tec",
            slotted,
            token_owner,
            route_share.reshape(pair_count),
            precision=highest,
        )
        combine = combine.reshape(token_count, expert_count, expert_local, capacity)
        feature_blocks = normed.reshape(token_count, group_count, model_width // group_count)
        outgoing = jnp.einsum(
            "aict,tgd->agicd", dispatch, feature_blocks, preferred_element_type=jnp.float32
        ).astype(jnp.bfloat16)
        flattened = outgoing.reshape(
            expert_count * group_count, expert_local, capacity, model_width // group_count
        )
        received = lax.all_to_all(
            flattened, ("expert", "group"), split_axis=0, concat_axis=0, tiled=True
        )
        gate_part = jnp.einsum(
            "seki,eif->sekf", received, gate_weight, preferred_element_type=jnp.float32
        ).astype(jnp.bfloat16)
        up_part = jnp.einsum(
            "seki,eif->sekf", received, up_weight, preferred_element_type=jnp.float32
        ).astype(jnp.bfloat16)
        gate_sum = lax.psum(gate_part, "group").astype(jnp.float32)
        up_sum = lax.psum(up_part, "group").astype(jnp.float32)
        hidden = (jax.nn.silu(gate_sum) * up_sum).astype(jnp.bfloat16)
        hidden = lax.all_gather(hidden, "tensor", axis=3, tiled=True)
        answered = jnp.einsum(
            "sekf,efo->seko", hidden, down_weight, preferred_element_type=jnp.float32
        ).astype(jnp.bfloat16)
        returned = lax.all_to_all(
            answered, ("expert", "group"), split_axis=0, concat_axis=0, tiled=True
        )
        returned = returned.reshape(
            expert_count, group_count, expert_local, capacity, column_width
        ).astype(jnp.float32)
        expert_mix = jnp.einsum("taic,agicd->tgd", combine, returned, precision=highest)
        own_columns = lax.dynamic_index_in_dim(
            residual.reshape(token_count, group_count, tensor_count, column_width),
            tensor_index,
            2,
            keepdims=False,
        )
        halves.append((own_columns + expert_mix).astype(jnp.bfloat16))
    stacked = jnp.stack(halves)
    layer_out = lax.all_gather(stacked, "tensor", axis=3, tiled=True).reshape(
        step_count, token_count, model_width
    )
    every_count = lax.all_gather(ancestor_counts, ("expert", "group"), axis=0, tiled=True)
    running = jnp.cumsum(every_count)
    first_index = lax.axis_index(("expert", "group")) * token_count
    own_index = first_index + jnp.arange(token_count, dtype=jnp.int32)
    ancestor = jnp.sum((running[None, :] <= own_index[:, None]).astype(jnp.int32), axis=1)
    widened = padded(both_kv, ((("expert", "group"), 1),), REACH)
    window_index = first_index - REACH + jnp.arange(token_count + 2 * REACH, dtype=jnp.int32)
    selector = (ancestor[:, None] == window_index[None, :]).astype(jnp.bfloat16)
    resampled = jnp.einsum(
        "tw,kwhld->kthld", selector, widened, preferred_element_type=jnp.float32
    ).astype(jnp.bfloat16)
    return (layer_out, resampled[0], resampled[1])


def solution(mesh):
    count = mesh.shape["expert"]
    fast = mesh.shape["group"] == 1 and mesh.shape["tensor"] == 2 and count % 2 == 0 and count & (count - 1) == 0
    in_specs = (
        P(None, ("parts", "expert", "group"), None),
        P(None, ("parts", "expert", "group"), "tensor", None),
        P(None, ("parts", "expert", "group"), "tensor", None),
        P(None, ("parts", "expert", "group"), "tensor", None),
        P(("parts", "expert", "group"), "tensor", None, None),
        P(("parts", "expert", "group"), "tensor", None, None),
        P(None, ("parts", "expert", "group"), None),
        P(None, ("parts", "expert", "group"), None),
        P(),
        P("expert", "group", "tensor"),
        P("expert", "group", "tensor"),
        P("expert", None, ("group", "tensor")),
        P(("parts", "expert", "group")),
    )
    out_specs = (
        P(None, ("parts", "expert", "group"), None),
        P(("parts", "expert", "group"), "tensor", None, None),
        P(("parts", "expert", "group"), "tensor", None, None),
    )
    return jax.shard_map(fast_shards if fast else shards, mesh=mesh, in_specs=in_specs, out_specs=out_specs, check_vma=False)
```

```python
import functools
import math

import jax
import jax.numpy as jnp
from jax import lax
from jax.experimental import pallas as pl
from jax.experimental.pallas import tpu as pltpu
from jax.sharding import PartitionSpec as P

REACH = 2
LANES = 128
f32, bf16 = jnp.float32, jnp.bfloat16

epsilon = 1e-06
highest = lax.Precision.HIGHEST


def dot(a, b, dims=((1,), (0,))):
    return lax.dot_general(a, b, (dims, ((), ())), preferred_element_type=f32)


def iota(shape, dim):
    return lax.broadcasted_iota(jnp.int32, shape, dim)


def packing(steps, tokens, heads):
    rows, per_part = (steps + 1) * tokens, heads // (steps + 1)
    tiles, count = steps * per_part, tokens * steps * heads
    target = iota((tiles * rows, count), 0)
    tile, inner = lax.div(target, rows), lax.rem(target, rows)
    is_extra = inner >= steps * tokens
    step = jnp.where(is_extra, lax.div(tile, per_part), lax.div(inner, tokens))
    token = lax.rem(inner, tokens)
    head = jnp.where(is_extra, tiles + lax.rem(tile, per_part), tile)
    chosen = (token * steps + step) * heads + head == iota((tiles * rows, count), 1)
    return chosen.astype(f32).astype(bf16)


def load_kernel(
    steps, ids_in, weights_in, counts_in, gain_in, hidden_in, q_in, nk_in, nv_in, ck_in, cv_in,
    ids_ref, weights_ref, counts_ref, gain_ref, hidden_ref, q_ref, nk_ref, nv_ref, ck_ref, cv_ref, chosen_ref, near_ref, far_ref, sems,
):
    pairs = (
        (ck_in, ck_ref), (cv_in, cv_ref), (nk_in, nk_ref), (nv_in, nv_ref), (q_in, q_ref), (hidden_in, hidden_ref),
        (gain_in, gain_ref), (ids_in, ids_ref), (weights_in, weights_ref), (counts_in, counts_ref),
    )
    copies = [pltpu.make_async_copy(source, target, sems.at[n]) for n, (source, target) in enumerate(pairs)]
    for copy in copies:
        copy.start()
    tokens, kv_heads, cached, width = ck_ref.shape
    chosen_ref[...] = packing(steps, tokens, q_ref.shape[2])
    for copy in copies:
        copy.wait()

    odd = lax.rem(lax.axis_index("expert"), 2)
    per = REACH * kv_heads

    early = 2 * per + per // 2

    def halo(start, kinds, slot):
        for cache_ref, new_ref in kinds:
            for r in range(REACH):
                for h in range(kv_heads):
                    out_ref, at = (near_ref, slot) if slot < early else (far_ref, slot - early)
                    out_ref[at * cached : (at + 1) * cached, :] = cache_ref[start + r, h]
                    yield from (new_ref[s, start + r, h : h + 1, :].astype(f32) for s in range(steps))
                    slot += 1

    def fill(near, far):
        rows = [*halo(near, (keys, values), 0), *halo(far, (keys, values), 2 * per)]
        for out_ref, own in ((near_ref, rows[: early * steps]), (far_ref, rows[early * steps :])):
            below = out_ref.shape[0] - len(own) // steps * cached
            block = jnp.concatenate(own + [jnp.zeros((below - len(own), width), f32)], axis=0)
            out_ref[out_ref.shape[0] - below :, :] = block.astype(bf16)

    keys, values = (ck_ref, nk_ref), (cv_ref, nv_ref)
    tail = tokens - REACH

    @pl.when(odd == 0)
    def _():
        fill(tail, 0)

    @pl.when(odd == 1)
    def _():
        fill(0, tail)


def weight_kernel(sides, after_ref, *refs):
    sources, targets, token_ref, sems = refs[: len(sides)], refs[len(sides) : -2], refs[-2], refs[-1]
    mine = lax.axis_index("tensor")
    copies = []
    for side, source, target in zip(sides, sources, targets):
        half = target.shape[1]
        place = mine if side == 0 else 1 - mine
        rows = pl.ds(pl.multiple_of(place * half, LANES), half)
        for e in range(source.shape[0]):
            copies.append(pltpu.make_async_copy(source.at[e, rows], target.at[e], sems.at[len(copies)]))
    for copy in copies:
        copy.start()
    for copy in copies:
        copy.wait()
    token_ref[...] = jnp.zeros_like(token_ref)


def attend_kernel(
    steps, experts, ids_ref, weights_ref, counts_ref, gain_ref, hidden_ref, q_ref, nk_ref, nv_ref, ck_ref, cv_ref, chosen_ref,
    send_ref, residual_ref, scores_ref,
):
    tokens, heads, width = q_ref.shape[1:]
    kv_heads, cached = ck_ref.shape[1:3]
    group = heads // kv_heads
    columns = heads * width
    part = columns // (steps + 1)
    main = steps * part
    rows = (steps + 1) * tokens
    base = lax.axis_index("tensor") * columns
    fresh = steps * kv_heads
    fresh_rows = -(-fresh // 16) * 16
    scale = 1.0 / math.sqrt(width)

    q_rows = steps * heads
    row = iota((q_rows, kv_heads * cached), 0)
    col = iota((q_rows, kv_heads * cached), 1)
    own_head = lax.div(lax.rem(row, heads), group) == lax.div(col, cached)
    row = iota((q_rows, fresh_rows), 0)
    col = iota((q_rows, fresh_rows), 1)
    own_new = (
        (lax.div(lax.rem(row, heads), group) == lax.rem(col, kv_heads))
        & (lax.div(col, kv_heads) <= lax.div(row, heads))
        & (col < fresh)
    )
    def with_new(new_ref, p):
        pieces = [new_ref[s, p].astype(f32) for s in range(steps)]
        return jnp.concatenate(pieces + [jnp.zeros((fresh_rows - fresh, width), f32)], axis=0).astype(bf16)

    every = range(tokens)
    q = [jnp.concatenate([q_ref[s, p] for s in range(steps)], axis=0) for p in every]
    old = [dot(q[p], ck_ref[p].reshape(kv_heads * cached, width), ((1,), (1,))) for p in every]
    new = [dot(q[p], with_new(nk_ref, p), ((1,), (1,))) for p in every]
    old = [jnp.where(own_head, x * scale, -1e30) for x in old]
    new = [jnp.where(own_new, x * scale, -1e30) for x in new]
    top = [jnp.maximum(jnp.max(old[p], axis=1, keepdims=True), jnp.max(new[p], axis=1, keepdims=True)) for p in every]
    old = [jnp.exp(old[p] - top[p]) for p in every]
    new = [jnp.exp(new[p] - top[p]) for p in every]
    inverse = [1.0 / (jnp.sum(old[p], axis=1, keepdims=True) + jnp.sum(new[p], axis=1, keepdims=True)) for p in every]
    old = [(old[p] * inverse[p]).astype(bf16) for p in every]
    new = [(new[p] * inverse[p]).astype(bf16) for p in every]
    attended = jnp.concatenate([
        (dot(old[p], cv_ref[p].reshape(kv_heads * cached, width)) + dot(new[p], with_new(nv_ref, p))).astype(bf16) for p in every
    ], axis=0)

    tiles = main // width
    moved = dot(chosen_ref[...], attended)
    for s in range(steps):
        residual_ref[s * tokens : (s + 1) * tokens, :] = hidden_ref[s, :, pl.ds(pl.multiple_of(base, LANES), main)].astype(f32)
        residual_ref[steps * tokens :, s * part : (s + 1) * part] = hidden_ref[
            s, :, pl.ds(pl.multiple_of(base + main, LANES), part)
        ].astype(f32)
    residual = residual_ref[...] + jnp.concatenate([moved[j * rows : (j + 1) * rows] for j in range(tiles)], axis=1)
    residual_ref[...] = residual
    gain_main = gain_ref[:, pl.ds(pl.multiple_of(base, LANES), main)]
    gain_last = gain_ref[:, pl.ds(pl.multiple_of(base + main, LANES), part)]
    in_main = iota((rows, main), 0) < steps * tokens
    gain = jnp.where(in_main, gain_main, jnp.concatenate([gain_last] * steps, axis=1))
    send_ref[:, :main] = (residual * gain).astype(bf16)

    squares = residual * residual
    lane = iota((tokens, LANES), 1)
    for s in range(steps):
        scores_ref[s * rows : (s + 1) * rows, :] = jnp.broadcast_to(
            jnp.sum(squares[:, s * part : (s + 1) * part], axis=1, keepdims=True), (rows, LANES))
    whole = sum(scores_ref[s * rows : (s + 1) * rows, :] for s in range(steps))
    scores_ref[steps * rows :, :] = whole
    pieces = []
    for s in range(steps):
        square_sum = (
            scores_ref[steps * rows + s * tokens : steps * rows + (s + 1) * tokens, :]
            + scores_ref[s * rows + steps * tokens : (s + 1) * rows, :]
        )
        ids, weights = ids_ref[s], weights_ref[s]
        share = weights / jnp.sum(weights, axis=1, keepdims=True)
        value = jnp.zeros((tokens, LANES), f32)
        expert = jnp.where(lane < experts, lane, lane - experts)
        for k in range(ids.shape[1]):
            value = jnp.where(ids[:, k : k + 1] == expert, share[:, k : k + 1], value)
        value = jnp.where(lane < 2 * experts, value, square_sum)
        high = value.astype(bf16).astype(f32)
        low = value - high
        piece = jnp.where((lane < experts) | (lane == 2 * experts), high, low)
        piece = jnp.where(lane < 2 * experts + 2, piece, 0.0)
        if s == 0:
            for p in range(tokens):
                here = (lane == 2 * experts + 2) & (iota((tokens, LANES), 0) == p)
                piece = jnp.where(here, counts_ref[p].astype(f32), piece)
        pieces.append(piece)
    pieces.append(jnp.zeros((tokens, LANES), f32))
    send_ref[:, main:] = jnp.concatenate(pieces, axis=0).astype(bf16)


def unpacked(packed, steps, tokens):
    rows, part = (steps + 1) * tokens, packed.shape[1] // steps
    cube = packed.reshape(packed.shape[0] // rows, rows, packed.shape[1])
    step = lax.div(iota((1, rows, part), 1), tokens)
    last = jnp.zeros((cube.shape[0], rows, part), f32)
    for s in range(steps):
        last = jnp.where(step == s, pltpu.roll(cube[:, :, s * part : (s + 1) * part], rows - (steps - s) * tokens, 1), last)
    return last.reshape(packed.shape[0], part)


def packed(plain, steps, tokens):
    rows, part = (steps + 1) * tokens, plain.shape[1] // (steps + 1)
    main = steps * part
    cube = plain.reshape(plain.shape[0] // rows, rows, plain.shape[1])
    last = cube[:, :, main:]
    extra = jnp.concatenate([pltpu.roll(last, (steps - s) * tokens, 1) for s in range(steps)], axis=2)
    in_main = iota((1, rows, main), 1) < steps * tokens
    return jnp.where(in_main, cube[:, :, :main], extra).reshape(plain.shape[0], main)


def halves(even_ref, odd_ref, at):
    return jnp.concatenate([even_ref[:, at], odd_ref[:, at]], axis=0)


def expert_products(steps, tokens, features, gate_ref, up_ref):
    main = features.shape[1]
    local = gate_ref.shape[0]
    extra = unpacked(features.astype(f32), steps, tokens).astype(bf16)
    return [
        dot(features, ref[e, :main, :]) + dot(extra, ref[e, main:, :]) for ref in (gate_ref, up_ref) for e in range(local)
    ]


def partial_kernel(steps, tokens, after_ref, also_after_ref, even_ref, odd_ref, gate_ref, up_ref, out_ref):
    main = even_ref.shape[1] - LANES
    products = expert_products(steps, tokens, halves(even_ref, odd_ref, slice(0, main)), gate_ref, up_ref)
    for n, product in enumerate(products):
        out_ref[n] = product


def hidden_kernel(steps, tokens, experts, partial_ref, even_ref, odd_ref, even_other_ref, odd_other_ref, gate_ref, up_ref, out_ref):
    main = even_ref.shape[1] - LANES
    total = 2 * even_ref.shape[0]
    rows = (steps + 1) * tokens
    columns = main + main // steps
    local, _, units = gate_ref.shape
    features = halves(even_other_ref, odd_other_ref, slice(0, main))
    products = expert_products(steps, tokens, features, gate_ref, up_ref)
    meta = halves(even_ref, odd_ref, slice(main, None)).astype(f32)
    meta_other = halves(even_other_ref, odd_other_ref, slice(main, None)).astype(f32)
    lane = iota(meta.shape, 1)
    valid = lax.rem(iota((total, 1), 0), rows) < steps * tokens
    in_squares = (lane == 2 * experts) | (lane == 2 * experts + 1)
    square_sum = jnp.sum(jnp.where(in_squares, meta + meta_other, 0.0), axis=1, keepdims=True)
    factor = jnp.where(valid, lax.rsqrt(square_sum / (2 * columns) + epsilon), 0.0)
    first_expert = lax.axis_index("expert") * local
    for e in range(local):
        at = first_expert + e
        share = jnp.sum(jnp.where((lane == at) | (lane == at + experts), meta, 0.0), axis=1, keepdims=True)
        gate = ((partial_ref[e] + products[e]) * factor).astype(bf16).astype(f32)
        up = ((partial_ref[local + e] + products[local + e]) * factor).astype(bf16).astype(f32)
        hidden = gate / (1.0 + jnp.exp(-gate)) * up * share
        out_ref[:, e * units : (e + 1) * units] = hidden.astype(bf16)


def down_kernel(steps, tokens, own_ref, other_ref, down_ref, kept_ref, leaving_ref):
    total, width = own_ref.shape
    local, _, columns = down_ref.shape
    units = width // local
    mine = lax.axis_index("tensor")
    product = 0.0
    for ref, half in ((own_ref, mine), (other_ref, 1 - mine)):
        start = pl.multiple_of(half * units, LANES)
        for e in range(local):
            product += dot(ref[:, e * units : (e + 1) * units], down_ref[e, pl.ds(start, units), :])
    product = packed(product, steps, tokens)
    kept_ref[...] = product[: total // 2]
    leaving_ref[...] = product[total // 2 :].astype(bf16)


def join_kernel(near_ref, rest_ref, out_ref):
    ahead = out_ref.shape[0] - rest_ref.shape[0]
    out_ref[:ahead, :] = near_ref[near_ref.shape[0] - ahead :, :]
    out_ref[ahead:, :] = rest_ref[...]


def resample_kernel(steps, early, counts_ref, near_ref, relay_ref, ck_ref, cv_ref, nk_ref, nv_ref, keys_ref, values_ref):
    tokens, kv_heads, cached, width = ck_ref.shape
    devices = counts_ref.shape[0]
    me = lax.axis_index("expert")
    first = me * tokens
    odd = lax.rem(me, 2)
    per = REACH * kv_heads
    running = jnp.int32(0)
    ancestors = [jnp.int32(0)] * tokens
    for d in range(devices):
        k = jnp.bitwise_xor(me, d)
        for p in range(tokens):
            running = running + counts_ref[k, p]
            for i in range(tokens):
                ancestors[i] = ancestors[i] + (running <= first + i).astype(jnp.int32)

    for i in range(tokens):
        offset = ancestors[i] - first

        @pl.when((offset >= 0) & (offset < tokens))
        def _():
            for out_ref, cache_ref, new_ref in ((keys_ref, ck_ref, nk_ref), (values_ref, cv_ref, nv_ref)):
                out_ref[i, :cached] = jnp.swapaxes(cache_ref[offset], 0, 1)
                for s in range(steps):
                    out_ref[i, cached + s] = new_ref[s, offset]

        def near_rows(slot):
            return slot * cached, early * cached + slot * steps

        def far_rows(slot):
            ahead = early - 2 * per
            if slot < ahead:
                return slot * cached, ahead * cached + (2 * per + slot) * steps
            begin = near_ref.shape[0] - 2 * per * cached
            return begin + (slot - ahead) * cached, begin + (2 * per - ahead) * cached + (slot - ahead) * steps

        def from_halo(ref, rows_of, at):
            for kind, out_ref in enumerate((keys_ref, values_ref)):
                places = [rows_of(kind * per + at * kv_heads + h) for h in range(kv_heads)]
                first_row, first_new = places[0]
                block = ref[first_row : first_row + kv_heads * cached, :].reshape(kv_heads, cached, width)
                out_ref[i, :cached] = jnp.swapaxes(block, 0, 1)
                aligned = first_new // 16 * 16
                fresh = ref[aligned : aligned + 32, :].astype(f32) if aligned + 32 <= ref.shape[0] else ref[ref.shape[0] - 32 :, :].astype(f32)
                aligned = min(aligned, ref.shape[0] - 32)
                for s in range(steps):
                    pair = [fresh[place + s - aligned : place + s - aligned + 1] for _, place in places]
                    out_ref[i, cached + s] = jnp.concatenate(pair, axis=0).astype(bf16)

        left, right = offset < 0, offset >= tokens
        near = (left & (odd == 1)) | (right & (odd == 0))
        far = (left & (odd == 0)) | (right & (odd == 1))
        at = jnp.where(left, offset + REACH, offset - tokens)
        for n in range(REACH):

            @pl.when(near & (at == n))
            def _():
                from_halo(near_ref, near_rows, n)

            @pl.when(far & (at == n))
            def _():
                from_halo(relay_ref, far_rows, n)


def add_kernel(a_ref, b_ref, out_ref):
    out_ref[...] = (a_ref[...] + b_ref[...].astype(f32)).astype(out_ref.dtype)


def total_kernel(count, *refs):
    out_ref = refs[-1]
    value = refs[0][...]
    for ref in refs[1 : count + 1]:
        value = value + ref[...].astype(f32)
    out_ref[...] = value.astype(out_ref.dtype)


def unpack_kernel(own_ref, other_ref, out_ref):
    steps, tokens, model_width = out_ref.shape
    columns = model_width // 2
    main = own_ref.shape[1]
    part = main // steps
    mine = lax.axis_index("tensor")
    for ref, half in ((own_ref, mine), (other_ref, 1 - mine)):
        block = ref[...].astype(f32)
        first = pl.multiple_of(half * columns, LANES)
        last = pl.multiple_of(half * columns + main, LANES)
        for s in range(steps):
            out_ref[s, :, pl.ds(first, main)] = block[s * tokens : (s + 1) * tokens].astype(bf16)
            out_ref[s, :, pl.ds(last, part)] = block[steps * tokens :, s * part : (s + 1) * part].astype(bf16)


VMEM = pl.BlockSpec(memory_space=pltpu.VMEM)
SMEM = pl.BlockSpec(memory_space=pltpu.SMEM)
HBM = pl.BlockSpec(memory_space=pltpu.HBM)


def call(kernel, out, specs, name, microseconds, scratch=(), limit=20):
    outs = jax.tree.map(lambda _: VMEM, out)
    return pl.pallas_call(
        kernel, out_shape=out, in_specs=specs, out_specs=outs, scratch_shapes=scratch, name=name,
        cost_estimate=pl.CostEstimate(flops=0, bytes_accessed=int(microseconds * 3.5e6), transcendentals=0),
        compiler_params=pltpu.CompilerParams(vmem_limit_bytes=limit << 20),
    )


def struct(shape, dtype):
    return jax.ShapeDtypeStruct(shape, dtype)


def in_hbm(value):
    return pltpu.with_memory_space_constraint(value, pltpu.HBM)


def fast_shards(
    hidden_in, queries, new_keys, new_values, cache_keys, cache_values, route_ids, route_weights, norm_gain,
    gate_weight, up_weight, down_weight, ancestor_counts,
):
    steps, tokens, heads, width = queries.shape
    kv_heads, cached = cache_keys.shape[1:3]
    count = lax.axis_size("expert")
    local, _, units = gate_weight.shape
    experts = local * count
    columns = down_weight.shape[2]
    part = columns // (steps + 1)
    main = steps * part
    rows = (steps + 1) * tokens
    per = REACH * kv_heads
    early = 2 * per + per // 2
    square = steps * tokens * heads
    chosen = pltpu.VMEM((square, square), bf16)
    halos = [pltpu.VMEM((slots * cached + -(-slots * steps // 16) * 16, width), bf16) for slots in (early, 4 * per - early)]

    def swap(value, offset):
        return lax.ppermute(value, "expert", [(i, i ^ offset) for i in range(count)])

    def sibling(value):
        return lax.ppermute(value, "tensor", [(0, 1), (1, 0)])

    inputs = (route_ids, route_weights, ancestor_counts, norm_gain.reshape(1, -1), hidden_in, queries, new_keys, new_values, cache_keys, cache_values)
    spaces = [pltpu.SMEM if value is ancestor_counts else pltpu.VMEM for value in inputs]
    loaded = pl.pallas_call(
        functools.partial(load_kernel, steps),
        out_shape=[space(value.shape, value.dtype) for space, value in zip(spaces, inputs)] + [chosen] + halos,
        in_specs=[HBM] * len(inputs), out_specs=[pl.BlockSpec(memory_space=space) for space in spaces] + [VMEM] * 3,
        scratch_shapes=[pltpu.SemaphoreType.DMA((len(inputs),))], name="load",
        compiler_params=pltpu.CompilerParams(vmem_limit_bytes=20 << 20),
    )(*(in_hbm(value) for value in inputs))
    *loaded, near, far = loaded
    near = swap(near, 1)
    new_keys, new_values, cache_keys, cache_values = loaded[6:10]
    send, residual = call(
        functools.partial(attend_kernel, steps, experts),
        (struct((rows, main + LANES), bf16), struct((rows, main), f32)),
        [VMEM, VMEM, SMEM] + [VMEM] * 8, "attend", 2.3, [pltpu.VMEM(((steps + 1) * rows, LANES), f32)],
    )(*loaded)

    far_first = range(count - 2, 0, -2)
    def fetch(after, parts, name):
        half = pltpu.VMEM((local, columns, units), gate_weight.dtype)
        sides = tuple(side for _, side in parts)
        return pl.pallas_call(
            functools.partial(weight_kernel, sides), out_shape=[half] * len(parts) + [pltpu.VMEM((8, LANES), f32)],
            in_specs=[VMEM] + [HBM] * len(parts), out_specs=[VMEM] * (len(parts) + 1),
            scratch_shapes=[pltpu.SemaphoreType.DMA((len(parts) * local,))], name=name,
            cost_estimate=pl.CostEstimate(flops=0, bytes_accessed=7_000_000, transcendentals=0),
            compiler_params=pltpu.CompilerParams(vmem_limit_bytes=16 << 20),
        )(after, *(in_hbm(weight) for weight, _ in parts))

    gate_own, token = fetch(residual, [(gate_weight, 0)], "gate")
    even = jnp.concatenate([send] + [swap(send, k) for k in far_first], axis=0)
    even, near, token = lax.optimization_barrier((even, near, token))
    odd = swap(even, 1)
    even_other = sibling(even)
    gate_other, up_own, up_other, token_up = fetch(even, [(gate_weight, 1), (up_weight, 0), (up_weight, 1)], "rest")
    odd, token_up, far = lax.optimization_barrier((odd, token_up, far))
    relayed = swap(far, 1)
    odd_other = sibling(odd)
    partial = call(
        functools.partial(partial_kernel, steps, tokens), struct((2 * local, count * rows, units), f32), [VMEM] * 6, "partial", 0.01,
    )(token, token_up, even, odd, gate_own, up_own)
    hidden = call(
        functools.partial(hidden_kernel, steps, tokens, experts),
        struct((count * rows, local * units), bf16), [VMEM] * 7, "hidden", 0.01,
    )(partial, even, odd, even_other, odd_other, gate_other, up_other)
    other_hidden = sibling(hidden)
    half = count // 2 * rows

    kept, leaving = call(
        functools.partial(down_kernel, steps, tokens), (struct((half, main), f32), struct((half, main), bf16)), [VMEM] * 3, "down", 0.01,
    )(hidden, other_hidden, down_weight)
    leaving, relayed = lax.optimization_barrier((leaving, relayed))
    arrived = swap(leaving, 1)
    ring = [(i, min(i + 2, count - 1) if i % 2 == 0 else max(i - 2, 0)) for i in range(count) if i != 1]
    joined = struct((near.shape[0] - 2 * per * cached + relayed.shape[0], width), bf16)
    far = lax.ppermute(call(join_kernel, joined, [VMEM] * 2, "join", 0.1)(near, relayed), "expert", ring)
    own_block, others = kept[:rows], call(add_kernel, struct((half - rows, main), bf16), [VMEM] * 2, "add", 0.1)(kept[rows:], arrived[rows:])

    counts = [block.reshape(count // 2, rows, main + LANES)[:, :tokens, main + 2 * experts + 2].astype(jnp.int32) for block in (even, odd)]
    place = [0, *far_first]
    counts = jnp.stack([counts[k % 2][place.index(k - k % 2)] for k in range(count)])
    out = struct((tokens, cached + steps, kv_heads, width), bf16)
    keys, values = call(functools.partial(resample_kernel, steps, early), (out, out), [SMEM] + [VMEM] * 6, "resample", 2.2)(
        counts, near, far, cache_keys, cache_values, new_keys, new_values
    )
    returned = [swap(others[n * rows : (n + 1) * rows], k) for n, k in enumerate(far_first)]
    keys, values, *returned = lax.optimization_barrier((keys, values, *returned))
    result = call(functools.partial(total_kernel, len(returned) + 2), struct((rows, main), bf16), [VMEM] * (len(returned) + 3), "total", 0.1)(
        residual, own_block, arrived[:rows], *returned
    )
    layer_out = call(unpack_kernel, struct((steps, tokens, 2 * columns), bf16), [VMEM] * 2, "unpack", 0.5)(result, sibling(result))
    return layer_out, keys.transpose(0, 2, 1, 3), values.transpose(0, 2, 1, 3)


def padded(cells, sides, width):
    for axis, dim in sides:
        count = lax.axis_size(axis)
        ends = count - 1
        head = lax.slice_in_dim(cells, 0, width, axis=dim)
        tail = lax.slice_in_dim(cells, cells.shape[dim] - width, cells.shape[dim], axis=dim)
        cells = jnp.concatenate(
            [
                lax.ppermute(tail, axis, [(i, (i + 1) % count) for i in range(ends)]),
                cells,
                lax.ppermute(head, axis, [((i + 1) % count, i) for i in range(ends)]),
            ],
            axis=dim,
        )
    return cells


def shards(
    hidden_in,
    queries,
    new_keys,
    new_values,
    cache_keys,
    cache_values,
    route_ids,
    route_weights,
    norm_gain,
    gate_weight,
    up_weight,
    down_weight,
    ancestor_counts,
):
    step_count, token_count, query_heads, head_width = queries.shape
    key_heads = cache_keys.shape[1]
    cached = cache_keys.shape[2]
    group_size = query_heads // key_heads
    cache_pair = jnp.stack([cache_keys, cache_values])
    fresh_pair = jnp.transpose(jnp.stack([new_keys, new_values]), (0, 2, 3, 1, 4))
    both_kv = jnp.concatenate([cache_pair, fresh_pair], axis=3)
    length = both_kv.shape[3]
    grouped = queries.reshape(step_count, token_count, key_heads, group_size, head_width)
    scores = jnp.einsum(
        "sphgd,phld->sphgl", grouped, both_kv[0], preferred_element_type=jnp.float32
    ) / math.sqrt(head_width)
    allowed = lax.broadcasted_iota(
        jnp.int32, (step_count, length), 1
    ) <= cached + lax.broadcasted_iota(jnp.int32, (step_count, length), 0)
    scores = jnp.where(allowed[:, None, None, None, :], scores, -1e30)
    exponent = jnp.exp(scores - jnp.max(scores, axis=-1, keepdims=True))
    attn_weights = (exponent / jnp.sum(exponent, axis=-1, keepdims=True)).astype(jnp.bfloat16)
    attended = jnp.einsum(
        "sphgl,phld->sphgd", attn_weights, both_kv[1], preferred_element_type=jnp.float32
    )
    attended = attended.astype(jnp.bfloat16).reshape(
        step_count, token_count, query_heads * head_width
    )
    attended = lax.all_gather(attended, "tensor", axis=2, tiled=True)
    expert_count = lax.axis_size("expert")
    group_count = lax.axis_size("group")
    tensor_count = lax.axis_size("tensor")
    tensor_index = lax.axis_index("tensor")
    expert_local = gate_weight.shape[0]
    experts_all = expert_local * expert_count
    chosen_count = route_ids.shape[2]
    model_width = hidden_in.shape[2]
    column_width = down_weight.shape[2]
    capacity = min(token_count, max(2, 2 * token_count * chosen_count // experts_all))
    pair_count = token_count * chosen_count
    expert_iota = jnp.arange(experts_all, dtype=jnp.int32)
    slot_iota = jnp.arange(capacity, dtype=jnp.int32)
    token_owner = (
        (jnp.arange(pair_count) // chosen_count)[:, None] == jnp.arange(token_count)[None, :]
    ).astype(jnp.float32)
    halves = []
    for step_index in range(step_count):
        residual = hidden_in[step_index].astype(jnp.float32) + attended[step_index].astype(
            jnp.float32
        )
        normed = (
            residual
            * lax.rsqrt(jnp.mean(residual * residual, axis=-1, keepdims=True) + epsilon)
            * norm_gain
        ).astype(jnp.bfloat16)
        chosen = route_ids[step_index].reshape(pair_count)
        route_share = route_weights[step_index] / jnp.sum(
            route_weights[step_index], axis=-1, keepdims=True
        )
        expert_hits = (chosen[:, None] == expert_iota[None, :]).astype(jnp.int32)
        position = jnp.sum((jnp.cumsum(expert_hits, axis=0) - expert_hits) * expert_hits, axis=1)
        slotted = (
            expert_hits[:, :, None]
            * (position[:, None, None] == slot_iota[None, None, :]).astype(jnp.int32)
        ).astype(jnp.float32)
        dispatch = jnp.einsum("rec,rt->ect", slotted, token_owner, precision=highest)
        dispatch = dispatch.reshape(expert_count, expert_local, capacity, token_count).astype(
            jnp.bfloat16
        )
        combine = jnp.einsum(
            "rec,rt,r->tec",
            slotted,
            token_owner,
            route_share.reshape(pair_count),
            precision=highest,
        )
        combine = combine.reshape(token_count, expert_count, expert_local, capacity)
        feature_blocks = normed.reshape(token_count, group_count, model_width // group_count)
        outgoing = jnp.einsum(
            "aict,tgd->agicd", dispatch, feature_blocks, preferred_element_type=jnp.float32
        ).astype(jnp.bfloat16)
        flattened = outgoing.reshape(
            expert_count * group_count, expert_local, capacity, model_width // group_count
        )
        received = lax.all_to_all(
            flattened, ("expert", "group"), split_axis=0, concat_axis=0, tiled=True
        )
        gate_part = jnp.einsum(
            "seki,eif->sekf", received, gate_weight, preferred_element_type=jnp.float32
        ).astype(jnp.bfloat16)
        up_part = jnp.einsum(
            "seki,eif->sekf", received, up_weight, preferred_element_type=jnp.float32
        ).astype(jnp.bfloat16)
        gate_sum = lax.psum(gate_part, "group").astype(jnp.float32)
        up_sum = lax.psum(up_part, "group").astype(jnp.float32)
        hidden = (jax.nn.silu(gate_sum) * up_sum).astype(jnp.bfloat16)
        hidden = lax.all_gather(hidden, "tensor", axis=3, tiled=True)
        answered = jnp.einsum(
            "sekf,efo->seko", hidden, down_weight, preferred_element_type=jnp.float32
        ).astype(jnp.bfloat16)
        returned = lax.all_to_all(
            answered, ("expert", "group"), split_axis=0, concat_axis=0, tiled=True
        )
        returned = returned.reshape(
            expert_count, group_count, expert_local, capacity, column_width
        ).astype(jnp.float32)
        expert_mix = jnp.einsum("taic,agicd->tgd", combine, returned, precision=highest)
        own_columns = lax.dynamic_index_in_dim(
            residual.reshape(token_count, group_count, tensor_count, column_width),
            tensor_index,
            2,
            keepdims=False,
        )
        halves.append((own_columns + expert_mix).astype(jnp.bfloat16))
    stacked = jnp.stack(halves)
    layer_out = lax.all_gather(stacked, "tensor", axis=3, tiled=True).reshape(
        step_count, token_count, model_width
    )
    every_count = lax.all_gather(ancestor_counts, ("expert", "group"), axis=0, tiled=True)
    running = jnp.cumsum(every_count)
    first_index = lax.axis_index(("expert", "group")) * token_count
    own_index = first_index + jnp.arange(token_count, dtype=jnp.int32)
    ancestor = jnp.sum((running[None, :] <= own_index[:, None]).astype(jnp.int32), axis=1)
    widened = padded(both_kv, ((("expert", "group"), 1),), REACH)
    window_index = first_index - REACH + jnp.arange(token_count + 2 * REACH, dtype=jnp.int32)
    selector = (ancestor[:, None] == window_index[None, :]).astype(jnp.bfloat16)
    resampled = jnp.einsum(
        "tw,kwhld->kthld", selector, widened, preferred_element_type=jnp.float32
    ).astype(jnp.bfloat16)
    return (layer_out, resampled[0], resampled[1])


def solution(mesh):
    count = mesh.shape["expert"]
    fast = mesh.shape["group"] == 1 and mesh.shape["tensor"] == 2 and count % 2 == 0 and count & (count - 1) == 0
    in_specs = (
        P(None, ("parts", "expert", "group"), None),
        P(None, ("parts", "expert", "group"), "tensor", None),
        P(None, ("parts", "expert", "group"), "tensor", None),
        P(None, ("parts", "expert", "group"), "tensor", None),
        P(("parts", "expert", "group"), "tensor", None, None),
        P(("parts", "expert", "group"), "tensor", None, None),
        P(None, ("parts", "expert", "group"), None),
        P(None, ("parts", "expert", "group"), None),
        P(),
        P("expert", "group", "tensor"),
        P("expert", "group", "tensor"),
        P("expert", None, ("group", "tensor")),
        P(("parts", "expert", "group")),
    )
    out_specs = (
        P(None, ("parts", "expert", "group"), None),
        P(("parts", "expert", "group"), "tensor", None, None),
        P(("parts", "expert", "group"), "tensor", None, None),
    )
    return jax.shard_map(fast_shards if fast else shards, mesh=mesh, in_specs=in_specs, out_specs=out_specs, check_vma=False)
```

```python
import functools
import math

import jax
import jax.numpy as jnp
from jax import lax
from jax.experimental import pallas as pl
from jax.experimental.pallas import tpu as pltpu
from jax.sharding import PartitionSpec as P

REACH = 2
LANES = 128
f32, bf16 = jnp.float32, jnp.bfloat16

epsilon = 1e-06
highest = lax.Precision.HIGHEST


def dot(a, b, dims=((1,), (0,))):
    return lax.dot_general(a, b, (dims, ((), ())), preferred_element_type=f32)


def iota(shape, dim):
    return lax.broadcasted_iota(jnp.int32, shape, dim)


def packing(steps, tokens, heads):
    rows, per_part = (steps + 1) * tokens, heads // (steps + 1)
    tiles, count = steps * per_part, tokens * steps * heads
    target = iota((tiles * rows, count), 0)
    tile, inner = lax.div(target, rows), lax.rem(target, rows)
    is_extra = inner >= steps * tokens
    step = jnp.where(is_extra, lax.div(tile, per_part), lax.div(inner, tokens))
    token = lax.rem(inner, tokens)
    head = jnp.where(is_extra, tiles + lax.rem(tile, per_part), tile)
    chosen = (token * steps + step) * heads + head == iota((tiles * rows, count), 1)
    return chosen.astype(f32).astype(bf16)


def load_kernel(
    steps, ids_in, weights_in, counts_in, gain_in, hidden_in, q_in, nk_in, nv_in, ck_in, cv_in,
    ids_ref, weights_ref, counts_ref, gain_ref, hidden_ref, q_ref, nk_ref, nv_ref, ck_ref, cv_ref, chosen_ref, near_ref, far_ref, sems,
):
    pairs = (
        (ck_in, ck_ref), (cv_in, cv_ref), (nk_in, nk_ref), (nv_in, nv_ref), (q_in, q_ref), (hidden_in, hidden_ref),
        (gain_in, gain_ref), (ids_in, ids_ref), (weights_in, weights_ref), (counts_in, counts_ref),
    )
    copies = [pltpu.make_async_copy(source, target, sems.at[n]) for n, (source, target) in enumerate(pairs)]
    for copy in copies:
        copy.start()
    tokens, kv_heads, cached, width = ck_ref.shape
    chosen_ref[...] = packing(steps, tokens, q_ref.shape[2])
    for copy in copies[:4]:
        copy.wait()

    odd = lax.rem(lax.axis_index("expert"), 2)
    per = REACH * kv_heads

    early = 2 * per + per // 2

    def halo(start, kinds, slot):
        for cache_ref, new_ref in kinds:
            for r in range(REACH):
                for h in range(kv_heads):
                    out_ref, at = (near_ref, slot) if slot < early else (far_ref, slot - early)
                    out_ref[at * cached : (at + 1) * cached, :] = cache_ref[start + r, h]
                    yield from (new_ref[s, start + r, h : h + 1, :].astype(f32) for s in range(steps))
                    slot += 1

    def fill(near, far):
        rows = [*halo(near, (keys, values), 0), *halo(far, (keys, values), 2 * per)]
        for out_ref, own in ((near_ref, rows[: early * steps]), (far_ref, rows[early * steps :])):
            below = out_ref.shape[0] - len(own) // steps * cached
            block = jnp.concatenate(own + [jnp.zeros((below - len(own), width), f32)], axis=0)
            out_ref[out_ref.shape[0] - below :, :] = block.astype(bf16)

    keys, values = (ck_ref, nk_ref), (cv_ref, nv_ref)
    tail = tokens - REACH

    @pl.when(odd == 0)
    def _():
        fill(tail, 0)

    @pl.when(odd == 1)
    def _():
        fill(0, tail)

    for copy in copies[4:]:
        copy.wait()


def weight_kernel(after_ref, source, own_ref, other_ref, token_ref, sems):
    half = own_ref.shape[1]
    mine = lax.axis_index("tensor")
    copies = []
    for target, place in ((own_ref, mine), (other_ref, 1 - mine)):
        rows = pl.ds(pl.multiple_of(place * half, LANES), half)
        for e in range(source.shape[0]):
            copies.append(pltpu.make_async_copy(source.at[e, rows], target.at[e], sems.at[len(copies)]))
    for copy in copies:
        copy.start()
    for copy in copies:
        copy.wait()
    token_ref[...] = jnp.zeros_like(token_ref)


def attend_kernel(
    steps, experts, ids_ref, weights_ref, counts_ref, gain_ref, hidden_ref, q_ref, nk_ref, nv_ref, ck_ref, cv_ref, chosen_ref,
    send_ref, residual_ref, scores_ref,
):
    tokens, heads, width = q_ref.shape[1:]
    kv_heads, cached = ck_ref.shape[1:3]
    group = heads // kv_heads
    columns = heads * width
    part = columns // (steps + 1)
    main = steps * part
    rows = (steps + 1) * tokens
    base = lax.axis_index("tensor") * columns
    fresh = steps * kv_heads
    fresh_rows = -(-fresh // 16) * 16
    scale = 1.0 / math.sqrt(width)

    q_rows = steps * heads
    row = iota((q_rows, kv_heads * cached), 0)
    col = iota((q_rows, kv_heads * cached), 1)
    own_head = lax.div(lax.rem(row, heads), group) == lax.div(col, cached)
    row = iota((q_rows, fresh_rows), 0)
    col = iota((q_rows, fresh_rows), 1)
    own_new = (
        (lax.div(lax.rem(row, heads), group) == lax.rem(col, kv_heads))
        & (lax.div(col, kv_heads) <= lax.div(row, heads))
        & (col < fresh)
    )
    def with_new(new_ref, p):
        pieces = [new_ref[s, p].astype(f32) for s in range(steps)]
        return jnp.concatenate(pieces + [jnp.zeros((fresh_rows - fresh, width), f32)], axis=0).astype(bf16)

    every = range(tokens)
    q = [jnp.concatenate([q_ref[s, p] for s in range(steps)], axis=0) for p in every]
    old = [dot(q[p], ck_ref[p].reshape(kv_heads * cached, width), ((1,), (1,))) for p in every]
    new = [dot(q[p], with_new(nk_ref, p), ((1,), (1,))) for p in every]
    old = [jnp.where(own_head, x * scale, -1e30) for x in old]
    new = [jnp.where(own_new, x * scale, -1e30) for x in new]
    top = [jnp.maximum(jnp.max(old[p], axis=1, keepdims=True), jnp.max(new[p], axis=1, keepdims=True)) for p in every]
    old = [jnp.exp(old[p] - top[p]) for p in every]
    new = [jnp.exp(new[p] - top[p]) for p in every]
    inverse = [1.0 / (jnp.sum(old[p], axis=1, keepdims=True) + jnp.sum(new[p], axis=1, keepdims=True)) for p in every]
    old = [(old[p] * inverse[p]).astype(bf16) for p in every]
    new = [(new[p] * inverse[p]).astype(bf16) for p in every]
    attended = jnp.concatenate([
        (dot(old[p], cv_ref[p].reshape(kv_heads * cached, width)) + dot(new[p], with_new(nv_ref, p))).astype(bf16) for p in every
    ], axis=0)

    tiles = main // width
    moved = dot(chosen_ref[...], attended)
    for s in range(steps):
        residual_ref[s * tokens : (s + 1) * tokens, :] = hidden_ref[s, :, pl.ds(pl.multiple_of(base, LANES), main)].astype(f32)
        residual_ref[steps * tokens :, s * part : (s + 1) * part] = hidden_ref[
            s, :, pl.ds(pl.multiple_of(base + main, LANES), part)
        ].astype(f32)
    residual = residual_ref[...] + jnp.concatenate([moved[j * rows : (j + 1) * rows] for j in range(tiles)], axis=1)
    residual_ref[...] = residual
    gain_main = gain_ref[:, pl.ds(pl.multiple_of(base, LANES), main)]
    gain_last = gain_ref[:, pl.ds(pl.multiple_of(base + main, LANES), part)]
    in_main = iota((rows, main), 0) < steps * tokens
    gain = jnp.where(in_main, gain_main, jnp.concatenate([gain_last] * steps, axis=1))
    send_ref[:, :main] = (residual * gain).astype(bf16)

    squares = residual * residual
    lane = iota((tokens, LANES), 1)
    for s in range(steps):
        scores_ref[s * rows : (s + 1) * rows, :] = jnp.broadcast_to(
            jnp.sum(squares[:, s * part : (s + 1) * part], axis=1, keepdims=True), (rows, LANES))
    whole = sum(scores_ref[s * rows : (s + 1) * rows, :] for s in range(steps))
    scores_ref[steps * rows :, :] = whole
    pieces = []
    for s in range(steps):
        square_sum = (
            scores_ref[steps * rows + s * tokens : steps * rows + (s + 1) * tokens, :]
            + scores_ref[s * rows + steps * tokens : (s + 1) * rows, :]
        )
        ids, weights = ids_ref[s], weights_ref[s]
        share = weights / jnp.sum(weights, axis=1, keepdims=True)
        value = jnp.zeros((tokens, LANES), f32)
        expert = jnp.where(lane < experts, lane, lane - experts)
        for k in range(ids.shape[1]):
            value = jnp.where(ids[:, k : k + 1] == expert, share[:, k : k + 1], value)
        value = jnp.where(lane < 2 * experts, value, square_sum)
        high = value.astype(bf16).astype(f32)
        low = value - high
        piece = jnp.where((lane < experts) | (lane == 2 * experts), high, low)
        piece = jnp.where(lane < 2 * experts + 2, piece, 0.0)
        if s == 0:
            for p in range(tokens):
                here = (lane == 2 * experts + 2) & (iota((tokens, LANES), 0) == p)
                piece = jnp.where(here, counts_ref[p].astype(f32), piece)
        pieces.append(piece)
    pieces.append(jnp.zeros((tokens, LANES), f32))
    send_ref[:, main:] = jnp.concatenate(pieces, axis=0).astype(bf16)


def unpacked(packed, steps, tokens):
    rows, part = (steps + 1) * tokens, packed.shape[1] // steps
    cube = packed.reshape(packed.shape[0] // rows, rows, packed.shape[1])
    step = lax.div(iota((1, rows, part), 1), tokens)
    last = jnp.zeros((cube.shape[0], rows, part), f32)
    for s in range(steps):
        last = jnp.where(step == s, pltpu.roll(cube[:, :, s * part : (s + 1) * part], rows - (steps - s) * tokens, 1), last)
    return last.reshape(packed.shape[0], part)


def packed(plain, steps, tokens):
    rows, part = (steps + 1) * tokens, plain.shape[1] // (steps + 1)
    main = steps * part
    cube = plain.reshape(plain.shape[0] // rows, rows, plain.shape[1])
    last = cube[:, :, main:]
    extra = jnp.concatenate([pltpu.roll(last, (steps - s) * tokens, 1) for s in range(steps)], axis=2)
    in_main = iota((1, rows, main), 1) < steps * tokens
    return jnp.where(in_main, cube[:, :, :main], extra).reshape(plain.shape[0], main)


def halves(even_ref, odd_ref, at):
    return jnp.concatenate([even_ref[:, at], odd_ref[:, at]], axis=0)


def expert_products(steps, tokens, features, gate_ref, up_ref):
    main = features.shape[1]
    local = gate_ref.shape[0]
    extra = unpacked(features.astype(f32), steps, tokens).astype(bf16)
    return [
        dot(features, ref[e, :main, :]) + dot(extra, ref[e, main:, :]) for ref in (gate_ref, up_ref) for e in range(local)
    ]


def partial_kernel(steps, tokens, after_ref, also_after_ref, even_ref, odd_ref, gate_ref, up_ref, out_ref):
    main = even_ref.shape[1] - LANES
    products = expert_products(steps, tokens, halves(even_ref, odd_ref, slice(0, main)), gate_ref, up_ref)
    for n, product in enumerate(products):
        out_ref[n] = product


def hidden_kernel(steps, tokens, experts, partial_ref, even_ref, odd_ref, even_other_ref, odd_other_ref, gate_ref, up_ref, out_ref):
    main = even_ref.shape[1] - LANES
    total = 2 * even_ref.shape[0]
    rows = (steps + 1) * tokens
    columns = main + main // steps
    local, _, units = gate_ref.shape
    features = halves(even_other_ref, odd_other_ref, slice(0, main))
    products = expert_products(steps, tokens, features, gate_ref, up_ref)
    meta = halves(even_ref, odd_ref, slice(main, None)).astype(f32)
    meta_other = halves(even_other_ref, odd_other_ref, slice(main, None)).astype(f32)
    lane = iota(meta.shape, 1)
    valid = lax.rem(iota((total, 1), 0), rows) < steps * tokens
    in_squares = (lane == 2 * experts) | (lane == 2 * experts + 1)
    square_sum = jnp.sum(jnp.where(in_squares, meta + meta_other, 0.0), axis=1, keepdims=True)
    factor = jnp.where(valid, lax.rsqrt(square_sum / (2 * columns) + epsilon), 0.0)
    first_expert = lax.axis_index("expert") * local
    for e in range(local):
        at = first_expert + e
        share = jnp.sum(jnp.where((lane == at) | (lane == at + experts), meta, 0.0), axis=1, keepdims=True)
        gate = ((partial_ref[e] + products[e]) * factor).astype(bf16).astype(f32)
        up = ((partial_ref[local + e] + products[local + e]) * factor).astype(bf16).astype(f32)
        hidden = gate / (1.0 + jnp.exp(-gate)) * up * share
        out_ref[:, e * units : (e + 1) * units] = hidden.astype(bf16)


def down_kernel(steps, tokens, own_ref, other_ref, down_ref, kept_ref, leaving_ref):
    total, width = own_ref.shape
    local, _, columns = down_ref.shape
    units = width // local
    mine = lax.axis_index("tensor")
    product = 0.0
    for ref, half in ((own_ref, mine), (other_ref, 1 - mine)):
        start = pl.multiple_of(half * units, LANES)
        for e in range(local):
            product += dot(ref[:, e * units : (e + 1) * units], down_ref[e, pl.ds(start, units), :])
    product = packed(product, steps, tokens)
    kept_ref[...] = product[: total // 2]
    leaving_ref[...] = product[total // 2 :].astype(bf16)


def join_kernel(near_ref, rest_ref, out_ref):
    ahead = out_ref.shape[0] - rest_ref.shape[0]
    out_ref[:ahead, :] = near_ref[near_ref.shape[0] - ahead :, :]
    out_ref[ahead:, :] = rest_ref[...]


def resample_kernel(steps, early, counts_ref, near_ref, relay_ref, ck_ref, cv_ref, nk_ref, nv_ref, keys_ref, values_ref):
    tokens, kv_heads, cached, width = ck_ref.shape
    devices = counts_ref.shape[0]
    me = lax.axis_index("expert")
    first = me * tokens
    odd = lax.rem(me, 2)
    per = REACH * kv_heads
    running = jnp.int32(0)
    ancestors = [jnp.int32(0)] * tokens
    for d in range(devices):
        k = jnp.bitwise_xor(me, d)
        for p in range(tokens):
            running = running + counts_ref[k, p]
            for i in range(tokens):
                ancestors[i] = ancestors[i] + (running <= first + i).astype(jnp.int32)

    for i in range(tokens):
        offset = ancestors[i] - first

        @pl.when((offset >= 0) & (offset < tokens))
        def _():
            for out_ref, cache_ref, new_ref in ((keys_ref, ck_ref, nk_ref), (values_ref, cv_ref, nv_ref)):
                out_ref[i, :cached] = jnp.swapaxes(cache_ref[offset], 0, 1)
                for s in range(steps):
                    out_ref[i, cached + s] = new_ref[s, offset]

        def near_rows(slot):
            return slot * cached, early * cached + slot * steps

        def far_rows(slot):
            ahead = early - 2 * per
            if slot < ahead:
                return slot * cached, ahead * cached + (2 * per + slot) * steps
            begin = near_ref.shape[0] - 2 * per * cached
            return begin + (slot - ahead) * cached, begin + (2 * per - ahead) * cached + (slot - ahead) * steps

        def from_halo(ref, rows_of, at):
            for kind, out_ref in enumerate((keys_ref, values_ref)):
                places = [rows_of(kind * per + at * kv_heads + h) for h in range(kv_heads)]
                first_row, first_new = places[0]
                block = ref[first_row : first_row + kv_heads * cached, :].reshape(kv_heads, cached, width)
                out_ref[i, :cached] = jnp.swapaxes(block, 0, 1)
                aligned = first_new // 16 * 16
                fresh = ref[aligned : aligned + 32, :].astype(f32) if aligned + 32 <= ref.shape[0] else ref[ref.shape[0] - 32 :, :].astype(f32)
                aligned = min(aligned, ref.shape[0] - 32)
                for s in range(steps):
                    pair = [fresh[place + s - aligned : place + s - aligned + 1] for _, place in places]
                    out_ref[i, cached + s] = jnp.concatenate(pair, axis=0).astype(bf16)

        left, right = offset < 0, offset >= tokens
        near = (left & (odd == 1)) | (right & (odd == 0))
        far = (left & (odd == 0)) | (right & (odd == 1))
        at = jnp.where(left, offset + REACH, offset - tokens)
        for n in range(REACH):

            @pl.when(near & (at == n))
            def _():
                from_halo(near_ref, near_rows, n)

            @pl.when(far & (at == n))
            def _():
                from_halo(relay_ref, far_rows, n)


def add_kernel(a_ref, b_ref, out_ref):
    out_ref[...] = (a_ref[...] + b_ref[...].astype(f32)).astype(out_ref.dtype)


def total_kernel(count, *refs):
    out_ref = refs[-1]
    value = refs[0][...]
    for ref in refs[1 : count + 1]:
        value = value + ref[...].astype(f32)
    out_ref[...] = value.astype(out_ref.dtype)


def unpack_kernel(own_ref, other_ref, out_ref):
    steps, tokens, model_width = out_ref.shape
    columns = model_width // 2
    main = own_ref.shape[1]
    part = main // steps
    mine = lax.axis_index("tensor")
    for ref, half in ((own_ref, mine), (other_ref, 1 - mine)):
        block = ref[...].astype(f32)
        first = pl.multiple_of(half * columns, LANES)
        last = pl.multiple_of(half * columns + main, LANES)
        for s in range(steps):
            out_ref[s, :, pl.ds(first, main)] = block[s * tokens : (s + 1) * tokens].astype(bf16)
            out_ref[s, :, pl.ds(last, part)] = block[steps * tokens :, s * part : (s + 1) * part].astype(bf16)


VMEM = pl.BlockSpec(memory_space=pltpu.VMEM)
SMEM = pl.BlockSpec(memory_space=pltpu.SMEM)
HBM = pl.BlockSpec(memory_space=pltpu.HBM)


def call(kernel, out, specs, name, microseconds, scratch=(), limit=20):
    outs = jax.tree.map(lambda _: VMEM, out)
    return pl.pallas_call(
        kernel, out_shape=out, in_specs=specs, out_specs=outs, scratch_shapes=scratch, name=name,
        cost_estimate=pl.CostEstimate(flops=0, bytes_accessed=int(microseconds * 3.5e6), transcendentals=0),
        compiler_params=pltpu.CompilerParams(vmem_limit_bytes=limit << 20),
    )


def struct(shape, dtype):
    return jax.ShapeDtypeStruct(shape, dtype)


def in_hbm(value):
    return pltpu.with_memory_space_constraint(value, pltpu.HBM)


def fast_shards(
    hidden_in, queries, new_keys, new_values, cache_keys, cache_values, route_ids, route_weights, norm_gain,
    gate_weight, up_weight, down_weight, ancestor_counts,
):
    steps, tokens, heads, width = queries.shape
    kv_heads, cached = cache_keys.shape[1:3]
    count = lax.axis_size("expert")
    local, _, units = gate_weight.shape
    experts = local * count
    columns = down_weight.shape[2]
    part = columns // (steps + 1)
    main = steps * part
    rows = (steps + 1) * tokens
    per = REACH * kv_heads
    early = 2 * per + per // 2
    square = steps * tokens * heads
    chosen = pltpu.VMEM((square, square), bf16)
    halos = [pltpu.VMEM((slots * cached + -(-slots * steps // 16) * 16, width), bf16) for slots in (early, 4 * per - early)]

    def swap(value, offset):
        return lax.ppermute(value, "expert", [(i, i ^ offset) for i in range(count)])

    def sibling(value):
        return lax.ppermute(value, "tensor", [(0, 1), (1, 0)])

    inputs = (route_ids, route_weights, ancestor_counts, norm_gain.reshape(1, -1), hidden_in, queries, new_keys, new_values, cache_keys, cache_values)
    spaces = [pltpu.SMEM if value is ancestor_counts else pltpu.VMEM for value in inputs]
    loaded = pl.pallas_call(
        functools.partial(load_kernel, steps),
        out_shape=[space(value.shape, value.dtype) for space, value in zip(spaces, inputs)] + [chosen] + halos,
        in_specs=[HBM] * len(inputs), out_specs=[pl.BlockSpec(memory_space=space) for space in spaces] + [VMEM] * 3,
        scratch_shapes=[pltpu.SemaphoreType.DMA((len(inputs),))], name="load",
        compiler_params=pltpu.CompilerParams(vmem_limit_bytes=20 << 20),
    )(*(in_hbm(value) for value in inputs))
    *loaded, near, far = loaded
    near = swap(near, 1)
    new_keys, new_values, cache_keys, cache_values = loaded[6:10]
    send, residual = call(
        functools.partial(attend_kernel, steps, experts),
        (struct((rows, main + LANES), bf16), struct((rows, main), f32)),
        [VMEM, VMEM, SMEM] + [VMEM] * 8, "attend", 2.3, [pltpu.VMEM(((steps + 1) * rows, LANES), f32)],
    )(*loaded)

    far_first = range(count - 2, 0, -2)
    def fetch(after, weight, name):
        half = pltpu.VMEM((local, columns, units), weight.dtype)
        return pl.pallas_call(
            weight_kernel, out_shape=[half, half, pltpu.VMEM((8, LANES), f32)],
            in_specs=[VMEM, HBM], out_specs=[VMEM] * 3, scratch_shapes=[pltpu.SemaphoreType.DMA((2 * local,))], name=name,
            cost_estimate=pl.CostEstimate(flops=0, bytes_accessed=7_000_000, transcendentals=0),
            compiler_params=pltpu.CompilerParams(vmem_limit_bytes=16 << 20),
        )(after, in_hbm(weight))

    gate_own, gate_other, token = fetch(residual, gate_weight, "gate")
    even = jnp.concatenate([send] + [swap(send, k) for k in far_first], axis=0)
    even, near, token = lax.optimization_barrier((even, near, token))
    odd = swap(even, 1)
    even_other = sibling(even)
    up_own, up_other, token_up = fetch(even, up_weight, "up")
    odd, token_up, far = lax.optimization_barrier((odd, token_up, far))
    relayed = swap(far, 1)
    odd_other = sibling(odd)
    partial = call(
        functools.partial(partial_kernel, steps, tokens), struct((2 * local, count * rows, units), f32), [VMEM] * 6, "partial", 0.01,
    )(token, token_up, even, odd, gate_own, up_own)
    hidden = call(
        functools.partial(hidden_kernel, steps, tokens, experts),
        struct((count * rows, local * units), bf16), [VMEM] * 7, "hidden", 0.01,
    )(partial, even, odd, even_other, odd_other, gate_other, up_other)
    other_hidden = sibling(hidden)
    half = count // 2 * rows

    kept, leaving = call(
        functools.partial(down_kernel, steps, tokens), (struct((half, main), f32), struct((half, main), bf16)), [VMEM] * 3, "down", 0.01,
    )(hidden, other_hidden, down_weight)
    leaving, relayed = lax.optimization_barrier((leaving, relayed))
    arrived = swap(leaving, 1)
    ring = [(i, i + 2 if i % 2 == 0 else i - 2) for i in range(count) if (i < count - 2 if i % 2 == 0 else i > 1)]
    joined = struct((near.shape[0] - 2 * per * cached + relayed.shape[0], width), bf16)
    far = lax.ppermute(call(join_kernel, joined, [VMEM] * 2, "join", 0.1)(near, relayed), "expert", ring)
    own_block, others = kept[:rows], call(add_kernel, struct((half - rows, main), bf16), [VMEM] * 2, "add", 0.1)(kept[rows:], arrived[rows:])

    counts = [block.reshape(count // 2, rows, main + LANES)[:, :tokens, main + 2 * experts + 2].astype(jnp.int32) for block in (even, odd)]
    place = [0, *far_first]
    counts = jnp.stack([counts[k % 2][place.index(k - k % 2)] for k in range(count)])
    out = struct((tokens, cached + steps, kv_heads, width), bf16)
    keys, values = call(functools.partial(resample_kernel, steps, early), (out, out), [SMEM] + [VMEM] * 6, "resample", 2.2)(
        counts, near, far, cache_keys, cache_values, new_keys, new_values
    )
    returned = [swap(others[n * rows : (n + 1) * rows], k) for n, k in enumerate(far_first)]
    keys, values, *returned = lax.optimization_barrier((keys, values, *returned))
    result = call(functools.partial(total_kernel, len(returned) + 2), struct((rows, main), bf16), [VMEM] * (len(returned) + 3), "total", 0.1)(
        residual, own_block, arrived[:rows], *returned
    )
    layer_out = call(unpack_kernel, struct((steps, tokens, 2 * columns), bf16), [VMEM] * 2, "unpack", 0.5)(result, sibling(result))
    return layer_out, keys.transpose(0, 2, 1, 3), values.transpose(0, 2, 1, 3)


def padded(cells, sides, width):
    for axis, dim in sides:
        count = lax.axis_size(axis)
        ends = count - 1
        head = lax.slice_in_dim(cells, 0, width, axis=dim)
        tail = lax.slice_in_dim(cells, cells.shape[dim] - width, cells.shape[dim], axis=dim)
        cells = jnp.concatenate(
            [
                lax.ppermute(tail, axis, [(i, (i + 1) % count) for i in range(ends)]),
                cells,
                lax.ppermute(head, axis, [((i + 1) % count, i) for i in range(ends)]),
            ],
            axis=dim,
        )
    return cells


def shards(
    hidden_in,
    queries,
    new_keys,
    new_values,
    cache_keys,
    cache_values,
    route_ids,
    route_weights,
    norm_gain,
    gate_weight,
    up_weight,
    down_weight,
    ancestor_counts,
):
    step_count, token_count, query_heads, head_width = queries.shape
    key_heads = cache_keys.shape[1]
    cached = cache_keys.shape[2]
    group_size = query_heads // key_heads
    cache_pair = jnp.stack([cache_keys, cache_values])
    fresh_pair = jnp.transpose(jnp.stack([new_keys, new_values]), (0, 2, 3, 1, 4))
    both_kv = jnp.concatenate([cache_pair, fresh_pair], axis=3)
    length = both_kv.shape[3]
    grouped = queries.reshape(step_count, token_count, key_heads, group_size, head_width)
    scores = jnp.einsum(
        "sphgd,phld->sphgl", grouped, both_kv[0], preferred_element_type=jnp.float32
    ) / math.sqrt(head_width)
    allowed = lax.broadcasted_iota(
        jnp.int32, (step_count, length), 1
    ) <= cached + lax.broadcasted_iota(jnp.int32, (step_count, length), 0)
    scores = jnp.where(allowed[:, None, None, None, :], scores, -1e30)
    exponent = jnp.exp(scores - jnp.max(scores, axis=-1, keepdims=True))
    attn_weights = (exponent / jnp.sum(exponent, axis=-1, keepdims=True)).astype(jnp.bfloat16)
    attended = jnp.einsum(
        "sphgl,phld->sphgd", attn_weights, both_kv[1], preferred_element_type=jnp.float32
    )
    attended = attended.astype(jnp.bfloat16).reshape(
        step_count, token_count, query_heads * head_width
    )
    attended = lax.all_gather(attended, "tensor", axis=2, tiled=True)
    expert_count = lax.axis_size("expert")
    group_count = lax.axis_size("group")
    tensor_count = lax.axis_size("tensor")
    tensor_index = lax.axis_index("tensor")
    expert_local = gate_weight.shape[0]
    experts_all = expert_local * expert_count
    chosen_count = route_ids.shape[2]
    model_width = hidden_in.shape[2]
    column_width = down_weight.shape[2]
    capacity = min(token_count, max(2, 2 * token_count * chosen_count // experts_all))
    pair_count = token_count * chosen_count
    expert_iota = jnp.arange(experts_all, dtype=jnp.int32)
    slot_iota = jnp.arange(capacity, dtype=jnp.int32)
    token_owner = (
        (jnp.arange(pair_count) // chosen_count)[:, None] == jnp.arange(token_count)[None, :]
    ).astype(jnp.float32)
    halves = []
    for step_index in range(step_count):
        residual = hidden_in[step_index].astype(jnp.float32) + attended[step_index].astype(
            jnp.float32
        )
        normed = (
            residual
            * lax.rsqrt(jnp.mean(residual * residual, axis=-1, keepdims=True) + epsilon)
            * norm_gain
        ).astype(jnp.bfloat16)
        chosen = route_ids[step_index].reshape(pair_count)
        route_share = route_weights[step_index] / jnp.sum(
            route_weights[step_index], axis=-1, keepdims=True
        )
        expert_hits = (chosen[:, None] == expert_iota[None, :]).astype(jnp.int32)
        position = jnp.sum((jnp.cumsum(expert_hits, axis=0) - expert_hits) * expert_hits, axis=1)
        slotted = (
            expert_hits[:, :, None]
            * (position[:, None, None] == slot_iota[None, None, :]).astype(jnp.int32)
        ).astype(jnp.float32)
        dispatch = jnp.einsum("rec,rt->ect", slotted, token_owner, precision=highest)
        dispatch = dispatch.reshape(expert_count, expert_local, capacity, token_count).astype(
            jnp.bfloat16
        )
        combine = jnp.einsum(
            "rec,rt,r->tec",
            slotted,
            token_owner,
            route_share.reshape(pair_count),
            precision=highest,
        )
        combine = combine.reshape(token_count, expert_count, expert_local, capacity)
        feature_blocks = normed.reshape(token_count, group_count, model_width // group_count)
        outgoing = jnp.einsum(
            "aict,tgd->agicd", dispatch, feature_blocks, preferred_element_type=jnp.float32
        ).astype(jnp.bfloat16)
        flattened = outgoing.reshape(
            expert_count * group_count, expert_local, capacity, model_width // group_count
        )
        received = lax.all_to_all(
            flattened, ("expert", "group"), split_axis=0, concat_axis=0, tiled=True
        )
        gate_part = jnp.einsum(
            "seki,eif->sekf", received, gate_weight, preferred_element_type=jnp.float32
        ).astype(jnp.bfloat16)
        up_part = jnp.einsum(
            "seki,eif->sekf", received, up_weight, preferred_element_type=jnp.float32
        ).astype(jnp.bfloat16)
        gate_sum = lax.psum(gate_part, "group").astype(jnp.float32)
        up_sum = lax.psum(up_part, "group").astype(jnp.float32)
        hidden = (jax.nn.silu(gate_sum) * up_sum).astype(jnp.bfloat16)
        hidden = lax.all_gather(hidden, "tensor", axis=3, tiled=True)
        answered = jnp.einsum(
            "sekf,efo->seko", hidden, down_weight, preferred_element_type=jnp.float32
        ).astype(jnp.bfloat16)
        returned = lax.all_to_all(
            answered, ("expert", "group"), split_axis=0, concat_axis=0, tiled=True
        )
        returned = returned.reshape(
            expert_count, group_count, expert_local, capacity, column_width
        ).astype(jnp.float32)
        expert_mix = jnp.einsum("taic,agicd->tgd", combine, returned, precision=highest)
        own_columns = lax.dynamic_index_in_dim(
            residual.reshape(token_count, group_count, tensor_count, column_width),
            tensor_index,
            2,
            keepdims=False,
        )
        halves.append((own_columns + expert_mix).astype(jnp.bfloat16))
    stacked = jnp.stack(halves)
    layer_out = lax.all_gather(stacked, "tensor", axis=3, tiled=True).reshape(
        step_count, token_count, model_width
    )
    every_count = lax.all_gather(ancestor_counts, ("expert", "group"), axis=0, tiled=True)
    running = jnp.cumsum(every_count)
    first_index = lax.axis_index(("expert", "group")) * token_count
    own_index = first_index + jnp.arange(token_count, dtype=jnp.int32)
    ancestor = jnp.sum((running[None, :] <= own_index[:, None]).astype(jnp.int32), axis=1)
    widened = padded(both_kv, ((("expert", "group"), 1),), REACH)
    window_index = first_index - REACH + jnp.arange(token_count + 2 * REACH, dtype=jnp.int32)
    selector = (ancestor[:, None] == window_index[None, :]).astype(jnp.bfloat16)
    resampled = jnp.einsum(
        "tw,kwhld->kthld", selector, widened, preferred_element_type=jnp.float32
    ).astype(jnp.bfloat16)
    return (layer_out, resampled[0], resampled[1])


def solution(mesh):
    count = mesh.shape["expert"]
    fast = mesh.shape["group"] == 1 and mesh.shape["tensor"] == 2 and count % 2 == 0 and count & (count - 1) == 0
    in_specs = (
        P(None, ("parts", "expert", "group"), None),
        P(None, ("parts", "expert", "group"), "tensor", None),
        P(None, ("parts", "expert", "group"), "tensor", None),
        P(None, ("parts", "expert", "group"), "tensor", None),
        P(("parts", "expert", "group"), "tensor", None, None),
        P(("parts", "expert", "group"), "tensor", None, None),
        P(None, ("parts", "expert", "group"), None),
        P(None, ("parts", "expert", "group"), None),
        P(),
        P("expert", "group", "tensor"),
        P("expert", "group", "tensor"),
        P("expert", None, ("group", "tensor")),
        P(("parts", "expert", "group")),
    )
    out_specs = (
        P(None, ("parts", "expert", "group"), None),
        P(("parts", "expert", "group"), "tensor", None, None),
        P(("parts", "expert", "group"), "tensor", None, None),
    )
    return jax.shard_map(fast_shards if fast else shards, mesh=mesh, in_specs=in_specs, out_specs=out_specs, check_vma=False)
```
